128 devices in a mesh: ctx: 16 (over z, x_hi, core), shard: 8 (over y, x_lo).
Axes of the slice: x: 4 (x_hi: 2, x_lo: 2; x = x_hi * 2 + x_lo), y: 4, z: 4, core: 2. Of those that a mesh axis runs over, the one named last changes fastest.
Arguments:
- hidden: bfloat16 [16384, 2048], P('ctx'), may hold values from -6 to 6
- ids: int32 [16384], P('ctx'), may hold values from 0 to 4
- table: bfloat16 [5, 2048], replicated, may hold values from -3 to 3
- proj_weight: bfloat16 [2048, 2, 4096], P(None, None, 'shard'), may hold values from -0.125 to 0.125
- bc_weight: bfloat16 [2048, 256], P(None, 'shard'), may hold values from -0.01171875 to 0.01171875
- dt_weight: bfloat16 [2048, 64], P(None, 'shard'), may hold values from -0.125 to 0.125
- dt_bias: float32 [64], P('shard'), may hold values from -1 to 1
- decay: float32 [64], P('shard'), may hold values from 3.0517578e-05 to 0.04
- conv_weight: float32 [4, 4096], P(None, 'shard'), may hold values from -3 to 3
- conv_bias: float32 [4096], P('shard'), may hold values from -0.5 to 0.5
- skip: float32 [64], P('shard'), may hold values from 0.5 to 1.5
- norm_gain: float32 [4096], P('shard'), may hold values from 0.5 to 1.5
- out_weight: bfloat16 [4096, 2048], P('shard'), may hold values from -0.09375 to 0.09375
Outputs:
- mixed: bfloat16 [2048, 16384], P('shard', 'ctx')
The draws below stay inside these ranges and needn't reach their ends.
All inputs are finite; a program needn't handle non-finite values.
Results may differ from the reference program's by a relative error of at most 0.0095.
Values may be sent and summed in bfloat16 or wider, within the bound.
A program may use at most 128 MiB of HBM per device.

```python
import math
import jax
import jax.numpy as jnp
from jax import lax

D = 2048
E = 4096
SN = 128
HEADDIM = 64
KCONV = 4
GROUP = 256
HEADS = 64
TOKENS = 16384


def place_ends(array, key, least, largest):
    shape = array.shape
    index_at = [jax.random.randint(jax.random.fold_in(key, axis), (), 0, shape[axis]) for axis in range(len(shape))]
    array = array.at[tuple(index_at)].set(least)
    longest = shape.index(max(shape))
    index_at[longest] = (index_at[longest] + 1) % shape[longest]
    return array.at[tuple(index_at)].set(largest)


def shard_levels(key, shape, cuts, least, high):
    loudness = 1.0
    for axis_at, blocks in cuts:
        heights = jax.random.uniform(jax.random.fold_in(jax.random.fold_in(key, 6), axis_at), (blocks,), jnp.float32, least / len(cuts), high / len(cuts))
        loudness = loudness * jnp.repeat(jnp.exp(heights), shape[axis_at] // blocks).reshape((-1,) + (1,) * (len(shape) - 1 - axis_at))
    return loudness


def scatter_about(key, shape, deviation, limit, cuts=(), held_as=jnp.bfloat16):
    factor_of = shard_levels(key, shape, cuts, -0.22, 0.18) if cuts else 1.0
    array = jax.random.normal(key, shape, jnp.float32) * deviation * factor_of
    return jnp.minimum(jnp.maximum(array, -limit), limit).astype(held_as)


def setup_inputs(seed: int = 0) -> dict:
    key_of = jax.random.split(jax.random.key(seed), 14)
    hidden = scatter_about(key_of[0], (TOKENS, D), 1.0, 6.0, ((0, 16),))
    ids = place_ends(jax.random.randint(key_of[1], (TOKENS,), 0, 5), jax.random.fold_in(key_of[1], 1), 0, 4).astype(jnp.int32)
    table = scatter_about(key_of[2], (5, D), 0.5, 3.0)
    proj_weight = scatter_about(key_of[3], (D, 2, E), D ** -0.5, 0.125, ((2, 8),))
    bc_weight = scatter_about(key_of[4], (D, 2 * SN), (D * SN) ** -0.5, 0.01171875, ((1, 8),))
    dt_weight = scatter_about(key_of[5], (D, HEADS), D ** -0.5, 0.125, ((1, 8),))
    dt_bias = jnp.clip(jax.random.uniform(key_of[6], (HEADS,), jnp.float32, -1.0, 1.0) * shard_levels(key_of[6], (HEADS,), ((0, 8),), -0.4, 0.0), -1.0, 1.0)
    decay = jnp.clip(jnp.exp(math.log(0.04) - 7.178332 * jax.random.uniform(key_of[7], (HEADS,), jnp.float32) ** shard_levels(key_of[7], (HEADS,), ((0, 8),), -0.2, 0.2)), 3.0517578125e-05, 0.04)
    conv_weight = scatter_about(key_of[8], (KCONV, E), 0.5, 3.0, ((1, 8),), jnp.float32)
    conv_bias = jnp.clip(jax.random.uniform(key_of[9], (E,), jnp.float32, -0.5, 0.5) * shard_levels(key_of[9], (E,), ((0, 8),), -0.4, 0.0), -0.5, 0.5)
    skip = jnp.clip(0.5 + 1.0 * jax.random.uniform(key_of[10], (HEADS,), jnp.float32) ** shard_levels(key_of[10], (HEADS,), ((0, 8),), -0.2, 0.2), 0.5, 1.5)
    norm_gain = jnp.clip(0.5 + 1.0 * jax.random.uniform(key_of[11], (E,), jnp.float32) ** shard_levels(key_of[11], (E,), ((0, 8),), -0.2, 0.2), 0.5, 1.5)
    out_weight = scatter_about(key_of[12], (E, D), E ** -0.5, 0.09375, ((0, 8),))
    return dict(hidden=hidden, ids=ids, table=table, proj_weight=proj_weight, bc_weight=bc_weight, dt_weight=dt_weight, dt_bias=dt_bias, decay=decay, conv_weight=conv_weight, conv_bias=conv_bias, skip=skip, norm_gain=norm_gain, out_weight=out_weight)


def scan_block(x_heads, b_rows, c_rows, step_sizes, decay, group_len):
    row_count, head_count, head_width = x_heads.shape
    state_len = b_rows.shape[1]
    group_total = row_count // group_len
    log_rates = -step_sizes * decay[None, :]
    x_blocks = x_heads.astype(jnp.float32).reshape(group_total, group_len, head_count, head_width)
    b_blocks = b_rows.astype(jnp.float32).reshape(group_total, group_len, state_len)
    c_blocks = c_rows.astype(jnp.float32).reshape(group_total, group_len, state_len)
    d_blocks = step_sizes.reshape(group_total, group_len, head_count)
    l_blocks = log_rates.reshape(group_total, group_len, head_count)
    positions = jnp.arange(group_len, dtype=jnp.int32)
    lower_mask = positions[:, None] >= positions[None, :]

    def advance(carried_state, pieces):
        x_piece, b_piece, c_piece, d_piece, l_piece = pieces
        running = jnp.cumsum(l_piece, axis=0)
        spread = running[:, None, :] - running[None, :, :]
        weights = jnp.exp(jnp.where(lower_mask[:, :, None], spread, -jnp.inf))
        scores = jnp.einsum('tn,sn->ts', c_piece, b_piece, precision=lax.Precision.HIGHEST)
        inputs = d_piece[:, :, None] * x_piece
        inner = jnp.einsum('tsh,shp->thp', scores[:, :, None] * weights, inputs, precision=lax.Precision.HIGHEST)
        from_state = jnp.exp(running)[:, :, None] * jnp.einsum('tn,hpn->thp', c_piece, carried_state, precision=lax.Precision.HIGHEST)
        remaining = jnp.exp(running[-1][None, :] - running)
        new_state = jnp.exp(running[-1])[:, None, None] * carried_state + jnp.einsum('sh,shp,sn->hpn', remaining, inputs, b_piece, precision=lax.Precision.HIGHEST)
        return (new_state, inner + from_state)
    start_state = jnp.zeros((head_count, head_width, state_len), jnp.float32)
    last_state, outputs = lax.scan(advance, start_state, (x_blocks, b_blocks, c_blocks, d_blocks, l_blocks))
    return (outputs.reshape(row_count, head_count, head_width), last_state)

def strand_pass(sequence, proj_weight, bc_weight, dt_weight, dt_bias, decay, conv_weight, conv_bias, skip, norm_gain):
    length = sequence.shape[0]
    gate_part = jnp.dot(sequence, proj_weight[:, 0, :], preferred_element_type=jnp.float32)
    x_inner = jnp.dot(sequence, proj_weight[:, 1, :], preferred_element_type=jnp.float32).astype(jnp.bfloat16)
    bc_rows = jnp.dot(sequence, bc_weight, preferred_element_type=jnp.float32).astype(jnp.bfloat16)
    step_sizes = jax.nn.softplus(jnp.dot(sequence, dt_weight, preferred_element_type=jnp.float32) + dt_bias)
    padded = jnp.concatenate([jnp.zeros((KCONV - 1, E), jnp.bfloat16), x_inner], 0)
    accum = jnp.zeros((length, E), jnp.float32) + conv_bias[None, :]
    for lag_index in range(KCONV):
        accum = accum + conv_weight[lag_index][None, :] * padded[lag_index:lag_index + length].astype(jnp.float32)
    x_conv = jax.nn.silu(accum).astype(jnp.bfloat16)
    x_heads = x_conv.reshape(length, HEADS, HEADDIM)
    outputs, last_state = scan_block(x_heads, bc_rows[:, :SN], bc_rows[:, SN:], step_sizes, decay, min(GROUP, length))
    outputs = outputs + skip[None, :, None] * x_heads.astype(jnp.float32)
    gated = outputs.reshape(length, E) * jax.nn.silu(gate_part)
    mean_sq = lax.optimization_barrier(jnp.mean(gated * gated, axis=-1, keepdims=True))
    return (gated * lax.rsqrt(mean_sq + 1e-05) * norm_gain[None, :]).astype(jnp.bfloat16)

def reference(hidden, ids, table, proj_weight, bc_weight, dt_weight, dt_bias, decay, conv_weight, conv_bias, skip, norm_gain, out_weight):
    forward = (hidden.astype(jnp.float32) + table[ids].astype(jnp.float32)).astype(jnp.bfloat16)
    flipped = forward[::-1, ::-1]
    normed_u = strand_pass(forward, proj_weight, bc_weight, dt_weight, dt_bias, decay, conv_weight, conv_bias, skip, norm_gain)
    normed_rc = strand_pass(flipped, proj_weight, bc_weight, dt_weight, dt_bias, decay, conv_weight, conv_bias, skip, norm_gain)
    out_u = jnp.dot(normed_u, out_weight, preferred_element_type=jnp.float32)
    out_rc = jnp.dot(normed_rc, out_weight, preferred_element_type=jnp.float32)
    return (out_u + out_rc[::-1, ::-1]).T.astype(jnp.bfloat16)
```

```python
import jax
import jax.numpy as jnp
from jax import lax
from jax.experimental import pallas as pl
from jax.experimental.pallas import tpu as pltpu
from jax.sharding import PartitionSpec as P

E = 4096
L = 128
TB = 256
XR = 160
HEADDIM = 64
MESH = pl.DeviceIdType.MESH
F32 = jnp.float32
BF16 = jnp.bfloat16
NT = (((1,), (1,)), ((), ()))
TN = (((0,), (0,)), ((), ()))


def dot(a, b, dims=(((1,), (0,)), ((), ())), **kw):
    return lax.dot_general(a, b, dims, preferred_element_type=F32, **kw)


def silu(x):
    half = 0.5 * x
    return half + half * jnp.tanh(half)


def iota(shape, dim):
    return lax.broadcasted_iota(jnp.int32, shape, dim)


def split(x):
    hi = x.astype(BF16).astype(F32)
    return hi, (x - hi).astype(BF16).astype(F32)


def rows_of(k, size):
    return pl.ds(pl.multiple_of(k * size, size), size)


def kernel(
    hid_hbm, ids_ref, table_ref, wx_hbm, wg_hbm, bcw_hbm, dtw_ref, cw_ref, cb_ref, gain_ref, wo_hbm,
    dtb_ref, decay_ref, skip_ref,
    out_ref,
    u, ur, wx, wg, wall, bcw, flip, xin, xc, bc, gate, ybuf, eexp, dtraw, rowsbuf, cols, arow, sch, sst,
    halo_out, halo_in, st_out, st_in, ch_out, ch_in, pl_out, pl_in, fin_out, fin_in,
    sq, nrm, part, rx, qbuf, ry, ry2, abuf, rx2,
    hsem, wsem, bsem, bgs, bgr, bcs, bcr, hs, hr, sts, stsr, chs, chr_, pls, plr, fis, fir, sqs, sqr,
    rxs, rxr, rys, ryr, ry2s, ry2r, rx2s, rx2r,
):
    T, D = u.shape
    wexp = ybuf
    EL = xc.shape[2]
    NB = T // TB
    NC = T // L
    H = EL // HEADDIM
    c = lax.axis_index("ctx")
    s = lax.axis_index("shard")
    z, xh, core = c // 4, (c // 2) % 2, c % 2
    y, xl = s // 2, s % 2

    def remote(src, dst, ss, rs, ctx=None, shard=None):
        return pltpu.make_async_remote_copy(
            src_ref=src, dst_ref=dst, send_sem=ss, recv_sem=rs,
            device_id={"ctx": c if ctx is None else ctx, "shard": s if shard is None else shard},
            device_id_type=MESH,
        )

    hcopies = [
        pltpu.make_async_copy(hid_hbm.at[pl.ds(b * TB, TB)], u.at[pl.ds(b * TB, TB)], hsem.at[b])
        for b in range(NB)
    ]
    wxc = pltpu.make_async_copy(wx_hbm, wx, wsem.at[0])
    wgc = pltpu.make_async_copy(wg_hbm, wg, wsem.at[1])
    woc = pltpu.make_async_copy(wo_hbm, wall.at[pl.ds(0, EL)], wsem.at[2])
    bown = pltpu.make_async_copy(bcw_hbm.at[core], bcw.at[s, core], bsem)
    hcopies[0].start()
    wxc.start()
    bown.start()
    for b in range(1, NB):
        hcopies[b].start()
    wgc.start()
    woc.start()

    mate = c + 1 - 2 * core
    other = (c + 16 + 2 * core - 1) % 16
    xmate = c + 2 - 4 * xh
    barrier = pltpu.get_barrier_semaphore()
    peers = [(mate, s), (other, s), (xmate, s)]
    peers += [((c + 4 * k) % 16, s) for k in range(1, 4)]
    peers += [(c, (s + k) % 8) for k in range(1, 8)]
    for pc, ps in peers:
        pl.semaphore_signal(barrier, inc=1, device_id={"ctx": pc, "shard": ps}, device_id_type=MESH)
    pl.semaphore_wait(barrier, len(peers))

    def gather(k):
        return remote(bcw_hbm.at[core], bcw.at[s, core], bgs.at[k - 1], bgr.at[k - 1], shard=(s + k) % 8)

    for k in range(1, 8):
        gather(k).start()

    flip[...] = jnp.where(iota((TB, TB), 0) + iota((TB, TB), 1) == TB - 1, 1.0, 0.0).astype(BF16)
    wxc.wait()
    nd = D // TB

    def front(b, _):
        rows = rows_of(b, TB)
        pltpu.make_async_copy(hid_hbm.at[rows], u.at[rows], hsem.at[b]).wait()
        hot = jnp.where(iota((16, TB), 0) == ids_ref[:, rows], 1.0, 0.0).astype(BF16)
        added = dot(hot, table_ref[...], TN)
        u[rows, :] = (u[rows, :].astype(F32) + added).astype(BF16)
        for i in range(nd):
            ur[rows, i * TB:(i + 1) * TB] = dot(
                u[rows, (nd - 1 - i) * TB:(nd - i) * TB], flip[...]
            ).astype(BF16)
        for i, v in enumerate((u, ur)):
            xv = dot(v[rows, :], wx[...]).astype(BF16)
            xin[i, pl.ds(pl.multiple_of(b * TB + 8, 8), TB), :] = xv.astype(F32)
            dr = dot(dtw_ref[...], v[rows, :], NT)
            for q in range(TB // L):
                dtraw[i, rows_of(b * (TB // L) + q, H), :] = dr[:, q * L:(q + 1) * L]
        return 0

    lax.fori_loop(0, NB, front, 0)

    halo_out[0] = xin[0, T - 8:T + 8, :].astype(BF16)
    halo_out[1] = xin[1, 8:24, :].astype(BF16)
    nxt, prv = (c + 1) % 16, (c + 15) % 16
    hcf = remote(halo_out.at[0], halo_in.at[0], hs.at[0], hr.at[0], ctx=nxt)
    hcr = remote(halo_out.at[1], halo_in.at[1], hs.at[1], hr.at[1], ctx=prv)
    hcf.start()
    hcr.start()

    bown.wait()
    for k in range(1, 8):
        gather(k).wait()
    swap = remote(bcw.at[:, core], bcw.at[:, core], bcs, bcr, ctx=mate)
    swap.start()

    head = iota((NC * H, L), 0) % H
    bias = jnp.zeros((NC * H, L), F32)
    rate = jnp.zeros((NC * H, L), F32)
    for h in range(H):
        bias = jnp.where(head == h, dtb_ref[h], bias)
        rate = jnp.where(head == h, decay_ref[h], rate)
    rowsbuf[...] = jnp.zeros_like(rowsbuf)
    before = iota((L, L), 0) <= iota((L, L), 1)
    after = iota((L, L), 0) >= iota((L, L), 1)
    for i in range(2):
        raw = dtraw[i] + bias
        dt = jnp.maximum(raw, 0.0) + jnp.log1p(jnp.exp(-jnp.abs(raw)))
        tri = jnp.where(before if i == 0 else after, 1.0, 0.0)
        g = dot(-dt * rate, tri, precision=lax.Precision.HIGHEST)
        total = g[:, L - 1:L] if i == 0 else g[:, 0:1]
        whi, wlo = split(jnp.exp(total - g) * dt)
        ehi, elo = split(jnp.exp(g))
        a = g - jnp.log(dt)
        for k in range(NC):
            sl = slice(k * H, (k + 1) * H)
            arow[i, k] = a[sl]
            for j, part_ in enumerate((g, whi, wlo, ehi, elo)):
                at = (5 * i + j) * H
                rowsbuf[k, at:at + H, :] = part_[sl]

    er, ec = iota((L, EL), 0), iota((L, EL), 1)

    def spread(first):
        hit = (er >= first) & (er < first + 2 * H) & (er % H == ec // HEADDIM)
        return jnp.where(hit, 1.0, 0.0).astype(BF16)

    spreads = [spread(5 * H * i + H + 2 * H * j) for i in range(2) for j in range(2)]

    def expand(k, _):
        rows = rows_of(k, L)
        t = rowsbuf[k].T
        cols[rows, :] = t
        tb = t.astype(BF16)
        for i in range(2):
            wexp[i, rows, :] = dot(tb, spreads[2 * i])
            eexp[i, rows, :] = dot(tb, spreads[2 * i + 1])
        return 0

    lax.fori_loop(0, NC, expand, 0)

    swap.wait()

    def proj_bc(b, _):
        rows = rows_of(b, TB)
        wb = bcw[...].reshape(8 * 32, D)
        for i, v in enumerate((u, ur)):
            bc[i, rows, :] = dot(v[rows, :], wb, NT).astype(BF16)
        return 0

    lax.fori_loop(0, NB, proj_bc, 0)

    hcf.wait()
    hcr.wait()
    xin[0, 0:8, :] = jnp.where(c > 0, halo_in[0, 8:16, :].astype(F32), 0.0)
    xin[1, T + 8:T + 16, :] = jnp.where(c < 15, halo_in[1, 0:8, :].astype(F32), 0.0)

    def chunk_state(k, _):
        rows = rows_of(k, L)
        for i in range(2):
            window = xin[i, pl.ds(pl.multiple_of(k * L, L), L + 16), :]
            acc = jnp.zeros((L, EL), F32) + cb_ref[...]
            for t in range(4):
                at = 8 - 3 + t if i == 0 else 8 + 3 - t
                acc = acc + cw_ref[t:t + 1, :] * window[at:at + L, :]
            xv = silu(acc).astype(BF16)
            xc[i, rows, :] = xv
            scaled = (wexp[i, rows, :] * xv.astype(F32)).astype(BF16)
            bt = bc[i, rows, 0:L].astype(F32).T.astype(BF16)
            sch[i, k] = dot(bt, scaled)
        return 0

    lax.fori_loop(0, NC, chunk_state, 0)

    def chunk_decay(i, k):
        at = k * L + (L - 1 if i == 0 else 0)
        return eexp[i, at:at + 1, :]

    def pack_decay(d):
        hi, lo = split(d)
        wide = (8, d.shape[1])
        return jnp.concatenate([jnp.broadcast_to(hi, wide), jnp.broadcast_to(lo, wide)], 0).astype(BF16)

    def load_state(ref):
        whole = ref[...]
        tail = whole[L:L + 16].astype(F32)
        return whole[:L].astype(F32), tail[0:1] + tail[8:9]

    for i in range(2):
        state, dec = None, None
        for k in (range(NC) if i == 0 else range(NC - 1, -1, -1)):
            d = chunk_decay(i, k)
            state = sch[i, k] if state is None else d * state + sch[i, k]
            dec = d if dec is None else dec * d
        st_out[i, 0:L, :] = state.astype(BF16)
        st_out[i, L:L + 16, :] = pack_decay(dec)

    sta = remote(st_out, st_in, sts, stsr, ctx=mate)
    sta.start()

    wgc.wait()

    def proj_gate(b, _):
        rows = rows_of(b, TB)
        for i, v in enumerate((u, ur)):
            gate[i, rows, :] = silu(dot(v[rows, :], wg[...]))
        return 0

    lax.fori_loop(0, NB // 2, proj_gate, 0)

    sta.wait()
    HC = EL // 2
    half = pl.ds(pl.multiple_of(core * HC, HC), HC)
    for i in range(2):
        ms, md = load_state(st_out.at[i, :, half])
        ts, td = load_state(st_in.at[i, :, half])
        mine_first = core == i
        state = jnp.where(mine_first, td * ms + ts, md * ts + ms)
        ch_out[i, 0:L, :] = state.astype(BF16)
        ch_out[i, L:L + 16, :] = pack_decay(md * td)
    cha = remote(ch_out, ch_in, chs, chr_, ctx=xmate)
    cha.start()

    lax.fori_loop(NB // 2, NB, proj_gate, 0)

    woc.wait()
    for i in range(nd):
        wall[EL:2 * EL, i * TB:(i + 1) * TB] = dot(
            wall[0:EL, (nd - 1 - i) * TB:(nd - i) * TB], flip[...]
        ).astype(BF16)

    cha.wait()
    for i in range(2):
        ms, md = load_state(ch_out.at[i])
        ts, td = load_state(ch_in.at[i])
        mine_first = xh == i
        state = jnp.where(mine_first, td * ms + ts, md * ts + ms)
        pl_out[i, 0:L, :] = state.astype(BF16)
        pl_out[i, L:L + 16, :] = pack_decay(md * td)

    def plane(k):
        return remote(
            pl_out.at[(z + k) // 4], pl_in.at[z], pls.at[k - 1], plr.at[k - 1], ctx=(c + 4 * k) % 16
        )

    for k in range(1, 4):
        plane(k).start()
    pl_in[z] = pl_out[0]

    lane = iota((L, L), 1)
    sk = jnp.zeros((1, EL), F32)
    for h in range(H):
        sk = jnp.where(iota((1, EL), 1) // HEADDIM == h, skip_ref[h], sk)

    def intra(k, _):
        rows = rows_of(k, L)
        for i in range(2):
            cb = dot(bc[i, rows, L:2 * L], bc[i, rows, 0:L], NT)
            keep = iota((L, L), 0) >= lane if i == 0 else iota((L, L), 0) <= lane
            ar = arow[i, k]
            for q in range(H // 2):
                ms = []
                for h in (2 * q, 2 * q + 1):
                    at = 5 * H * i + h
                    d = cols[rows, at:at + 1] - ar[h:h + 1, :]
                    ms.append((jnp.exp(jnp.where(keep, d, -1e30)) * cb).astype(BF16))
                xp = xc[i, rows, q * L:(q + 1) * L]
                zero = jnp.zeros_like(xp)
                left = jnp.where(lane < HEADDIM, xp, zero)
                right = jnp.where(lane < HEADDIM, zero, xp)
                yq = dot(jnp.concatenate(ms, 1), jnp.concatenate([left, right], 0))
                ybuf[i, rows, q * L:(q + 1) * L] = yq + sk[:, q * L:(q + 1) * L] * xp.astype(F32)
        return 0

    lax.fori_loop(0, NC, intra, 0)

    for k in range(1, 4):
        plane(k).wait_send()
        pltpu.make_async_remote_copy(
            src_ref=pl_out.at[0], dst_ref=pl_in.at[(z + 4 - k) % 4], send_sem=pls.at[k - 1],
            recv_sem=plr.at[k - 1], device_id={"ctx": (c + 4 * k) % 16, "shard": s}, device_id_type=MESH,
        ).wait_recv()
    for i in range(2):
        acc = jnp.zeros((L, HC), F32)
        for zz in (range(3) if i == 0 else range(3, 0, -1)):
            ps, pd = load_state(pl_in.at[zz])
            acc = jnp.where((zz < z) if i == 0 else (zz > z), pd * acc + ps, acc)
        ts, td = load_state(ch_in.at[i])
        acc = jnp.where(xh != i, td * acc + ts, acc)
        fin_out[i] = acc.astype(BF16)
    fina = remote(fin_out, fin_in, fis, fir, ctx=mate)
    fina.start()
    fina.wait()

    for i in range(2):
        mine, theirs = fin_out[i].astype(F32), fin_in[i].astype(F32)
        entering = jnp.where(
            core == 0, jnp.concatenate([mine, theirs], 1), jnp.concatenate([theirs, mine], 1)
        )
        ts, td = load_state(st_in.at[i])
        state = jnp.where(core != i, td * entering + ts, entering)
        order = range(NC) if i == 0 else range(NC - 1, -1, -1)
        for k in order:
            sst[i, k] = state.astype(BF16)
            state = chunk_decay(i, k) * state + sch[i, k]

    def sums(j, k):
        return remote(sq.at[j, s], sq.at[j, s], sqs.at[j, k - 1], sqr.at[j, k - 1], shard=(s + k) % 8)

    def gated_block(j):
        total = jnp.zeros((8, TB), F32)
        for i in range(2):
            pick = jnp.where(iota((8, EL), 0) // 4 == i, 1.0, 0.0).astype(BF16)
            for q in range(TB // L):
                k = j * (TB // L) + q
                rows = slice(k * L, (k + 1) * L)
                yv = ybuf[i, rows, :] + eexp[i, rows, :] * dot(bc[i, rows, L:2 * L], sst[i, k])
                ybuf[i, rows, :] = yv * gate[i, rows, :]
            rows = slice(j * TB, (j + 1) * TB)
            gv = ybuf[i, rows, :]
            total = total + dot(pick, (gv * gv).astype(BF16), NT)
        sq[j, s] = total
        for k in range(1, 8):
            sums(j, k).start()

    def wait_sums(j):
        for k in range(1, 8):
            sums(j, k).wait_send()
            pltpu.make_async_remote_copy(
                src_ref=sq.at[j, s], dst_ref=sq.at[j, (s + 8 - k) % 8], send_sem=sqs.at[j, k - 1],
                recv_sem=sqr.at[j, k - 1], device_id={"ctx": c, "shard": (s + k) % 8}, device_id_type=MESH,
            ).wait_recv()

    xs = s + 1 - 2 * xl

    def cross(j):
        return remote(
            part.at[j, 1 - xl, :, pl.ds(0, XR), :], rx.at[j], rxs.at[j], rxr.at[j], shard=xs
        )

    def along(j, k):
        yk = (y + k) % 4
        return remote(
            part.at[j, :, yk, pl.ds(XR, TB - XR), :], ry2.at[j, k - 1], ry2s.at[j, k - 1], ry2r.at[j, k - 1],
            shard=yk * 2 + xl,
        )

    def along2(j, k):
        yk = (y + k) % 4
        return remote(qbuf.at[j, yk], ry.at[j, k - 1], rys.at[j, k - 1], ryr.at[j, k - 1], shard=yk * 2 + xl)

    def cross2(j):
        return remote(abuf.at[j], rx2.at[j], rx2s.at[j], rx2r.at[j], shard=xs)

    def product_block(j):
        wait_sums(j)
        total = sq[j, 0]
        for k in range(1, 8):
            total = total + sq[j, k]
        scale = lax.rsqrt(total / E + 1e-05)
        rows = slice(j * TB, (j + 1) * TB)
        for q in range(TB // L):
            col = jnp.concatenate([scale[:, q * L:(q + 1) * L]] * (L // 8), 0).T
            sub = slice(j * TB + q * L, j * TB + (q + 1) * L)
            for i in range(2):
                nv = ybuf[i, sub, :] * col[:, 4 * i:4 * i + 1] * gain_ref[...]
                nrm[sub, i * EL:(i + 1) * EL] = nv.astype(BF16)

        def piece(p, _):
            xx = lax.rem(p // 4 + 1 + xl, 2)
            yy = lax.rem(p, 4)
            colsl = rows_of(yy * 2 + xx, TB)
            part[j, xx, yy] = dot(nrm[rows, :], wall[:, colsl]).astype(BF16)
            return 0

        lax.fori_loop(0, 4, piece, 0)
        cross(j).start()
        lax.fori_loop(4, 8, piece, 0)
        for k in range(1, 4):
            along(j, k).start()

    def middle_block(j):
        cross(j).wait()
        for k in range(4):
            yk = (y + k) % 4
            both = part[j, xl, yk, 0:XR, :].astype(F32) + rx[j, yk].astype(F32)
            qbuf[j, yk] = both.astype(BF16)
            if k:
                along2(j, k).start()
        for k in range(1, 4):
            along(j, k).wait()
        for m in range(2):
            xx = (xl + 1 + m) % 2
            acc = part[j, xx, y, XR:TB, :].astype(F32)
            for k in range(1, 4):
                acc = acc + ry2[j, k - 1, xx].astype(F32)
            if m == 0:
                abuf[j] = acc.astype(BF16)
                cross2(j).start()
            else:
                keepbuf = acc
        return keepbuf

    def last_block(j, own):
        for k in range(1, 4):
            along2(j, k).wait()
        acc = qbuf[j, y].astype(F32)
        for k in range(1, 4):
            acc = acc + ry[j, k - 1].astype(F32)
        cross2(j).wait()
        low = own + rx2[j].astype(F32)
        whole = jnp.concatenate([acc, low], 0)
        out_ref[:, j * TB:(j + 1) * TB] = whole.T.astype(BF16)

    kept = [None] * NB
    gated_block(0)
    gated_block(1)
    product_block(0)
    gated_block(2)
    product_block(1)
    gated_block(3)
    kept[0] = middle_block(0)
    product_block(2)
    kept[1] = middle_block(1)
    product_block(3)
    kept[2] = middle_block(2)
    kept[3] = middle_block(3)
    for j in range(NB):
        last_block(j, kept[j])


def per_device(
    hidden, ids, table, proj_weight, bc_weight, dt_weight, dt_bias, decay, conv_weight, conv_bias, skip,
    norm_gain, out_weight,
):
    T, D = hidden.shape
    EL = conv_bias.shape[0]
    H = EL // HEADDIM
    NB, NC = T // TB, T // L
    vm = pl.BlockSpec(memory_space=pltpu.VMEM)
    sm = pl.BlockSpec(memory_space=pltpu.SMEM)
    hbm = pl.BlockSpec(memory_space=pl.ANY)
    V = pltpu.VMEM
    dma = pltpu.SemaphoreType.DMA
    scratch = [
        V((T, D), BF16), V((T, D), BF16),
        V((D, EL), BF16), V((D, EL), BF16), V((2 * EL, D), BF16),
        V((8, 2, 16, D), BF16), V((TB, TB), BF16),
        V((2, T + 16, EL), F32), V((2, T, EL), BF16), V((2, T, 2 * L), BF16),
        V((2, T, EL), F32), V((2, T, EL), F32), V((2, T, EL), F32),
        V((2, NC * H, L), F32), V((NC, L, L), F32), V((T, L), F32), V((2, NC, H, L), F32),
        V((2, NC, L, EL), F32), V((2, NC, L, EL), BF16),
        V((2, 16, EL), BF16), V((2, 16, EL), BF16),
        V((2, L + 16, EL), BF16), V((2, L + 16, EL), BF16),
        V((2, L + 16, EL // 2), BF16), V((2, L + 16, EL // 2), BF16),
        V((2, L + 16, EL // 2), BF16), V((4, L + 16, EL // 2), BF16),
        V((2, L, EL // 2), BF16), V((2, L, EL // 2), BF16),
        V((NB, 8, 8, TB), F32), V((T, 2 * EL), BF16), V((NB, 2, 4, TB, TB), BF16),
        V((NB, 4, XR, TB), BF16), V((NB, 4, XR, TB), BF16), V((NB, 3, XR, TB), BF16),
        V((NB, 3, 2, TB - XR, TB), BF16), V((NB, TB - XR, TB), BF16), V((NB, TB - XR, TB), BF16),
        dma((NB,)), dma((3,)), dma, dma((7,)), dma((7,)), dma, dma, dma((2,)), dma((2,)), dma, dma, dma, dma,
        dma((3,)), dma((3,)), dma, dma, dma((NB, 7)), dma((NB, 7)),
        dma((NB,)), dma((NB,)), dma((NB, 3)), dma((NB, 3)), dma((NB, 3)), dma((NB, 3)), dma((NB,)), dma((NB,)),
    ]
    return pl.pallas_call(
        kernel,
        out_shape=jax.ShapeDtypeStruct((D // 8, T), BF16),
        in_specs=[hbm, vm, vm, hbm, hbm, hbm, vm, vm, vm, vm, hbm, sm, sm, sm],
        out_specs=vm,
        scratch_shapes=scratch,
        compiler_params=pltpu.CompilerParams(
            collective_id=0, has_side_effects=True, vmem_limit_bytes=60 * 1024 * 1024
        ),
        cost_estimate=pl.CostEstimate(flops=20_000_000_000, bytes_accessed=16_000_000, transcendentals=4_000_000),
    )(
        hidden, ids.reshape(1, T), jnp.pad(table, ((0, 16 - table.shape[0]), (0, 0))),
        proj_weight[:, 1, :], proj_weight[:, 0, :], bc_weight.T.reshape(2, 16, D), dt_weight.T,
        conv_weight, conv_bias.reshape(1, EL), norm_gain.reshape(1, EL), out_weight,
        dt_bias, decay, skip,
    )


def solution(mesh):
    in_specs = (
        P("ctx", None), P("ctx"), P(), P(None, None, "shard"), P(None, "shard"), P(None, "shard"), P("shard"),
        P("shard"), P(None, "shard"), P("shard"), P("shard"), P("shard"), P("shard", None),
    )
    return jax.shard_map(
        per_device, mesh=mesh, in_specs=in_specs, out_specs=P("shard", "ctx"), check_vma=False
    )
```

```python
import jax
import jax.numpy as jnp
from jax import lax
from jax.experimental import pallas as pl
from jax.experimental.pallas import tpu as pltpu
from jax.sharding import PartitionSpec as P

E = 4096
L = 128
TB = 256
XR = 160
HEADDIM = 64
MESH = pl.DeviceIdType.MESH
F32 = jnp.float32
BF16 = jnp.bfloat16
NT = (((1,), (1,)), ((), ()))
TN = (((0,), (0,)), ((), ()))


def dot(a, b, dims=(((1,), (0,)), ((), ())), **kw):
    return lax.dot_general(a, b, dims, preferred_element_type=F32, **kw)


def silu(x):
    half = 0.5 * x
    return half + half * jnp.tanh(half)


def iota(shape, dim):
    return lax.broadcasted_iota(jnp.int32, shape, dim)


def split(x):
    hi = x.astype(BF16).astype(F32)
    return hi, (x - hi).astype(BF16).astype(F32)


def rows_of(k, size):
    return pl.ds(pl.multiple_of(k * size, size), size)


def kernel(
    hid_hbm, ids_ref, table_ref, w_hbm, bcw_hbm, dtw_ref, cw_ref, cb_ref, gain_ref, wo_hbm,
    dtb_ref, decay_ref, skip_ref,
    out_ref,
    u, ur, wraw, wx, wg, wall, bcw, flip, xin, xc, bc, gate, ybuf, dtraw, rowsbuf, cols, arow, sch, sst,
    halo_out, halo_in, st_out, st_in, ch_out, ch_in, pl_out, pl_in, fin_out, fin_in,
    sq, nrm, part, rx, qbuf, ry, ry2, abuf, rx2,
    hsem, wsem, wosem, bsem, bgs, bgr, bcs, bcr, hs, hr, sts, stsr, chs, chr_, pls, plr, fis, fir, sqs, sqr,
    rxs, rxr, rys, ryr, ry2s, ry2r, rx2s, rx2r,
):
    T, D = u.shape
    EL = xc.shape[2]
    NB = T // TB
    NC = T // L
    H = EL // HEADDIM
    c = lax.axis_index("ctx")
    s = lax.axis_index("shard")
    z, xh, core = c // 4, (c // 2) % 2, c % 2
    y, xl = s // 2, s % 2

    def remote(src, dst, ss, rs, ctx=None, shard=None):
        return pltpu.make_async_remote_copy(
            src_ref=src, dst_ref=dst, send_sem=ss, recv_sem=rs,
            device_id={"ctx": c if ctx is None else ctx, "shard": s if shard is None else shard},
            device_id_type=MESH,
        )

    WR = D // NB
    hcopies = [
        pltpu.make_async_copy(hid_hbm.at[pl.ds(b * TB, TB)], u.at[pl.ds(b * TB, TB)], hsem.at[b])
        for b in range(NB)
    ]
    wcopies = [
        pltpu.make_async_copy(w_hbm.at[pl.ds(b * WR, WR)], wraw.at[pl.ds(b * WR, WR)], wsem.at[b])
        for b in range(NB)
    ]
    woc = pltpu.make_async_copy(wo_hbm, wall.at[pl.ds(0, EL)], wosem)
    bown = pltpu.make_async_copy(bcw_hbm.at[core], bcw.at[s, core], bsem)
    for b in range(NB):
        hcopies[b].start()
        wcopies[b].start()
    bown.start()

    mate = c + 1 - 2 * core
    other = (c + 16 + 2 * core - 1) % 16
    xmate = c + 2 - 4 * xh
    barrier = pltpu.get_barrier_semaphore()
    peers = [(mate, s), (other, s), (xmate, s)]
    peers += [((c + 4 * k) % 16, s) for k in range(1, 4)]
    peers += [(c, (s + k) % 8) for k in range(1, 8)]
    for pc, ps in peers:
        pl.semaphore_signal(barrier, inc=1, device_id={"ctx": pc, "shard": ps}, device_id_type=MESH)
    pl.semaphore_wait(barrier, len(peers))

    def gather(k):
        return remote(bcw_hbm.at[core], bcw.at[s, core], bgs.at[k - 1], bgr.at[k - 1], shard=(s + k) % 8)

    for k in range(1, 8):
        gather(k).start()

    flip[...] = jnp.where(iota((TB, TB), 0) + iota((TB, TB), 1) == TB - 1, 1.0, 0.0).astype(BF16)
    nd = D // TB
    for b in range(NB):
        rows = slice(b * TB, (b + 1) * TB)
        hcopies[b].wait()
        hot = jnp.where(iota((table_ref.shape[0], TB), 0) == ids_ref[:, rows], 1.0, 0.0).astype(BF16)
        added = dot(hot, table_ref[...], TN)
        u[rows, :] = (u[rows, :].astype(F32) + added).astype(BF16)
        for i in range(nd):
            ur[rows, i * TB:(i + 1) * TB] = dot(
                u[rows, (nd - 1 - i) * TB:(nd - i) * TB], flip[...]
            ).astype(BF16)
        wcopies[b].wait()
        for k in range(WR // L):
            wr = slice(b * WR + k * L, b * WR + (k + 1) * L)
            pair = jnp.swapaxes(wraw[wr, :, :], 0, 1)
            wg[wr, :] = pair[0]
            wx[wr, :] = pair[1]
    woc.start()

    PB = 512
    for b in range(T // PB):
        rows = slice(b * PB, (b + 1) * PB)
        for i, v in enumerate((u, ur)):
            xv = dot(v[rows, :], wx[...]).astype(BF16)
            xin[i, 8 + b * PB:8 + (b + 1) * PB, :] = xv.astype(F32)
            dr = dot(dtw_ref[...], v[rows, :], NT)
            for q in range(PB // L):
                k = b * (PB // L) + q
                dtraw[i, k * H:(k + 1) * H, :] = dr[:, q * L:(q + 1) * L]

    halo_out[0] = xin[0, T - 8:T + 8, :].astype(BF16)
    halo_out[1] = xin[1, 8:24, :].astype(BF16)
    nxt, prv = (c + 1) % 16, (c + 15) % 16
    hcf = remote(halo_out.at[0], halo_in.at[0], hs.at[0], hr.at[0], ctx=nxt)
    hcr = remote(halo_out.at[1], halo_in.at[1], hs.at[1], hr.at[1], ctx=prv)
    hcf.start()
    hcr.start()

    bown.wait()
    for k in range(1, 8):
        gather(k).wait()
    swap = remote(bcw.at[:, core], bcw.at[:, core], bcs, bcr, ctx=mate)
    swap.start()

    head = iota((NC * H, L), 0) % H
    bias = jnp.zeros((NC * H, L), F32)
    rate = jnp.zeros((NC * H, L), F32)
    for h in range(H):
        bias = jnp.where(head == h, dtb_ref[h], bias)
        rate = jnp.where(head == h, decay_ref[h], rate)
    rowsbuf[...] = jnp.zeros_like(rowsbuf)
    before = iota((L, L), 0) <= iota((L, L), 1)
    after = iota((L, L), 0) >= iota((L, L), 1)
    decs = []
    for i in range(2):
        raw = dtraw[i] + bias
        dt = jnp.maximum(raw, 0.0) + jnp.log1p(jnp.exp(-jnp.abs(raw)))
        tri = jnp.where(before if i == 0 else after, 1.0, 0.0)
        g = dot(-dt * rate, tri, precision=lax.Precision.HIGHEST)
        total = g[:, L - 1:L] if i == 0 else g[:, 0:1]
        whi, wlo = split(jnp.exp(total - g) * dt)
        ehi, elo = split(jnp.exp(g))
        a = g - jnp.log(dt)
        owner = iota((NC * H, EL), 0) % H == iota((NC * H, EL), 1) // HEADDIM
        chunk_of = jnp.where(iota((NC, NC * H), 1) // H == iota((NC, NC * H), 0), 1.0, 0.0).astype(BF16)
        thi, tlo = split(jnp.where(owner, jnp.exp(total), 0.0))
        dec_rows = dot(chunk_of, thi.astype(BF16)) + dot(chunk_of, tlo.astype(BF16))
        decs.append([dec_rows[k:k + 1, :] for k in range(NC)])
        for k in range(NC):
            sl = slice(k * H, (k + 1) * H)
            arow[i, k] = a[sl]
            for j, part_ in enumerate((g, whi, wlo, ehi, elo)):
                at = (5 * i + j) * H
                rowsbuf[k, at:at + H, :] = part_[sl]

    er, ec = iota((L, EL), 0), iota((L, EL), 1)

    def spread(first):
        hit = (er >= first) & (er < first + 2 * H) & (er % H == ec // HEADDIM)
        return jnp.where(hit, 1.0, 0.0).astype(BF16)

    spreads = [spread(5 * H * i + H + 2 * H * j) for i in range(2) for j in range(2)]
    for k in range(NC):
        cols[k * L:(k + 1) * L, :] = rowsbuf[k].T

    swap.wait()
    for b in range(T // PB):
        rows = slice(b * PB, (b + 1) * PB)
        for i, v in enumerate((u, ur)):
            bc[i, rows, :] = dot(v[rows, :], bcw[...].reshape(8 * 32, D), NT).astype(BF16)

    hcf.wait()
    hcr.wait()
    xin[0, 0:8, :] = jnp.where(c > 0, halo_in[0, 8:16, :].astype(F32), 0.0)
    xin[1, T + 8:T + 16, :] = jnp.where(c < 15, halo_in[1, 0:8, :].astype(F32), 0.0)

    def chunk_state(k, _):
        rows = rows_of(k, L)
        for i in range(2):
            window = xin[i, pl.ds(pl.multiple_of(k * L, L), L + 16), :]
            acc = jnp.zeros((L, EL), F32) + cb_ref[...]
            for t in range(4):
                at = 8 - 3 + t if i == 0 else 8 + 3 - t
                acc = acc + cw_ref[t:t + 1, :] * window[at:at + L, :]
            xv = silu(acc).astype(BF16)
            xc[i, rows, :] = xv
            wexp = dot(cols[rows, :].astype(BF16), spreads[2 * i])
            scaled = (wexp * xv.astype(F32)).astype(BF16)
            bt = bc[i, rows, 0:L].astype(F32).T.astype(BF16)
            sch[i, k] = dot(bt, scaled)
        return 0

    lax.fori_loop(0, NC, chunk_state, 0, unroll=2)

    def pack_decay(d):
        hi, lo = split(d)
        wide = (8, d.shape[1])
        return jnp.concatenate([jnp.broadcast_to(hi, wide), jnp.broadcast_to(lo, wide)], 0).astype(BF16)

    def load_state(ref):
        whole = ref[...]
        tail = whole[L:L + 16].astype(F32)
        return whole[:L].astype(F32), tail[0:1] + tail[8:9]

    for i in range(2):
        state, dec = None, None
        for k in (range(NC) if i == 0 else range(NC - 1, -1, -1)):
            d = decs[i][k]
            state = sch[i, k] if state is None else d * state + sch[i, k]
            dec = d if dec is None else dec * d
        st_out[i, 0:L, :] = state.astype(BF16)
        st_out[i, L:L + 16, :] = pack_decay(dec)

    sta = remote(st_out, st_in, sts, stsr, ctx=mate)
    sta.start()

    lane = iota((L, L), 1)
    sk = jnp.zeros((1, EL), F32)
    for h in range(H):
        sk = jnp.where(iota((1, EL), 1) // HEADDIM == h, skip_ref[h], sk)

    def late_block(j):
        rows = slice(j * TB, (j + 1) * TB)
        for i, v in enumerate((u, ur)):
            gate[i, rows, :] = silu(dot(v[rows, :], wg[...]))
        for k in range(j * (TB // L), (j + 1) * (TB // L)):
            rows = slice(k * L, (k + 1) * L)
            for i in range(2):
                cb = dot(bc[i, rows, L:2 * L], bc[i, rows, 0:L], NT)
                keep = iota((L, L), 0) >= lane if i == 0 else iota((L, L), 0) <= lane
                ar = arow[i, k]
                for q in range(H // 2):
                    ms = []
                    for h in (2 * q, 2 * q + 1):
                        at = 5 * H * i + h
                        d = cols[rows, at:at + 1] - ar[h:h + 1, :]
                        ms.append((jnp.exp(jnp.where(keep, d, -1e30)) * cb).astype(BF16))
                    xp = xc[i, rows, q * L:(q + 1) * L]
                    zero = jnp.zeros_like(xp)
                    left = jnp.where(lane < HEADDIM, xp, zero)
                    right = jnp.where(lane < HEADDIM, zero, xp)
                    yq = dot(jnp.concatenate(ms, 1), jnp.concatenate([left, right], 0))
                    ybuf[i, rows, q * L:(q + 1) * L] = yq + sk[:, q * L:(q + 1) * L] * xp.astype(F32)

    woc.wait()
    for i in range(nd):
        wall[EL:2 * EL, i * TB:(i + 1) * TB] = dot(
            wall[0:EL, (nd - 1 - i) * TB:(nd - i) * TB], flip[...]
        ).astype(BF16)

    sta.wait()
    HC = EL // 2
    half = pl.ds(pl.multiple_of(core * HC, HC), HC)
    for i in range(2):
        ms, md = load_state(st_out.at[i, :, half])
        ts, td = load_state(st_in.at[i, :, half])
        mine_first = core == i
        state = jnp.where(mine_first, td * ms + ts, md * ts + ms)
        ch_out[i, 0:L, :] = state.astype(BF16)
        ch_out[i, L:L + 16, :] = pack_decay(md * td)
    cha = remote(ch_out, ch_in, chs, chr_, ctx=xmate)
    cha.start()

    late_block(0)

    cha.wait()
    for i in range(2):
        ms, md = load_state(ch_out.at[i])
        ts, td = load_state(ch_in.at[i])
        mine_first = xh == i
        state = jnp.where(mine_first, td * ms + ts, md * ts + ms)
        pl_out[i, 0:L, :] = state.astype(BF16)
        pl_out[i, L:L + 16, :] = pack_decay(md * td)

    def plane(k):
        return remote(
            pl_out.at[(z + k) // 4], pl_in.at[z], pls.at[k - 1], plr.at[k - 1], ctx=(c + 4 * k) % 16
        )

    for k in range(1, 4):
        plane(k).start()
    pl_in[z] = pl_out[0]

    late_block(1)

    for k in range(1, 4):
        plane(k).wait_send()
        pltpu.make_async_remote_copy(
            src_ref=pl_out.at[0], dst_ref=pl_in.at[(z + 4 - k) % 4], send_sem=pls.at[k - 1],
            recv_sem=plr.at[k - 1], device_id={"ctx": (c + 4 * k) % 16, "shard": s}, device_id_type=MESH,
        ).wait_recv()
    for i in range(2):
        acc = jnp.zeros((L, HC), F32)
        for zz in (range(3) if i == 0 else range(3, 0, -1)):
            ps, pd = load_state(pl_in.at[zz])
            acc = jnp.where((zz < z) if i == 0 else (zz > z), pd * acc + ps, acc)
        ts, td = load_state(ch_in.at[i])
        acc = jnp.where(xh != i, td * acc + ts, acc)
        fin_out[i] = acc.astype(BF16)
    fina = remote(fin_out, fin_in, fis, fir, ctx=mate)
    fina.start()
    fina.wait()

    for i in range(2):
        mine, theirs = fin_out[i].astype(F32), fin_in[i].astype(F32)
        entering = jnp.where(
            core == 0, jnp.concatenate([mine, theirs], 1), jnp.concatenate([theirs, mine], 1)
        )
        ts, td = load_state(st_in.at[i])
        state = jnp.where(core != i, td * entering + ts, entering)
        order = range(NC) if i == 0 else range(NC - 1, -1, -1)
        for k in order:
            sst[i, k] = state.astype(BF16)
            state = decs[i][k] * state + sch[i, k]

    def sums(j, k):
        return remote(sq.at[j, s], sq.at[j, s], sqs.at[j, k - 1], sqr.at[j, k - 1], shard=(s + k) % 8)

    def gated_block(j):
        total = jnp.zeros((8, TB), F32)
        for i in range(2):
            pick = jnp.where(iota((8, EL), 0) // 4 == i, 1.0, 0.0).astype(BF16)
            for q in range(TB // L):
                k = j * (TB // L) + q
                rows = slice(k * L, (k + 1) * L)
                eexp = dot(cols[rows, :].astype(BF16), spreads[2 * i + 1])
                yv = ybuf[i, rows, :] + eexp * dot(bc[i, rows, L:2 * L], sst[i, k])
                ybuf[i, rows, :] = yv * gate[i, rows, :]
            rows = slice(j * TB, (j + 1) * TB)
            gv = ybuf[i, rows, :]
            total = total + dot(pick, (gv * gv).astype(BF16), NT)
        sq[j, s] = total
        for k in range(1, 8):
            sums(j, k).start()

    def wait_sums(j):
        for k in range(1, 8):
            sums(j, k).wait_send()
            pltpu.make_async_remote_copy(
                src_ref=sq.at[j, s], dst_ref=sq.at[j, (s + 8 - k) % 8], send_sem=sqs.at[j, k - 1],
                recv_sem=sqr.at[j, k - 1], device_id={"ctx": c, "shard": (s + k) % 8}, device_id_type=MESH,
            ).wait_recv()

    xs = s + 1 - 2 * xl

    def cross(j):
        return remote(
            part.at[j, 1 - xl, :, pl.ds(0, XR), :], rx.at[j], rxs.at[j], rxr.at[j], shard=xs
        )

    def along(j, k):
        yk = (y + k) % 4
        return remote(
            part.at[j, :, yk, pl.ds(XR, TB - XR), :], ry2.at[j, k - 1], ry2s.at[j, k - 1], ry2r.at[j, k - 1],
            shard=yk * 2 + xl,
        )

    def along2(j, k):
        yk = (y + k) % 4
        return remote(qbuf.at[j, yk], ry.at[j, k - 1], rys.at[j, k - 1], ryr.at[j, k - 1], shard=yk * 2 + xl)

    def cross2(j):
        return remote(abuf.at[j], rx2.at[j], rx2s.at[j], rx2r.at[j], shard=xs)

    def product_block(j):
        wait_sums(j)
        total = sq[j, 0]
        for k in range(1, 8):
            total = total + sq[j, k]
        scale = lax.rsqrt(total / E + 1e-05)
        rows = slice(j * TB, (j + 1) * TB)
        for q in range(TB // L):
            col = jnp.concatenate([scale[:, q * L:(q + 1) * L]] * (L // 8), 0).T
            sub = slice(j * TB + q * L, j * TB + (q + 1) * L)
            for i in range(2):
                nv = ybuf[i, sub, :] * col[:, 4 * i:4 * i + 1] * gain_ref[...]
                nrm[sub, i * EL:(i + 1) * EL] = nv.astype(BF16)

        for p in range(8):
            xx = lax.rem(p // 4 + 1 + xl, 2)
            yy = p % 4
            part[j, xx, yy] = dot(nrm[rows, :], wall[:, rows_of(yy * 2 + xx, TB)]).astype(BF16)
            if p == 3:
                cross(j).start()
        for k in range(1, 4):
            along(j, k).start()

    def middle_block(j):
        cross(j).wait()
        for k in range(4):
            yk = (y + k) % 4
            both = part[j, xl, yk, 0:XR, :].astype(F32) + rx[j, yk].astype(F32)
            qbuf[j, yk] = both.astype(BF16)
            if k:
                along2(j, k).start()
        for k in range(1, 4):
            along(j, k).wait()
        for m in range(2):
            xx = (xl + 1 + m) % 2
            acc = part[j, xx, y, XR:TB, :].astype(F32)
            for k in range(1, 4):
                acc = acc + ry2[j, k - 1, xx].astype(F32)
            if m == 0:
                abuf[j] = acc.astype(BF16)
                cross2(j).start()
            else:
                keepbuf = acc
        return keepbuf

    def last_block(j, own):
        for k in range(1, 4):
            along2(j, k).wait()
        acc = qbuf[j, y].astype(F32)
        for k in range(1, 4):
            acc = acc + ry[j, k - 1].astype(F32)
        cross2(j).wait()
        low = own + rx2[j].astype(F32)
        whole = jnp.concatenate([acc, low], 0)
        out_ref[:, j * TB:(j + 1) * TB] = whole.T.astype(BF16)

    kept = [None] * NB
    gated_block(0)
    gated_block(1)
    product_block(0)
    late_block(2)
    gated_block(2)
    product_block(1)
    late_block(3)
    gated_block(3)
    kept[0] = middle_block(0)
    product_block(2)
    kept[1] = middle_block(1)
    product_block(3)
    kept[2] = middle_block(2)
    kept[3] = middle_block(3)
    for j in range(NB):
        last_block(j, kept[j])


def per_device(
    hidden, ids, table, proj_weight, bc_weight, dt_weight, dt_bias, decay, conv_weight, conv_bias, skip,
    norm_gain, out_weight,
):
    T, D = hidden.shape
    EL = conv_bias.shape[0]
    H = EL // HEADDIM
    NB, NC = T // TB, T // L
    vm = pl.BlockSpec(memory_space=pltpu.VMEM)
    sm = pl.BlockSpec(memory_space=pltpu.SMEM)
    hbm = pl.BlockSpec(memory_space=pl.ANY)
    V = pltpu.VMEM
    dma = pltpu.SemaphoreType.DMA
    scratch = [
        V((T, D), BF16), V((T, D), BF16),
        V((D, 2, EL), BF16), V((D, EL), BF16), V((D, EL), BF16), V((2 * EL, D), BF16),
        V((8, 2, 16, D), BF16), V((TB, TB), BF16),
        V((2, T + 16, EL), F32), V((2, T, EL), BF16), V((2, T, 2 * L), BF16),
        V((2, T, EL), F32), V((2, T, EL), F32),
        V((2, NC * H, L), F32), V((NC, L, L), F32), V((T, L), F32), V((2, NC, H, L), F32),
        V((2, NC, L, EL), F32), V((2, NC, L, EL), BF16),
        V((2, 16, EL), BF16), V((2, 16, EL), BF16),
        V((2, L + 16, EL), BF16), V((2, L + 16, EL), BF16),
        V((2, L + 16, EL // 2), BF16), V((2, L + 16, EL // 2), BF16),
        V((2, L + 16, EL // 2), BF16), V((4, L + 16, EL // 2), BF16),
        V((2, L, EL // 2), BF16), V((2, L, EL // 2), BF16),
        V((NB, 8, 8, TB), F32), V((T, 2 * EL), BF16), V((NB, 2, 4, TB, TB), BF16),
        V((NB, 4, XR, TB), BF16), V((NB, 4, XR, TB), BF16), V((NB, 3, XR, TB), BF16),
        V((NB, 3, 2, TB - XR, TB), BF16), V((NB, TB - XR, TB), BF16), V((NB, TB - XR, TB), BF16),
        dma((NB,)), dma((NB,)), dma, dma, dma((7,)), dma((7,)), dma, dma, dma((2,)), dma((2,)), dma, dma, dma, dma,
        dma((3,)), dma((3,)), dma, dma, dma((NB, 7)), dma((NB, 7)),
        dma((NB,)), dma((NB,)), dma((NB, 3)), dma((NB, 3)), dma((NB, 3)), dma((NB, 3)), dma((NB,)), dma((NB,)),
    ]
    return pl.pallas_call(
        kernel,
        out_shape=jax.ShapeDtypeStruct((D // 8, T), BF16),
        in_specs=[hbm, vm, vm, hbm, hbm, vm, vm, vm, vm, hbm, sm, sm, sm],
        out_specs=vm,
        scratch_shapes=scratch,
        compiler_params=pltpu.CompilerParams(
            collective_id=0, has_side_effects=True, vmem_limit_bytes=60 * 1024 * 1024
        ),
        cost_estimate=pl.CostEstimate(flops=20_000_000_000, bytes_accessed=16_000_000, transcendentals=4_000_000),
    )(
        hidden, ids.reshape(1, T), table, proj_weight, bc_weight.T.reshape(2, 16, D), dt_weight.T,
        conv_weight, conv_bias.reshape(1, EL), norm_gain.reshape(1, EL), out_weight,
        dt_bias, decay, skip,
    )


def solution(mesh):
    in_specs = (
        P("ctx", None), P("ctx"), P(), P(None, None, "shard"), P(None, "shard"), P(None, "shard"), P("shard"),
        P("shard"), P(None, "shard"), P("shard"), P("shard"), P("shard"), P("shard", None),
    )
    return jax.shard_map(
        per_device, mesh=mesh, in_specs=in_specs, out_specs=P("shard", "ctx"), check_vma=False
    )
```

```python
import jax
import jax.numpy as jnp
from jax import lax
from jax.experimental import pallas as pl
from jax.experimental.pallas import tpu as pltpu
from jax.sharding import PartitionSpec as P

E = 4096
L = 128
TB = 256
XR = 160
HEADDIM = 64
MESH = pl.DeviceIdType.MESH
F32 = jnp.float32
BF16 = jnp.bfloat16
NT = (((1,), (1,)), ((), ()))
TN = (((0,), (0,)), ((), ()))


def dot(a, b, dims=(((1,), (0,)), ((), ())), **kw):
    return lax.dot_general(a, b, dims, preferred_element_type=F32, **kw)


def silu(x):
    half = 0.5 * x
    return half + half * jnp.tanh(half)


def iota(shape, dim):
    return lax.broadcasted_iota(jnp.int32, shape, dim)


def split(x):
    hi = x.astype(BF16).astype(F32)
    return hi, (x - hi).astype(BF16).astype(F32)


def rows_of(k, size):
    return pl.ds(pl.multiple_of(k * size, size), size)


def kernel(
    hid_hbm, ids_ref, table_ref, w_hbm, bcw_hbm, dtw_ref, cw_ref, cb_ref, gain_ref, wo_hbm,
    dtb_ref, decay_ref, skip_ref,
    out_ref,
    u, ur, wraw, wx, wg, wall, bcw, flip, xin, xc, bt, ct, cm, gate, ybuf, dtraw, rowsbuf, cols, arow, sch, sst,
    halo_out, halo_in, st_out, st_in, ch_out, ch_in, fin_out, fin_in,
    sq, nrm, part, rx, qbuf, ry, ry2, abuf, rx2,
    hsem, wsem, wosem, bsem, bgs, bgr, bcs, bcr, hs, hr, sts, stsr, chs, chr_, fis, fir, sqs, sqr,
    rxs, rxr, rys, ryr, ry2s, ry2r, rx2s, rx2r,
):
    T, D = u.shape
    EL = xc.shape[2]
    NB = T // TB
    NC = T // L
    H = EL // HEADDIM
    c = lax.axis_index("ctx")
    s = lax.axis_index("shard")
    z, xh, core = c // 4, (c // 2) % 2, c % 2
    y, xl = s // 2, s % 2

    def remote(src, dst, ss, rs, ctx=None, shard=None):
        return pltpu.make_async_remote_copy(
            src_ref=src, dst_ref=dst, send_sem=ss, recv_sem=rs,
            device_id={"ctx": c if ctx is None else ctx, "shard": s if shard is None else shard},
            device_id_type=MESH,
        )

    WR = D // NB
    hcopies = [
        pltpu.make_async_copy(hid_hbm.at[pl.ds(b * TB, TB)], u.at[pl.ds(b * TB, TB)], hsem.at[b])
        for b in range(NB)
    ]
    wcopies = [
        pltpu.make_async_copy(w_hbm.at[pl.ds(b * WR, WR)], wraw.at[pl.ds(b * WR, WR)], wsem.at[b])
        for b in range(NB)
    ]
    woc = pltpu.make_async_copy(wo_hbm, wall.at[pl.ds(0, EL)], wosem)
    bown = pltpu.make_async_copy(bcw_hbm.at[core], bcw.at[core * 8 + s], bsem)
    hcopies[0].start()
    for b in range(NB):
        wcopies[b].start()
    bown.start()
    for b in range(1, NB):
        hcopies[b].start()

    mate = c + 1 - 2 * core
    other = (c + 16 + 2 * core - 1) % 16
    chip = c // 2
    barrier = pltpu.get_barrier_semaphore()
    peers = [(mate, s), (other, s)]
    peers += [((c + 2 * k) % 16, s) for k in range(1, 8)]
    peers += [(c, (s + k) % 8) for k in range(1, 8)]
    for pc, ps in peers:
        pl.semaphore_signal(barrier, inc=1, device_id={"ctx": pc, "shard": ps}, device_id_type=MESH)
    pl.semaphore_wait(barrier, len(peers))

    def gather(k):
        return remote(bcw_hbm.at[core], bcw.at[core * 8 + s], bgs.at[k - 1], bgr.at[k - 1], shard=(s + k) % 8)

    for k in range(1, 8):
        gather(k).start()

    flip[...] = jnp.where(iota((TB, TB), 0) + iota((TB, TB), 1) == TB - 1, 1.0, 0.0).astype(BF16)
    bcw[16] = jnp.concatenate([dtw_ref[...].astype(F32), jnp.zeros((16 - H, D), F32)], 0).astype(BF16)
    nd = D // TB
    for b in range(NB):
        rows = slice(b * TB, (b + 1) * TB)
        hcopies[b].wait()
        hot = jnp.where(iota((table_ref.shape[0], TB), 0) == ids_ref[:, rows], 1.0, 0.0).astype(BF16)
        added = dot(hot, table_ref[...], TN)
        u[rows, :] = (u[rows, :].astype(F32) + added).astype(BF16)
        for i in range(nd):
            ur[rows, i * TB:(i + 1) * TB] = dot(
                u[rows, (nd - 1 - i) * TB:(nd - i) * TB], flip[...]
            ).astype(BF16)
        if b == 0:
            for m in range(NB):
                wcopies[m].wait()
                for k in range(WR // L):
                    wr = slice(m * WR + k * L, m * WR + (k + 1) * L)
                    pair = jnp.swapaxes(wraw[wr, :, :], 0, 1)
                    wg[wr, :] = pair[0]
                    wx[wr, :] = pair[1]
        for i, v in enumerate((u, ur)):
            xv = dot(v[rows, :], wx[...]).astype(BF16)
            xin[i, 8 + b * TB:8 + (b + 1) * TB, :] = xv.astype(F32)
    woc.start()

    halo_out[0] = xin[0, T - 8:T + 8, :].astype(BF16)
    halo_out[1] = xin[1, 8:24, :].astype(BF16)
    nxt, prv = (c + 1) % 16, (c + 15) % 16
    hcf = remote(halo_out.at[0], halo_in.at[0], hs.at[0], hr.at[0], ctx=nxt)
    hcr = remote(halo_out.at[1], halo_in.at[1], hs.at[1], hr.at[1], ctx=prv)
    hcf.start()
    hcr.start()

    bown.wait()
    for k in range(1, 8):
        gather(k).wait()
    swap = remote(bcw.at[pl.ds(core * 8, 8)], bcw.at[pl.ds(core * 8, 8)], bcs, bcr, ctx=mate)
    swap.start()
    swap.wait()

    for b in range(NB):
        rows = slice(b * TB, (b + 1) * TB)
        for i, v in enumerate((u, ur)):
            r = dot(bcw[...].reshape(17 * 16, D), v[rows, :], NT)
            half = L // 2
            for m in range(2):
                bt[i, m * half:(m + 1) * half, rows] = r[m * L:m * L + half].astype(BF16)
                ct[i, m * half:(m + 1) * half, rows] = r[m * L + half:(m + 1) * L].astype(BF16)
            for q in range(TB // L):
                k = b * (TB // L) + q
                dtraw[i, k * H:(k + 1) * H, :] = r[2 * L:2 * L + H, q * L:(q + 1) * L]

    head = iota((NC * H, L), 0) % H
    bias = jnp.zeros((NC * H, L), F32)
    rate = jnp.zeros((NC * H, L), F32)
    for h in range(H):
        bias = jnp.where(head == h, dtb_ref[h], bias)
        rate = jnp.where(head == h, decay_ref[h], rate)
    rowsbuf[...] = jnp.zeros_like(rowsbuf)
    before = iota((L, L), 0) <= iota((L, L), 1)
    after = iota((L, L), 0) >= iota((L, L), 1)
    decs = []
    for i in range(2):
        raw = dtraw[i] + bias
        dt = jnp.maximum(raw, 0.0) + jnp.log1p(jnp.exp(-jnp.abs(raw)))
        tri = jnp.where(before if i == 0 else after, 1.0, 0.0)
        g = dot(-dt * rate, tri, precision=lax.Precision.HIGHEST)
        total = g[:, L - 1:L] if i == 0 else g[:, 0:1]
        whi, wlo = split(jnp.exp(total - g) * dt)
        ehi, elo = split(jnp.exp(g))
        a = g - jnp.log(dt)
        owner = iota((NC * H, EL), 0) % H == iota((NC * H, EL), 1) // HEADDIM
        chunk_of = jnp.where(iota((NC, NC * H), 1) // H == iota((NC, NC * H), 0), 1.0, 0.0).astype(BF16)
        thi, tlo = split(jnp.where(owner, jnp.exp(total), 0.0))
        dec_rows = dot(chunk_of, thi.astype(BF16)) + dot(chunk_of, tlo.astype(BF16))
        decs.append([dec_rows[k:k + 1, :] for k in range(NC)])
        for k in range(NC):
            sl = slice(k * H, (k + 1) * H)
            arow[i, k] = a[sl]
            for j, part_ in enumerate((g, whi, wlo, ehi, elo)):
                at = (5 * i + j) * H
                rowsbuf[k, at:at + H, :] = part_[sl]

    er, ec = iota((L, EL), 0), iota((L, EL), 1)

    def spread(first):
        hit = (er >= first) & (er < first + 2 * H) & (er % H == ec // HEADDIM)
        return jnp.where(hit, 1.0, 0.0).astype(BF16)

    spreads = [spread(5 * H * i + H + 2 * H * j) for i in range(2) for j in range(2)]
    for k in range(NC):
        cols[k * L:(k + 1) * L, :] = rowsbuf[k].T

    hcf.wait()
    hcr.wait()
    xin[0, 0:8, :] = jnp.where(c > 0, halo_in[0, 8:16, :].astype(F32), 0.0)
    xin[1, T + 8:T + 16, :] = jnp.where(c < 15, halo_in[1, 0:8, :].astype(F32), 0.0)

    half_w, half_b = 0.5 * cw_ref[...], 0.5 * cb_ref[...]

    def chunk_state(k):
        rows = slice(k * L, (k + 1) * L)
        for i in range(2):
            window = xin[i, k * L:(k + 1) * L + 16, :]
            acc = jnp.zeros((L, EL), F32) + half_b
            for t in range(4):
                at = 8 - 3 + t if i == 0 else 8 + 3 - t
                acc = acc + half_w[t:t + 1, :] * window[at:at + L, :]
            xv = (acc + acc * jnp.tanh(acc)).astype(BF16)
            xc[i, rows, :] = xv
            wexp = dot(cols[rows, :].astype(BF16), spreads[2 * i])
            scaled = (wexp * xv.astype(F32)).astype(BF16)
            sch[i, k] = dot(bt[i, :, rows], scaled)

    for k in range(NC):
        chunk_state(k)

    def pack_decay(d):
        hi, lo = split(d)
        wide = (8, d.shape[1])
        return jnp.concatenate([jnp.broadcast_to(hi, wide), jnp.broadcast_to(lo, wide)], 0).astype(BF16)

    def load_state(ref):
        whole = ref[...]
        tail = whole[L:L + 16].astype(F32)
        return whole[:L].astype(F32), tail[0:1] + tail[8:9]

    for i in range(2):
        state, dec = None, None
        for k in (range(NC) if i == 0 else range(NC - 1, -1, -1)):
            d = decs[i][k]
            state = sch[i, k] if state is None else d * state + sch[i, k]
            dec = d if dec is None else dec * d
        st_out[i, 0:L, :] = state.astype(BF16)
        st_out[i, L:L + 16, :] = pack_decay(dec)

    sta = remote(st_out, st_in, sts, stsr, ctx=mate)
    sta.start()

    lane = iota((L, L), 1)
    sk = jnp.zeros((1, EL), F32)
    for h in range(H):
        sk = jnp.where(iota((1, EL), 1) // HEADDIM == h, skip_ref[h], sk)

    def late_block(j):
        rows = slice(j * TB, (j + 1) * TB)
        for i, v in enumerate((u, ur)):
            gate[i, rows, :] = silu(dot(v[rows, :], wg[...]))
        for k in range(j * (TB // L), (j + 1) * (TB // L)):
            rows = slice(k * L, (k + 1) * L)
            for i in range(2):
                cv = ct[i, :, rows].astype(F32).T.astype(BF16)
                cm[i, rows, :] = cv
                cb = dot(cv, bt[i, :, rows])
                keep = iota((L, L), 0) >= lane if i == 0 else iota((L, L), 0) <= lane
                ar = arow[i, k]
                for q in range(H // 2):
                    ms = []
                    for h in (2 * q, 2 * q + 1):
                        at = 5 * H * i + h
                        d = cols[rows, at:at + 1] - ar[h:h + 1, :]
                        ms.append((jnp.exp(jnp.where(keep, d, -1e30)) * cb).astype(BF16))
                    xp = xc[i, rows, q * L:(q + 1) * L]
                    zero = jnp.zeros_like(xp)
                    left = jnp.where(lane < HEADDIM, xp, zero)
                    right = jnp.where(lane < HEADDIM, zero, xp)
                    yq = dot(jnp.concatenate(ms, 1), jnp.concatenate([left, right], 0))
                    ybuf[i, rows, q * L:(q + 1) * L] = yq + sk[:, q * L:(q + 1) * L] * xp.astype(F32)

    woc.wait()
    for i in range(nd):
        wall[EL:2 * EL, i * TB:(i + 1) * TB] = dot(
            wall[0:EL, (nd - 1 - i) * TB:(nd - i) * TB], flip[...]
        ).astype(BF16)

    sta.wait()
    HC = EL // 2
    half = pl.ds(pl.multiple_of(core * HC, HC), HC)
    for i in range(2):
        ms, md = load_state(st_out.at[i, :, half])
        ts, td = load_state(st_in.at[i, :, half])
        state = jnp.where(core == i, td * ms + ts, md * ts + ms)
        ch_out[i, 0:L, :] = state.astype(BF16)
        ch_out[i, L:L + 16, :] = pack_decay(md * td)

    def chips(k):
        return remote(
            ch_out.at[(chip + k) // 8], ch_in.at[chip], chs.at[k - 1], chr_.at[k - 1], ctx=(c + 2 * k) % 16
        )

    for k in range(1, 8):
        chips(k).start()
    ch_in[chip] = ch_out[0]

    late_block(0)

    late_block(1)

    for k in range(1, 8):
        chips(k).wait_send()
        pltpu.make_async_remote_copy(
            src_ref=ch_out.at[0], dst_ref=ch_in.at[(chip + 8 - k) % 8], send_sem=chs.at[k - 1],
            recv_sem=chr_.at[k - 1], device_id={"ctx": (c + 2 * k) % 16, "shard": s}, device_id_type=MESH,
        ).wait_recv()
    entries = [jnp.zeros((L, HC), F32), jnp.zeros((L, HC), F32)]
    for pp in range(7):
        ps, pd = load_state(ch_in.at[pp])
        entries[0] = jnp.where(pp < chip, pd * entries[0] + ps, entries[0])
    for pp in range(7, 0, -1):
        ps, pd = load_state(ch_in.at[pp])
        entries[1] = jnp.where(pp > chip, pd * entries[1] + ps, entries[1])
    for i in range(2):
        fin_out[i] = entries[i].astype(BF16)
    fina = remote(fin_out, fin_in, fis, fir, ctx=mate)
    fina.start()
    fina.wait()

    for i in range(2):
        mine, theirs = fin_out[i].astype(F32), fin_in[i].astype(F32)
        entering = jnp.where(
            core == 0, jnp.concatenate([mine, theirs], 1), jnp.concatenate([theirs, mine], 1)
        )
        ts, td = load_state(st_in.at[i])
        state = jnp.where(core != i, td * entering + ts, entering)
        order = range(NC) if i == 0 else range(NC - 1, -1, -1)
        for k in order:
            sst[i, k] = state.astype(BF16)
            state = decs[i][k] * state + sch[i, k]

    def sums(j, k):
        return remote(sq.at[j, s], sq.at[j, s], sqs.at[j, k - 1], sqr.at[j, k - 1], shard=(s + k) % 8)

    def gated_block(j):
        total = jnp.zeros((8, TB), F32)
        for i in range(2):
            pick = jnp.where(iota((8, EL), 0) // 4 == i, 1.0, 0.0).astype(BF16)
            for q in range(TB // L):
                k = j * (TB // L) + q
                rows = slice(k * L, (k + 1) * L)
                eexp = dot(cols[rows, :].astype(BF16), spreads[2 * i + 1])
                yv = ybuf[i, rows, :] + eexp * dot(cm[i, rows, :], sst[i, k])
                ybuf[i, rows, :] = yv * gate[i, rows, :]
            rows = slice(j * TB, (j + 1) * TB)
            gv = ybuf[i, rows, :]
            total = total + dot(pick, (gv * gv).astype(BF16), NT)
        sq[j, s] = total
        for k in range(1, 8):
            sums(j, k).start()

    def wait_sums(j):
        for k in range(1, 8):
            sums(j, k).wait_send()
            pltpu.make_async_remote_copy(
                src_ref=sq.at[j, s], dst_ref=sq.at[j, (s + 8 - k) % 8], send_sem=sqs.at[j, k - 1],
                recv_sem=sqr.at[j, k - 1], device_id={"ctx": c, "shard": (s + k) % 8}, device_id_type=MESH,
            ).wait_recv()

    xs = s + 1 - 2 * xl

    def cross(j):
        return remote(
            part.at[j, 1 - xl, :, pl.ds(0, XR), :], rx.at[j], rxs.at[j], rxr.at[j], shard=xs
        )

    def along(j, k):
        yk = (y + k) % 4
        return remote(
            part.at[j, :, yk, pl.ds(XR, TB - XR), :], ry2.at[j, k - 1], ry2s.at[j, k - 1], ry2r.at[j, k - 1],
            shard=yk * 2 + xl,
        )

    def along2(j, k):
        yk = (y + k) % 4
        return remote(qbuf.at[j, yk], ry.at[j, k - 1], rys.at[j, k - 1], ryr.at[j, k - 1], shard=yk * 2 + xl)

    def cross2(j):
        return remote(abuf.at[j], rx2.at[j], rx2s.at[j], rx2r.at[j], shard=xs)

    def product_block(j):
        wait_sums(j)
        total = sq[j, 0]
        for k in range(1, 8):
            total = total + sq[j, k]
        scale = lax.rsqrt(total / E + 1e-05)
        rows = slice(j * TB, (j + 1) * TB)
        for q in range(TB // L):
            col = jnp.concatenate([scale[:, q * L:(q + 1) * L]] * (L // 8), 0).T
            sub = slice(j * TB + q * L, j * TB + (q + 1) * L)
            for i in range(2):
                nv = ybuf[i, sub, :] * col[:, 4 * i:4 * i + 1] * gain_ref[...]
                nrm[sub, i * EL:(i + 1) * EL] = nv.astype(BF16)

        for p in range(8):
            xx = lax.rem(p // 4 + 1 + xl, 2)
            yy = p % 4
            part[j, xx, yy] = dot(nrm[rows, :], wall[:, rows_of(yy * 2 + xx, TB)]).astype(BF16)
            if p == 3:
                cross(j).start()
        for k in range(1, 4):
            along(j, k).start()

    def middle_block(j):
        cross(j).wait()
        for k in range(4):
            yk = (y + k) % 4
            both = part[j, xl, yk, 0:XR, :].astype(F32) + rx[j, yk].astype(F32)
            qbuf[j, yk] = both.astype(BF16)
            if k:
                along2(j, k).start()
        for k in range(1, 4):
            along(j, k).wait()
        for m in range(2):
            xx = (xl + 1 + m) % 2
            acc = part[j, xx, y, XR:TB, :].astype(F32)
            for k in range(1, 4):
                acc = acc + ry2[j, k - 1, xx].astype(F32)
            if m == 0:
                abuf[j] = acc.astype(BF16)
                cross2(j).start()
            else:
                keepbuf = acc
        return keepbuf

    def last_block(j, own):
        for k in range(1, 4):
            along2(j, k).wait()
        acc = qbuf[j, y].astype(F32)
        for k in range(1, 4):
            acc = acc + ry[j, k - 1].astype(F32)
        cross2(j).wait()
        low = own + rx2[j].astype(F32)
        whole = jnp.concatenate([acc, low], 0)
        out_ref[:, j * TB:(j + 1) * TB] = whole.T.astype(BF16)

    kept = [None] * NB
    gated_block(0)
    gated_block(1)
    late_block(2)
    product_block(0)
    gated_block(2)
    product_block(1)
    late_block(3)
    gated_block(3)
    kept[0] = middle_block(0)
    product_block(2)
    kept[1] = middle_block(1)
    product_block(3)
    kept[2] = middle_block(2)
    kept[3] = middle_block(3)
    for j in range(NB):
        last_block(j, kept[j])


def per_device(
    hidden, ids, table, proj_weight, bc_weight, dt_weight, dt_bias, decay, conv_weight, conv_bias, skip,
    norm_gain, out_weight,
):
    T, D = hidden.shape
    EL = conv_bias.shape[0]
    H = EL // HEADDIM
    NB, NC = T // TB, T // L
    vm = pl.BlockSpec(memory_space=pltpu.VMEM)
    sm = pl.BlockSpec(memory_space=pltpu.SMEM)
    hbm = pl.BlockSpec(memory_space=pl.ANY)
    V = pltpu.VMEM
    dma = pltpu.SemaphoreType.DMA
    scratch = [
        V((T, D), BF16), V((T, D), BF16),
        V((D, 2, EL), BF16), V((D, EL), BF16), V((D, EL), BF16), V((2 * EL, D), BF16),
        V((17, 16, D), BF16), V((TB, TB), BF16),
        V((2, T + 16, EL), F32), V((2, T, EL), BF16), V((2, L, T), BF16), V((2, L, T), BF16), V((2, T, L), BF16),
        V((2, T, EL), F32), V((2, T, EL), F32),
        V((2, NC * H, L), F32), V((NC, L, L), F32), V((T, L), F32), V((2, NC, H, L), F32),
        V((2, NC, L, EL), F32), V((2, NC, L, EL), BF16),
        V((2, 16, EL), BF16), V((2, 16, EL), BF16),
        V((2, L + 16, EL), BF16), V((2, L + 16, EL), BF16),
        V((2, L + 16, EL // 2), BF16), V((8, L + 16, EL // 2), BF16),
        V((2, L, EL // 2), BF16), V((2, L, EL // 2), BF16),
        V((NB, 8, 8, TB), F32), V((T, 2 * EL), BF16), V((NB, 2, 4, TB, TB), BF16),
        V((NB, 4, XR, TB), BF16), V((NB, 4, XR, TB), BF16), V((NB, 3, XR, TB), BF16),
        V((NB, 3, 2, TB - XR, TB), BF16), V((NB, TB - XR, TB), BF16), V((NB, TB - XR, TB), BF16),
        dma((NB,)), dma((NB,)), dma, dma, dma((7,)), dma((7,)), dma, dma, dma((2,)), dma((2,)), dma, dma, dma((7,)), dma((7,)),
        dma, dma, dma((NB, 7)), dma((NB, 7)),
        dma((NB,)), dma((NB,)), dma((NB, 3)), dma((NB, 3)), dma((NB, 3)), dma((NB, 3)), dma((NB,)), dma((NB,)),
    ]
    return pl.pallas_call(
        kernel,
        out_shape=jax.ShapeDtypeStruct((D // 8, T), BF16),
        in_specs=[hbm, vm, vm, hbm, hbm, vm, vm, vm, vm, hbm, sm, sm, sm],
        out_specs=vm,
        scratch_shapes=scratch,
        compiler_params=pltpu.CompilerParams(
            collective_id=0, has_side_effects=True, vmem_limit_bytes=60 * 1024 * 1024
        ),
        cost_estimate=pl.CostEstimate(flops=20_000_000_000, bytes_accessed=16_000_000, transcendentals=4_000_000),
    )(
        hidden, ids.reshape(1, T), table, proj_weight, bc_weight.T.reshape(2, 16, D), dt_weight.T,
        conv_weight, conv_bias.reshape(1, EL), norm_gain.reshape(1, EL), out_weight,
        dt_bias, decay, skip,
    )


def solution(mesh):
    in_specs = (
        P("ctx", None), P("ctx"), P(), P(None, None, "shard"), P(None, "shard"), P(None, "shard"), P("shard"),
        P("shard"), P(None, "shard"), P("shard"), P("shard"), P("shard"), P("shard", None),
    )
    return jax.shard_map(
        per_device, mesh=mesh, in_specs=in_specs, out_specs=P("shard", "ctx"), check_vma=False
    )
```

```python
import jax
import jax.numpy as jnp
from jax import lax
from jax.experimental import pallas as pl
from jax.experimental.pallas import tpu as pltpu
from jax.sharding import PartitionSpec as P

E = 4096
L = 128
TB = 256
BLOCKS = (
    (0, 256, 112, 48, 80), (256, 256, 112, 48, 80), (512, 256, 112, 48, 80),
    (768, 128, 64, 32, 32), (896, 128, 64, 32, 32),
)
NR = len(BLOCKS)
XM, XH, YM, YH = 112, 64, 144, 80
HEADDIM = 64
MESH = pl.DeviceIdType.MESH
F32 = jnp.float32
BF16 = jnp.bfloat16
NT = (((1,), (1,)), ((), ()))
TN = (((0,), (0,)), ((), ()))


def dot(a, b, dims=(((1,), (0,)), ((), ())), **kw):
    return lax.dot_general(a, b, dims, preferred_element_type=F32, **kw)


def silu(x):
    half = 0.5 * x
    return half + half * jnp.tanh(half)


def iota(shape, dim):
    return lax.broadcasted_iota(jnp.int32, shape, dim)


def split(x):
    hi = x.astype(BF16).astype(F32)
    return hi, (x - hi).astype(BF16).astype(F32)


def rows_of(k, size):
    return pl.ds(pl.multiple_of(k * size, size), size)


def kernel(
    hid_hbm, ids_ref, table_ref, w_hbm, bcw_hbm, dtw_ref, cw_ref, cb_ref, gain_ref, wo_hbm,
    dtb_ref, decay_ref, skip_ref,
    out_ref,
    u, ur, wraw, wx, wg, wall, bcw, flip, xin, xc, bt, ct, cm, gate, ybuf, dtraw, rowsbuf, cols, arow, sch, sst,
    halo_out, halo_in, st_out, st_in, ch_out, ch_in, fin_out, fin_in,
    sq, nrm, part, rx, qbuf, abuf, rx2, xa, xb, xaa, xba, xprev, xnext, ya, yb, yaa, yba, yprev, ynext,
    hsem, wsem, wosem, bsem, bgs, bgr, bcs, bcr, hs, hr, sts, stsr, chs, chr_, fis, fir, sqs, sqr,
    rxs, rxr, rx2s, rx2r, xss, xsr, yss, ysr,
):
    T, D = u.shape
    EL = xc.shape[2]
    NB = T // TB
    NC = T // L
    H = EL // HEADDIM
    c = lax.axis_index("ctx")
    s = lax.axis_index("shard")
    z, xh, core = c // 4, (c // 2) % 2, c % 2
    y, xl = s // 2, s % 2

    def remote(src, dst, ss, rs, ctx=None, shard=None):
        return pltpu.make_async_remote_copy(
            src_ref=src, dst_ref=dst, send_sem=ss, recv_sem=rs,
            device_id={"ctx": c if ctx is None else ctx, "shard": s if shard is None else shard},
            device_id_type=MESH,
        )

    WR = D // NB
    hcopies = [
        pltpu.make_async_copy(hid_hbm.at[pl.ds(b * TB, TB)], u.at[pl.ds(b * TB, TB)], hsem.at[b])
        for b in range(NB)
    ]
    wcopies = [
        pltpu.make_async_copy(w_hbm.at[pl.ds(b * WR, WR)], wraw.at[pl.ds(b * WR, WR)], wsem.at[b])
        for b in range(NB)
    ]
    woc = pltpu.make_async_copy(wo_hbm, wall.at[pl.ds(0, EL)], wosem)
    bown = pltpu.make_async_copy(bcw_hbm.at[core], bcw.at[core * 8 + s], bsem)
    for b in range(NB):
        hcopies[b].start()
    for b in range(NB):
        wcopies[b].start()
    bown.start()

    mate = c + 1 - 2 * core
    other = (c + 16 + 2 * core - 1) % 16
    chip = c // 2
    barrier = pltpu.get_barrier_semaphore()
    peers = [(mate, s), (other, s)]
    peers += [((c + 2 * k) % 16, s) for k in range(1, 8)]
    peers += [(c, (s + k) % 8) for k in range(1, 8)]
    for pc, ps in peers:
        pl.semaphore_signal(barrier, inc=1, device_id={"ctx": pc, "shard": ps}, device_id_type=MESH)
    pl.semaphore_wait(barrier, len(peers))

    def gather(k):
        return remote(bcw_hbm.at[core], bcw.at[core * 8 + s], bgs.at[k - 1], bgr.at[k - 1], shard=(s + k) % 8)

    for k in range(1, 8):
        gather(k).start()

    flip[...] = jnp.where(iota((TB, TB), 0) + iota((TB, TB), 1) == TB - 1, 1.0, 0.0).astype(BF16)
    bcw[16] = jnp.concatenate([dtw_ref[...].astype(F32), jnp.zeros((16 - H, D), F32)], 0).astype(BF16)
    nd = D // TB
    for b in range(NB):
        rows = slice(b * TB, (b + 1) * TB)
        hcopies[b].wait()
        hot = jnp.where(iota((table_ref.shape[0], TB), 0) == ids_ref[:, rows], 1.0, 0.0).astype(BF16)
        added = dot(hot, table_ref[...], TN)
        u[rows, :] = (u[rows, :].astype(F32) + added).astype(BF16)
        for i in range(nd):
            ur[rows, i * TB:(i + 1) * TB] = dot(
                u[rows, (nd - 1 - i) * TB:(nd - i) * TB], flip[...]
            ).astype(BF16)
    for m in range(NB):
        wcopies[m].wait()
        for k in range(WR // L):
            wr = slice(m * WR + k * L, m * WR + (k + 1) * L)
            pair = jnp.swapaxes(wraw[wr, :, :], 0, 1)
            wg[wr, :] = pair[0]
            wx[wr, :] = pair[1]
    PB = 512
    for b in range(T // PB):
        rows = slice(b * PB, (b + 1) * PB)
        for i, v in enumerate((u, ur)):
            xv = dot(v[rows, :], wx[...]).astype(BF16)
            xin[i, 8 + b * PB:8 + (b + 1) * PB, :] = xv.astype(F32)
    woc.start()

    halo_out[0] = xin[0, T - 8:T + 8, :].astype(BF16)
    halo_out[1] = xin[1, 8:24, :].astype(BF16)
    nxt, prv = (c + 1) % 16, (c + 15) % 16
    hcf = remote(halo_out.at[0], halo_in.at[0], hs.at[0], hr.at[0], ctx=nxt)
    hcr = remote(halo_out.at[1], halo_in.at[1], hs.at[1], hr.at[1], ctx=prv)
    hcf.start()
    hcr.start()

    bown.wait()
    for k in range(1, 8):
        gather(k).wait()
    swap = remote(bcw.at[pl.ds(core * 8, 8)], bcw.at[pl.ds(core * 8, 8)], bcs, bcr, ctx=mate)
    swap.start()

    hcf.wait()
    hcr.wait()
    xin[0, 0:8, :] = jnp.where(c > 0, halo_in[0, 8:16, :].astype(F32), 0.0)
    xin[1, T + 8:T + 16, :] = jnp.where(c < 15, halo_in[1, 0:8, :].astype(F32), 0.0)
    half_w, half_b = 0.5 * cw_ref[...], 0.5 * cb_ref[...]
    for k in range(NC):
        for i in range(2):
            window = xin[i, k * L:(k + 1) * L + 16, :]
            acc = jnp.zeros((L, EL), F32) + half_b
            for t in range(4):
                at = 8 - 3 + t if i == 0 else 8 + 3 - t
                acc = acc + half_w[t:t + 1, :] * window[at:at + L, :]
            xc[i, k * L:(k + 1) * L, :] = (acc + acc * jnp.tanh(acc)).astype(BF16)
    swap.wait()

    for b in range(NB):
        rows = slice(b * TB, (b + 1) * TB)
        for i, v in enumerate((u, ur)):
            r = dot(bcw[...].reshape(17 * 16, D), v[rows, :], NT)
            half = L // 2
            for m in range(2):
                bt[i, m * half:(m + 1) * half, rows] = r[m * L:m * L + half].astype(BF16)
                ct[i, m * half:(m + 1) * half, rows] = r[m * L + half:(m + 1) * L].astype(BF16)
            for q in range(TB // L):
                k = b * (TB // L) + q
                dtraw[i, k * H:(k + 1) * H, :] = r[2 * L:2 * L + H, q * L:(q + 1) * L]

    head = iota((NC * H, L), 0) % H
    bias = jnp.zeros((NC * H, L), F32)
    rate = jnp.zeros((NC * H, L), F32)
    for h in range(H):
        bias = jnp.where(head == h, dtb_ref[h], bias)
        rate = jnp.where(head == h, decay_ref[h], rate)
    rowsbuf[...] = jnp.zeros_like(rowsbuf)
    before = iota((L, L), 0) <= iota((L, L), 1)
    after = iota((L, L), 0) >= iota((L, L), 1)
    decs = []
    for i in range(2):
        raw = dtraw[i] + bias
        dt = jnp.maximum(raw, 0.0) + jnp.log1p(jnp.exp(-jnp.abs(raw)))
        tri = jnp.where(before if i == 0 else after, 1.0, 0.0)
        g = dot(-dt * rate, tri, precision=lax.Precision.HIGHEST)
        total = g[:, L - 1:L] if i == 0 else g[:, 0:1]
        whi, wlo = split(jnp.exp(total - g) * dt)
        ehi, elo = split(jnp.exp(g))
        a = g - jnp.log(dt)
        owner = iota((NC * H, EL), 0) % H == iota((NC * H, EL), 1) // HEADDIM
        chunk_of = jnp.where(iota((NC, NC * H), 1) // H == iota((NC, NC * H), 0), 1.0, 0.0).astype(BF16)
        thi, tlo = split(jnp.where(owner, jnp.exp(total), 0.0))
        dec_rows = dot(chunk_of, thi.astype(BF16)) + dot(chunk_of, tlo.astype(BF16))
        decs.append([dec_rows[k:k + 1, :] for k in range(NC)])
        for k in range(NC):
            sl = slice(k * H, (k + 1) * H)
            arow[i, k] = a[sl]
            for j, part_ in enumerate((g, whi, wlo, ehi, elo)):
                at = (5 * i + j) * H
                rowsbuf[k, at:at + H, :] = part_[sl]

    er, ec = iota((L, EL), 0), iota((L, EL), 1)

    def spread(first):
        hit = (er >= first) & (er < first + 2 * H) & (er % H == ec // HEADDIM)
        return jnp.where(hit, 1.0, 0.0).astype(BF16)

    spreads = [spread(5 * H * i + H + 2 * H * j) for i in range(2) for j in range(2)]
    for k in range(NC):
        cols[k * L:(k + 1) * L, :] = rowsbuf[k].T

    for k in range(NC):
        rows = slice(k * L, (k + 1) * L)
        for i in range(2):
            wexp = dot(cols[rows, :].astype(BF16), spreads[2 * i])
            scaled = (wexp * xc[i, rows, :].astype(F32)).astype(BF16)
            sch[i, k] = dot(bt[i, :, rows], scaled)

    def pack_decay(d):
        hi, lo = split(d)
        wide = (8, d.shape[1])
        return jnp.concatenate([jnp.broadcast_to(hi, wide), jnp.broadcast_to(lo, wide)], 0).astype(BF16)

    def load_state(ref):
        whole = ref[...]
        tail = whole[L:L + 16].astype(F32)
        return whole[:L].astype(F32), tail[0:1] + tail[8:9]

    for i in range(2):
        state, dec = None, None
        for k in (range(NC) if i == 0 else range(NC - 1, -1, -1)):
            d = decs[i][k]
            state = sch[i, k] if state is None else d * state + sch[i, k]
            dec = d if dec is None else dec * d
        st_out[i, 0:L, :] = state.astype(BF16)
        st_out[i, L:L + 16, :] = pack_decay(dec)

    sta = remote(st_out, st_in, sts, stsr, ctx=mate)
    sta.start()

    lane = iota((L, L), 1)
    sk = jnp.zeros((1, EL), F32)
    for h in range(H):
        sk = jnp.where(iota((1, EL), 1) // HEADDIM == h, skip_ref[h], sk)

    def late_block(j):
        rows = slice(j * TB, (j + 1) * TB)
        for i, v in enumerate((u, ur)):
            gate[i, rows, :] = silu(dot(v[rows, :], wg[...]))
        for k in range(j * (TB // L), (j + 1) * (TB // L)):
            rows = slice(k * L, (k + 1) * L)
            for i in range(2):
                cv = ct[i, :, rows].astype(F32).T.astype(BF16)
                cm[i, rows, :] = cv
                cb = dot(cv, bt[i, :, rows])
                keep = iota((L, L), 0) >= lane if i == 0 else iota((L, L), 0) <= lane
                ar = arow[i, k]
                for q in range(H // 2):
                    ms = []
                    for h in (2 * q, 2 * q + 1):
                        at = 5 * H * i + h
                        d = cols[rows, at:at + 1] - ar[h:h + 1, :]
                        ms.append((jnp.exp(jnp.where(keep, d, -1e30)) * cb).astype(BF16))
                    xp = xc[i, rows, q * L:(q + 1) * L]
                    zero = jnp.zeros_like(xp)
                    left = jnp.where(lane < HEADDIM, xp, zero)
                    right = jnp.where(lane < HEADDIM, zero, xp)
                    yq = dot(jnp.concatenate(ms, 1), jnp.concatenate([left, right], 0))
                    ybuf[i, rows, q * L:(q + 1) * L] = yq + sk[:, q * L:(q + 1) * L] * xp.astype(F32)

    woc.wait()
    for i in range(nd):
        wall[EL:2 * EL, i * TB:(i + 1) * TB] = dot(
            wall[0:EL, (nd - 1 - i) * TB:(nd - i) * TB], flip[...]
        ).astype(BF16)

    sta.wait()
    HC = EL // 2
    half = pl.ds(pl.multiple_of(core * HC, HC), HC)
    for i in range(2):
        ms, md = load_state(st_out.at[i, :, half])
        ts, td = load_state(st_in.at[i, :, half])
        state = jnp.where(core == i, td * ms + ts, md * ts + ms)
        ch_out[i, 0:L, :] = state.astype(BF16)
        ch_out[i, L:L + 16, :] = pack_decay(md * td)

    def chips(k):
        return remote(
            ch_out.at[(chip + k) // 8], ch_in.at[chip], chs.at[k - 1], chr_.at[k - 1], ctx=(c + 2 * k) % 16
        )

    for k in range(1, 8):
        chips(k).start()
    ch_in[chip] = ch_out[0]

    late_block(0)

    late_block(1)

    for k in range(1, 8):
        chips(k).wait_send()
        pltpu.make_async_remote_copy(
            src_ref=ch_out.at[0], dst_ref=ch_in.at[(chip + 8 - k) % 8], send_sem=chs.at[k - 1],
            recv_sem=chr_.at[k - 1], device_id={"ctx": (c + 2 * k) % 16, "shard": s}, device_id_type=MESH,
        ).wait_recv()
    entries = [jnp.zeros((L, HC), F32), jnp.zeros((L, HC), F32)]
    for pp in range(7):
        ps, pd = load_state(ch_in.at[pp])
        entries[0] = jnp.where(pp < chip, pd * entries[0] + ps, entries[0])
    for pp in range(7, 0, -1):
        ps, pd = load_state(ch_in.at[pp])
        entries[1] = jnp.where(pp > chip, pd * entries[1] + ps, entries[1])
    for i in range(2):
        fin_out[i] = entries[i].astype(BF16)
    fina = remote(fin_out, fin_in, fis, fir, ctx=mate)
    fina.start()
    fina.wait()

    for i in range(2):
        mine, theirs = fin_out[i].astype(F32), fin_in[i].astype(F32)
        entering = jnp.where(
            core == 0, jnp.concatenate([mine, theirs], 1), jnp.concatenate([theirs, mine], 1)
        )
        ts, td = load_state(st_in.at[i])
        state = jnp.where(core != i, td * entering + ts, entering)
        order = range(NC) if i == 0 else range(NC - 1, -1, -1)
        for k in order:
            sst[i, k] = state.astype(BF16)
            state = decs[i][k] * state + sch[i, k]

    def sums(j, k):
        return remote(sq.at[j, s], sq.at[j, s], sqs.at[j, k - 1], sqr.at[j, k - 1], shard=(s + k) % 8)

    def gated_block(j):
        total = jnp.zeros((8, TB), F32)
        for i in range(2):
            pick = jnp.where(iota((8, EL), 0) // 4 == i, 1.0, 0.0).astype(BF16)
            for q in range(TB // L):
                k = j * (TB // L) + q
                rows = slice(k * L, (k + 1) * L)
                eexp = dot(cols[rows, :].astype(BF16), spreads[2 * i + 1])
                yv = ybuf[i, rows, :] + eexp * dot(cm[i, rows, :], sst[i, k])
                ybuf[i, rows, :] = yv * gate[i, rows, :]
            rows = slice(j * TB, (j + 1) * TB)
            gv = ybuf[i, rows, :]
            total = total + dot(pick, (gv * gv).astype(BF16), NT)
        sq[j, s] = total
        for k in range(1, 8):
            sums(j, k).start()

    def wait_sums(j):
        for k in range(1, 8):
            sums(j, k).wait_send()
            pltpu.make_async_remote_copy(
                src_ref=sq.at[j, s], dst_ref=sq.at[j, (s + 8 - k) % 8], send_sem=sqs.at[j, k - 1],
                recv_sem=sqr.at[j, k - 1], device_id={"ctx": c, "shard": (s + k) % 8}, device_id_type=MESH,
            ).wait_recv()

    xs = s + 1 - 2 * xl
    up, down, across = (y + 1) % 4, (y + 3) % 4, (y + 2) % 4

    def cross(j):
        xr = BLOCKS[j][2]
        return remote(
            part.at[j, 1 - xl, :, pl.ds(0, xr), :], rx.at[j, :, pl.ds(0, xr), :], rxs.at[j], rxr.at[j], shard=xs
        )

    def cross2(j):
        n = BLOCKS[j][1] - BLOCKS[j][2]
        return remote(abuf.at[j, pl.ds(0, n)], rx2.at[j, pl.ds(0, n)], rx2s.at[j], rx2r.at[j], shard=xs)

    def ring_y(j, step):
        n, xr, h0 = BLOCKS[j][1], BLOCKS[j][2], BLOCKS[j][4]
        h1 = n - xr - h0
        lo, hi = pl.ds(0, h0), pl.ds(h0, h1)
        plo, phi = pl.ds(xr, h0), pl.ds(xr + h0, h1)
        src, dst, to = [
            (part.at[j, :, across, plo, :], ya.at[j, :, lo, :], up),
            (part.at[j, :, across, phi, :], yb.at[j, :, pl.ds(0, h1), :], down),
            (part.at[j, :, up, phi, :], yprev.at[j, :, hi, :], up),
            (part.at[j, :, down, plo, :], ynext.at[j, :, lo, :], down),
            (yaa.at[j, :, lo, :], yprev.at[j, :, lo, :], up),
            (yba.at[j, :, pl.ds(0, h1), :], ynext.at[j, :, hi, :], down),
        ][step]
        return remote(src, dst, yss.at[j, step], ysr.at[j, step], shard=to * 2 + xl)

    def ring_x(j, step):
        xr, h0 = BLOCKS[j][2], BLOCKS[j][3]
        h1 = xr - h0
        lo, hi = pl.ds(0, h0), pl.ds(h0, h1)
        src, dst, to = [
            (qbuf.at[j, across, lo, :], xa.at[j, lo, :], up),
            (qbuf.at[j, across, hi, :], xb.at[j, pl.ds(0, h1), :], down),
            (qbuf.at[j, up, hi, :], xprev.at[j, hi, :], up),
            (qbuf.at[j, down, lo, :], xnext.at[j, lo, :], down),
            (xaa.at[j, lo, :], xprev.at[j, lo, :], up),
            (xba.at[j, pl.ds(0, h1), :], xnext.at[j, hi, :], down),
        ][step]
        return remote(src, dst, xss.at[j, step], xsr.at[j, step], shard=to * 2 + xl)

    def product_block(j):
        r0, n, xr = BLOCKS[j][:3]
        tb = r0 // TB
        if r0 % TB == 0:
            wait_sums(tb)
        total = sq[tb, 0]
        for k in range(1, 8):
            total = total + sq[tb, k]
        scale = lax.rsqrt(total / E + 1e-05)
        rows = slice(r0, r0 + n)
        for q in range(r0, r0 + n, L):
            at = q % TB
            col = jnp.concatenate([scale[:, at:at + L]] * (L // 8), 0).T
            sub = slice(q, q + L)
            for i in range(2):
                nv = ybuf[i, sub, :] * col[:, 4 * i:4 * i + 1] * gain_ref[...]
                nrm[sub, i * EL:(i + 1) * EL] = nv.astype(BF16)
        for p in range(8):
            xx = lax.rem(p // 4 + 1 + xl, 2)
            yy = p % 4
            part[j, xx, yy, 0:n, :] = dot(nrm[rows, :], wall[:, rows_of(yy * 2 + xx, TB)]).astype(BF16)
            if p == 3:
                cross(j).start()
        for step in range(4):
            ring_y(j, step).start()

    def middle_block(j):
        n, xr, h0 = BLOCKS[j][1], BLOCKS[j][2], BLOCKS[j][4]
        h1 = n - xr - h0
        cross(j).wait()
        for yk in range(4):
            both = part[j, xl, yk, 0:xr, :].astype(F32) + rx[j, yk, 0:xr, :].astype(F32)
            qbuf[j, yk, 0:xr, :] = both.astype(BF16)
        for step in range(4):
            ring_x(j, step).start()
        for step in range(2):
            ring_y(j, step).wait()
        for m in range(2):
            both = part[j, m, up, xr:xr + h0, :].astype(F32) + ya[j, m, 0:h0, :].astype(F32)
            yaa[j, m, 0:h0, :] = both.astype(BF16)
            both = part[j, m, down, xr + h0:n, :].astype(F32) + yb[j, m, 0:h1, :].astype(F32)
            yba[j, m, 0:h1, :] = both.astype(BF16)
        for step in range(4, 6):
            ring_y(j, step).start()

    def third_block(j):
        n, xr, h0 = BLOCKS[j][1:4]
        h1 = xr - h0
        for step in range(2):
            ring_x(j, step).wait()
        both = qbuf[j, up, 0:h0, :].astype(F32) + xa[j, 0:h0, :].astype(F32)
        xaa[j, 0:h0, :] = both.astype(BF16)
        both = qbuf[j, down, h0:xr, :].astype(F32) + xb[j, 0:h1, :].astype(F32)
        xba[j, 0:h1, :] = both.astype(BF16)
        for step in range(4, 6):
            ring_x(j, step).start()
        for step in range(2, 6):
            ring_y(j, step).wait()
        sums_ = []
        for m in range(2):
            xx = (xl + 1 + m) % 2
            acc = part[j, xx, y, xr:n, :].astype(F32)
            acc = acc + yprev[j, xx, 0:n - xr, :].astype(F32) + ynext[j, xx, 0:n - xr, :].astype(F32)
            sums_.append(acc)
        abuf[j, 0:n - xr, :] = sums_[0].astype(BF16)
        cross2(j).start()
        return sums_[1]

    def last_block(j, own):
        r0, n, xr = BLOCKS[j][:3]
        for step in range(2, 6):
            ring_x(j, step).wait()
        acc = qbuf[j, y, 0:xr, :].astype(F32)
        acc = acc + xprev[j, 0:xr, :].astype(F32) + xnext[j, 0:xr, :].astype(F32)
        cross2(j).wait()
        low = own + rx2[j, 0:n - xr, :].astype(F32)
        out_ref[:, r0:r0 + n] = jnp.concatenate([acc, low], 0).T.astype(BF16)

    kept = [None] * len(BLOCKS)
    gated_block(0)
    gated_block(1)
    late_block(2)
    product_block(0)
    gated_block(2)
    product_block(1)
    late_block(3)
    gated_block(3)
    middle_block(0)
    product_block(2)
    middle_block(1)
    kept[0] = third_block(0)
    product_block(3)
    middle_block(2)
    kept[1] = third_block(1)
    product_block(4)
    last_block(0, kept[0])
    middle_block(3)
    kept[2] = third_block(2)
    middle_block(4)
    last_block(1, kept[1])
    kept[3] = third_block(3)
    kept[4] = third_block(4)
    last_block(2, kept[2])
    last_block(3, kept[3])
    last_block(4, kept[4])


def per_device(
    hidden, ids, table, proj_weight, bc_weight, dt_weight, dt_bias, decay, conv_weight, conv_bias, skip,
    norm_gain, out_weight,
):
    T, D = hidden.shape
    EL = conv_bias.shape[0]
    H = EL // HEADDIM
    NB, NC = T // TB, T // L
    vm = pl.BlockSpec(memory_space=pltpu.VMEM)
    sm = pl.BlockSpec(memory_space=pltpu.SMEM)
    hbm = pl.BlockSpec(memory_space=pl.ANY)
    V = pltpu.VMEM
    dma = pltpu.SemaphoreType.DMA
    scratch = [
        V((T, D), BF16), V((T, D), BF16),
        V((D, 2, EL), BF16), V((D, EL), BF16), V((D, EL), BF16), V((2 * EL, D), BF16),
        V((17, 16, D), BF16), V((TB, TB), BF16),
        V((2, T + 16, EL), F32), V((2, T, EL), BF16), V((2, L, T), BF16), V((2, L, T), BF16), V((2, T, L), BF16),
        V((2, T, EL), F32), V((2, T, EL), F32),
        V((2, NC * H, L), F32), V((NC, L, L), F32), V((T, L), F32), V((2, NC, H, L), F32),
        V((2, NC, L, EL), F32), V((2, NC, L, EL), BF16),
        V((2, 16, EL), BF16), V((2, 16, EL), BF16),
        V((2, L + 16, EL), BF16), V((2, L + 16, EL), BF16),
        V((2, L + 16, EL // 2), BF16), V((8, L + 16, EL // 2), BF16),
        V((2, L, EL // 2), BF16), V((2, L, EL // 2), BF16),
        V((NB, 8, 8, TB), F32), V((T, 2 * EL), BF16), V((NR, 2, 4, TB, TB), BF16),
        V((NR, 4, XM, TB), BF16), V((NR, 4, XM, TB), BF16), V((NR, YM, TB), BF16), V((NR, YM, TB), BF16),
        V((NR, XH, TB), BF16), V((NR, XH, TB), BF16), V((NR, XH, TB), BF16), V((NR, XH, TB), BF16),
        V((NR, XM, TB), BF16), V((NR, XM, TB), BF16),
        V((NR, 2, YH, TB), BF16), V((NR, 2, YH, TB), BF16), V((NR, 2, YH, TB), BF16), V((NR, 2, YH, TB), BF16),
        V((NR, 2, YM, TB), BF16), V((NR, 2, YM, TB), BF16),
        dma((NB,)), dma((NB,)), dma, dma, dma((7,)), dma((7,)), dma, dma, dma((2,)), dma((2,)), dma, dma, dma((7,)), dma((7,)),
        dma, dma, dma((NB, 7)), dma((NB, 7)),
        dma((NR,)), dma((NR,)), dma((NR,)), dma((NR,)), dma((NR, 6)), dma((NR, 6)), dma((NR, 6)), dma((NR, 6)),
    ]
    return pl.pallas_call(
        kernel,
        out_shape=jax.ShapeDtypeStruct((D // 8, T), BF16),
        in_specs=[hbm, vm, vm, hbm, hbm, vm, vm, vm, vm, hbm, sm, sm, sm],
        out_specs=vm,
        scratch_shapes=scratch,
        compiler_params=pltpu.CompilerParams(
            collective_id=0, has_side_effects=True, vmem_limit_bytes=60 * 1024 * 1024
        ),
        cost_estimate=pl.CostEstimate(flops=20_000_000_000, bytes_accessed=16_000_000, transcendentals=4_000_000),
    )(
        hidden, ids.reshape(1, T), table, proj_weight, bc_weight.T.reshape(2, 16, D), dt_weight.T,
        conv_weight, conv_bias.reshape(1, EL), norm_gain.reshape(1, EL), out_weight,
        dt_bias, decay, skip,
    )


def solution(mesh):
    in_specs = (
        P("ctx", None), P("ctx"), P(), P(None, None, "shard"), P(None, "shard"), P(None, "shard"), P("shard"),
        P("shard"), P(None, "shard"), P("shard"), P("shard"), P("shard"), P("shard", None),
    )
    return jax.shard_map(
        per_device, mesh=mesh, in_specs=in_specs, out_specs=P("shard", "ctx"), check_vma=False
    )
```

```python
import jax
import jax.numpy as jnp
from jax import lax
from jax.experimental import pallas as pl
from jax.experimental.pallas import tpu as pltpu
from jax.sharding import PartitionSpec as P

E = 4096
L = 128
TB = 256
BLOCKS = (
    (0, 256, 112, 48, 80), (256, 256, 112, 48, 80), (512, 256, 112, 48, 80),
    (768, 128, 64, 32, 32), (896, 128, 64, 32, 32),
)
NR = len(BLOCKS)
XM, XH, YM, YH = 112, 64, 144, 80
HEADDIM = 64
MESH = pl.DeviceIdType.MESH
F32 = jnp.float32
BF16 = jnp.bfloat16
NT = (((1,), (1,)), ((), ()))
TN = (((0,), (0,)), ((), ()))


def dot(a, b, dims=(((1,), (0,)), ((), ())), **kw):
    return lax.dot_general(a, b, dims, preferred_element_type=F32, **kw)


def silu(x):
    half = 0.5 * x
    return half + half * jnp.tanh(half)


def iota(shape, dim):
    return lax.broadcasted_iota(jnp.int32, shape, dim)


def split(x):
    hi = x.astype(BF16).astype(F32)
    return hi, (x - hi).astype(BF16).astype(F32)


def rows_of(k, size):
    return pl.ds(pl.multiple_of(k * size, size), size)


def kernel(
    hid_hbm, ids_ref, table_ref, w_hbm, bcw_hbm, dtw_ref, cw_ref, cb_ref, gain_ref, wo_hbm,
    dtb_ref, decay_ref, skip_ref,
    out_ref,
    u, ur, wraw, wx, wg, wall, bcw, flip, xin, xc, bt, ct, cm, gate, ybuf, dtraw, rowsbuf, cols, arow, sch, enter,
    halo_out, halo_in, st_out, st_in, ch_out, ch_in, fin_out, fin_in,
    sq, nrm, part, rx, qbuf, abuf, rx2, xa, xb, xaa, xba, xprev, xnext, ya, yb, yaa, yba, yprev, ynext,
    hsem, wsem, wosem, bsem, bgs, bgr, bcs, bcr, hs, hr, sts, stsr, chs, chr_, fis, fir, sqs, sqr,
    rxs, rxr, rx2s, rx2r, xss, xsr, yss, ysr,
):
    T, D = u.shape
    EL = xc.shape[2]
    NB = T // TB
    NC = T // L
    H = EL // HEADDIM
    c = lax.axis_index("ctx")
    s = lax.axis_index("shard")
    z, xh, core = c // 4, (c // 2) % 2, c % 2
    y, xl = s // 2, s % 2

    def remote(src, dst, ss, rs, ctx=None, shard=None):
        return pltpu.make_async_remote_copy(
            src_ref=src, dst_ref=dst, send_sem=ss, recv_sem=rs,
            device_id={"ctx": c if ctx is None else ctx, "shard": s if shard is None else shard},
            device_id_type=MESH,
        )

    WR = D // NB
    hcopies = [
        pltpu.make_async_copy(hid_hbm.at[pl.ds(b * TB, TB)], u.at[pl.ds(b * TB, TB)], hsem.at[b])
        for b in range(NB)
    ]
    wcopies = [
        pltpu.make_async_copy(w_hbm.at[pl.ds(b * WR, WR)], wraw.at[pl.ds(b * WR, WR)], wsem.at[b])
        for b in range(NB)
    ]
    woc = pltpu.make_async_copy(wo_hbm, wall.at[pl.ds(0, EL)], wosem)
    bown = pltpu.make_async_copy(bcw_hbm.at[core], bcw.at[core * 8 + s], bsem)
    for b in range(NB):
        hcopies[b].start()
    for b in range(NB):
        wcopies[b].start()
    bown.start()

    mate = c + 1 - 2 * core
    other = (c + 16 + 2 * core - 1) % 16
    chip = c // 2
    barrier = pltpu.get_barrier_semaphore()
    peers = [(mate, s), (other, s)]
    peers += [((c + 2 * k) % 16, s) for k in range(1, 8)]
    peers += [(c, (s + k) % 8) for k in range(1, 8)]
    for pc, ps in peers:
        pl.semaphore_signal(barrier, inc=1, device_id={"ctx": pc, "shard": ps}, device_id_type=MESH)
    pl.semaphore_wait(barrier, len(peers))

    def gather(k):
        return remote(bcw_hbm.at[core], bcw.at[core * 8 + s], bgs.at[k - 1], bgr.at[s], shard=(s + k) % 8)

    for k in range(1, 8):
        gather(k).start()

    flip[...] = jnp.where(iota((TB, TB), 0) + iota((TB, TB), 1) == TB - 1, 1.0, 0.0).astype(BF16)
    bcw[16] = jnp.concatenate([dtw_ref[...].astype(F32), jnp.zeros((16 - H, D), F32)], 0).astype(BF16)
    nd = D // TB
    for b in range(NB):
        rows = slice(b * TB, (b + 1) * TB)
        hcopies[b].wait()
        hot = jnp.where(iota((table_ref.shape[0], TB), 0) == ids_ref[:, rows], 1.0, 0.0).astype(BF16)
        added = dot(hot, table_ref[...], TN)
        u[rows, :] = (u[rows, :].astype(F32) + added).astype(BF16)
        for i in range(nd):
            ur[rows, i * TB:(i + 1) * TB] = dot(
                u[rows, (nd - 1 - i) * TB:(nd - i) * TB], flip[...]
            ).astype(BF16)
    for m in range(NB):
        wcopies[m].wait()
        for k in range(WR // L):
            wr = slice(m * WR + k * L, m * WR + (k + 1) * L)
            pair = jnp.swapaxes(wraw[wr, :, :], 0, 1)
            wg[wr, :] = pair[0]
            wx[wr, :] = pair[1]
    PB = 512
    for b in range(T // PB):
        rows = slice(b * PB, (b + 1) * PB)
        for i, v in enumerate((u, ur)):
            xv = dot(v[rows, :], wx[...]).astype(BF16)
            xin[i, 8 + b * PB:8 + (b + 1) * PB, :] = xv.astype(F32)
    woc.start()

    halo_out[0] = xin[0, T - 8:T + 8, :].astype(BF16)
    halo_out[1] = xin[1, 8:24, :].astype(BF16)
    nxt, prv = (c + 1) % 16, (c + 15) % 16
    hcf = remote(halo_out.at[0], halo_in.at[0], hs.at[0], hr.at[0], ctx=nxt)
    hcr = remote(halo_out.at[1], halo_in.at[1], hs.at[1], hr.at[1], ctx=prv)
    hcf.start()
    hcr.start()

    def swap(m):
        at = pl.ds(core * 8 + 4 * m, 4)
        return remote(bcw.at[at], bcw.at[at], bcs.at[m], bcr.at[m], ctx=mate)

    bown.wait()
    for m in range(2):
        for src in range(4 * m, 4 * m + 4):
            @pl.when(s != src)
            def _():
                remote(
                    bcw_hbm.at[core], bcw.at[core * 8 + src], bgs.at[0], bgr.at[src], shard=(s + 1) % 8
                ).wait_recv()
        swap(m).start()
    for k in range(1, 8):
        gather(k).wait_send()

    half_w, half_b = 0.5 * cw_ref[...], 0.5 * cb_ref[...]

    def convolve(i, k):
        window = xin[i, k * L:(k + 1) * L + 16, :]
        acc = jnp.zeros((L, EL), F32) + half_b
        for t in range(4):
            at = 8 - 3 + t if i == 0 else 8 + 3 - t
            acc = acc + half_w[t:t + 1, :] * window[at:at + L, :]
        xc[i, k * L:(k + 1) * L, :] = (acc + acc * jnp.tanh(acc)).astype(BF16)

    for k in range(NC):
        if k > 0:
            convolve(0, k)
        if k < NC - 1:
            convolve(1, k)

    def gate_block(j):
        rows = slice(j * TB, (j + 1) * TB)
        for i, v in enumerate((u, ur)):
            gate[i, rows, :] = silu(dot(v[rows, :], wg[...]))

    gate_block(0)
    swap(0).wait()

    wb = jnp.concatenate([bcw[0:4], bcw[8:12], bcw[16:17]], 0).reshape(L + 16, D)
    for b in range(NB):
        rows = slice(b * TB, (b + 1) * TB)
        for i, v in enumerate((u, ur)):
            r = dot(wb, v[rows, :], NT)
            bt[i, :, rows] = r[0:L].astype(BF16)
            for q in range(TB // L):
                k = b * (TB // L) + q
                dtraw[i, k * H:(k + 1) * H, :] = r[L:L + H, q * L:(q + 1) * L]

    head = iota((NC * H, L), 0) % H
    bias = jnp.zeros((NC * H, L), F32)
    rate = jnp.zeros((NC * H, L), F32)
    for h in range(H):
        bias = jnp.where(head == h, dtb_ref[h], bias)
        rate = jnp.where(head == h, decay_ref[h], rate)
    rowsbuf[...] = jnp.zeros_like(rowsbuf)
    before = iota((L, L), 0) <= iota((L, L), 1)
    after = iota((L, L), 0) >= iota((L, L), 1)
    decs = []
    for i in range(2):
        raw = dtraw[i] + bias
        dt = jnp.maximum(raw, 0.0) + jnp.log1p(jnp.exp(-jnp.abs(raw)))
        tri = jnp.where(before if i == 0 else after, 1.0, 0.0)
        g = dot(-dt * rate, tri, precision=lax.Precision.HIGHEST)
        total = g[:, L - 1:L] if i == 0 else g[:, 0:1]
        whi, wlo = split(jnp.exp(total - g) * dt)
        ehi, elo = split(jnp.exp(g))
        a = g - jnp.log(dt)
        owner = iota((NC * H, EL), 0) % H == iota((NC * H, EL), 1) // HEADDIM
        chunk_of = jnp.where(iota((NC, NC * H), 1) // H == iota((NC, NC * H), 0), 1.0, 0.0).astype(BF16)
        thi, tlo = split(jnp.where(owner, jnp.exp(total), 0.0))
        dec_rows = dot(chunk_of, thi.astype(BF16)) + dot(chunk_of, tlo.astype(BF16))
        decs.append([dec_rows[k:k + 1, :] for k in range(NC)])
        for k in range(NC):
            sl = slice(k * H, (k + 1) * H)
            arow[i, k] = a[sl]
            for j, part_ in enumerate((g, whi, wlo, ehi, elo)):
                at = (5 * i + j) * H
                rowsbuf[k, at:at + H, :] = part_[sl]

    er, ec = iota((L, EL), 0), iota((L, EL), 1)

    def spread(first):
        hit = (er >= first) & (er < first + 2 * H) & (er % H == ec // HEADDIM)
        return jnp.where(hit, 1.0, 0.0).astype(BF16)

    spreads = [spread(5 * H * i + H + 2 * H * j) for i in range(2) for j in range(2)]
    for k in range(NC):
        cols[k * L:(k + 1) * L, :] = rowsbuf[k].T

    hcf.wait()
    hcr.wait()
    xin[0, 0:8, :] = jnp.where(c > 0, halo_in[0, 8:16, :].astype(F32), 0.0)
    xin[1, T + 8:T + 16, :] = jnp.where(c < 15, halo_in[1, 0:8, :].astype(F32), 0.0)
    convolve(0, 0)
    convolve(1, NC - 1)
    for k in range(NC):
        rows = slice(k * L, (k + 1) * L)
        for i in range(2):
            wexp = dot(cols[rows, :].astype(BF16), spreads[2 * i])
            scaled = (wexp * xc[i, rows, :].astype(F32)).astype(BF16)
            sch[i, k] = dot(bt[i, :, rows], scaled)

    def pack_decay(d):
        hi, lo = split(d)
        wide = (8, d.shape[1])
        return jnp.concatenate([jnp.broadcast_to(hi, wide), jnp.broadcast_to(lo, wide)], 0).astype(BF16)

    def load_state(ref):
        whole = ref[...]
        tail = whole[L:L + 16].astype(F32)
        return whole[:L].astype(F32), tail[0:1] + tail[8:9]

    reach = [[None] * NC, [None] * NC]
    for i in range(2):
        state, dec = jnp.zeros((L, EL), F32), jnp.ones((1, EL), F32)
        for k in (range(NC) if i == 0 else range(NC - 1, -1, -1)):
            reach[i][k] = dec
            own = sch[i, k]
            sch[i, k] = state
            state = decs[i][k] * state + own
            dec = dec * decs[i][k]
        st_out[i, 0:L, :] = state.astype(BF16)
        st_out[i, L:L + 16, :] = pack_decay(dec)

    sta = remote(st_out, st_in, sts, stsr, ctx=mate)
    sta.start()

    lane = iota((L, L), 1)
    sk = jnp.zeros((1, EL), F32)
    for h in range(H):
        sk = jnp.where(iota((1, EL), 1) // HEADDIM == h, skip_ref[h], sk)

    def late_block(j):
        if j > 0:
            gate_block(j)
        for k in range(j * (TB // L), (j + 1) * (TB // L)):
            rows = slice(k * L, (k + 1) * L)
            for i in range(2):
                cv = ct[i, :, rows].astype(F32).T.astype(BF16)
                cm[i, rows, :] = cv
                cb = dot(cv, bt[i, :, rows])
                keep = iota((L, L), 0) >= lane if i == 0 else iota((L, L), 0) <= lane
                ar = arow[i, k]
                for q in range(H // 2):
                    ms = []
                    for h in (2 * q, 2 * q + 1):
                        at = 5 * H * i + h
                        d = cols[rows, at:at + 1] - ar[h:h + 1, :]
                        ms.append((jnp.exp(jnp.where(keep, d, -1e30)) * cb).astype(BF16))
                    xp = xc[i, rows, q * L:(q + 1) * L]
                    zero = jnp.zeros_like(xp)
                    left = jnp.where(lane < HEADDIM, xp, zero)
                    right = jnp.where(lane < HEADDIM, zero, xp)
                    yq = dot(jnp.concatenate(ms, 1), jnp.concatenate([left, right], 0))
                    ybuf[i, rows, q * L:(q + 1) * L] = yq + sk[:, q * L:(q + 1) * L] * xp.astype(F32)

    swap(1).wait()
    wc = jnp.concatenate([bcw[4:8], bcw[12:16]], 0).reshape(L, D)
    for b in range(NB):
        rows = slice(b * TB, (b + 1) * TB)
        for i, v in enumerate((u, ur)):
            ct[i, :, rows] = dot(wc, v[rows, :], NT).astype(BF16)

    woc.wait()
    for i in range(nd):
        wall[EL:2 * EL, i * TB:(i + 1) * TB] = dot(
            wall[0:EL, (nd - 1 - i) * TB:(nd - i) * TB], flip[...]
        ).astype(BF16)

    sta.wait()
    HC = EL // 2
    half = pl.ds(pl.multiple_of(core * HC, HC), HC)
    for i in range(2):
        ms, md = load_state(st_out.at[i, :, half])
        ts, td = load_state(st_in.at[i, :, half])
        state = jnp.where(core == i, td * ms + ts, md * ts + ms)
        ch_out[i, 0:L, :] = state.astype(BF16)
        ch_out[i, L:L + 16, :] = pack_decay(md * td)

    def chips(k):
        return remote(
            ch_out.at[(chip + k) // 8], ch_in.at[chip], chs.at[k - 1], chr_.at[k - 1], ctx=(c + 2 * k) % 16
        )

    for k in range(1, 8):
        chips(k).start()
    ch_in[chip] = ch_out[0]

    late_block(0)

    late_block(1)
    late_block(2)

    for k in range(1, 8):
        chips(k).wait_send()
        pltpu.make_async_remote_copy(
            src_ref=ch_out.at[0], dst_ref=ch_in.at[(chip + 8 - k) % 8], send_sem=chs.at[k - 1],
            recv_sem=chr_.at[k - 1], device_id={"ctx": (c + 2 * k) % 16, "shard": s}, device_id_type=MESH,
        ).wait_recv()
    entries = [jnp.zeros((L, HC), F32), jnp.zeros((L, HC), F32)]
    for pp in range(7):
        ps, pd = load_state(ch_in.at[pp])
        entries[0] = jnp.where(pp < chip, pd * entries[0] + ps, entries[0])
    for pp in range(7, 0, -1):
        ps, pd = load_state(ch_in.at[pp])
        entries[1] = jnp.where(pp > chip, pd * entries[1] + ps, entries[1])
    for i in range(2):
        fin_out[i] = entries[i].astype(BF16)
    fina = remote(fin_out, fin_in, fis, fir, ctx=mate)
    fina.start()
    fina.wait()

    for i in range(2):
        mine, theirs = fin_out[i].astype(F32), fin_in[i].astype(F32)
        entering = jnp.where(
            core == 0, jnp.concatenate([mine, theirs], 1), jnp.concatenate([theirs, mine], 1)
        )
        ts, td = load_state(st_in.at[i])
        enter[i] = jnp.where(core != i, td * entering + ts, entering)

    def sums(j, k):
        return remote(sq.at[j, s], sq.at[j, s], sqs.at[j, k - 1], sqr.at[j, k - 1], shard=(s + k) % 8)

    def gated_block(j):
        total = jnp.zeros((8, TB), F32)
        for i in range(2):
            pick = jnp.where(iota((8, EL), 0) // 4 == i, 1.0, 0.0).astype(BF16)
            for q in range(TB // L):
                k = j * (TB // L) + q
                rows = slice(k * L, (k + 1) * L)
                eexp = dot(cols[rows, :].astype(BF16), spreads[2 * i + 1])
                yv = ybuf[i, rows, :] + eexp * dot(cm[i, rows, :], (sch[i, k] + reach[i][k] * enter[i]).astype(BF16))
                ybuf[i, rows, :] = yv * gate[i, rows, :]
            rows = slice(j * TB, (j + 1) * TB)
            gv = ybuf[i, rows, :]
            total = total + dot(pick, (gv * gv).astype(BF16), NT)
        sq[j, s] = total
        for k in range(1, 8):
            sums(j, k).start()

    def wait_sums(j):
        for k in range(1, 8):
            sums(j, k).wait_send()
            pltpu.make_async_remote_copy(
                src_ref=sq.at[j, s], dst_ref=sq.at[j, (s + 8 - k) % 8], send_sem=sqs.at[j, k - 1],
                recv_sem=sqr.at[j, k - 1], device_id={"ctx": c, "shard": (s + k) % 8}, device_id_type=MESH,
            ).wait_recv()

    xs = s + 1 - 2 * xl
    up, down, across = (y + 1) % 4, (y + 3) % 4, (y + 2) % 4

    def cross(j):
        xr = BLOCKS[j][2]
        return remote(
            part.at[j, 1 - xl, :, pl.ds(0, xr), :], rx.at[j, :, pl.ds(0, xr), :], rxs.at[j], rxr.at[j], shard=xs
        )

    def cross2(j):
        n = BLOCKS[j][1] - BLOCKS[j][2]
        return remote(abuf.at[j, pl.ds(0, n)], rx2.at[j, pl.ds(0, n)], rx2s.at[j], rx2r.at[j], shard=xs)

    def ring_y(j, step):
        n, xr, h0 = BLOCKS[j][1], BLOCKS[j][2], BLOCKS[j][4]
        h1 = n - xr - h0
        lo, hi = pl.ds(0, h0), pl.ds(h0, h1)
        plo, phi = pl.ds(xr, h0), pl.ds(xr + h0, h1)
        src, dst, to = [
            (part.at[j, :, across, plo, :], ya.at[j, :, lo, :], up),
            (part.at[j, :, across, phi, :], yb.at[j, :, pl.ds(0, h1), :], down),
            (part.at[j, :, up, phi, :], yprev.at[j, :, hi, :], up),
            (part.at[j, :, down, plo, :], ynext.at[j, :, lo, :], down),
            (yaa.at[j, :, lo, :], yprev.at[j, :, lo, :], up),
            (yba.at[j, :, pl.ds(0, h1), :], ynext.at[j, :, hi, :], down),
        ][step]
        return remote(src, dst, yss.at[j, step], ysr.at[j, step], shard=to * 2 + xl)

    def ring_x(j, step):
        xr, h0 = BLOCKS[j][2], BLOCKS[j][3]
        h1 = xr - h0
        lo, hi = pl.ds(0, h0), pl.ds(h0, h1)
        src, dst, to = [
            (qbuf.at[j, across, lo, :], xa.at[j, lo, :], up),
            (qbuf.at[j, across, hi, :], xb.at[j, pl.ds(0, h1), :], down),
            (qbuf.at[j, up, hi, :], xprev.at[j, hi, :], up),
            (qbuf.at[j, down, lo, :], xnext.at[j, lo, :], down),
            (xaa.at[j, lo, :], xprev.at[j, lo, :], up),
            (xba.at[j, pl.ds(0, h1), :], xnext.at[j, hi, :], down),
        ][step]
        return remote(src, dst, xss.at[j, step], xsr.at[j, step], shard=to * 2 + xl)

    def product_block(j):
        r0, n, xr = BLOCKS[j][:3]
        tb = r0 // TB
        if r0 % TB == 0:
            wait_sums(tb)
        total = sq[tb, 0]
        for k in range(1, 8):
            total = total + sq[tb, k]
        scale = lax.rsqrt(total / E + 1e-05)
        rows = slice(r0, r0 + n)
        for q in range(r0, r0 + n, L):
            at = q % TB
            col = jnp.concatenate([scale[:, at:at + L]] * (L // 8), 0).T
            sub = slice(q, q + L)
            for i in range(2):
                nv = ybuf[i, sub, :] * col[:, 4 * i:4 * i + 1] * gain_ref[...]
                nrm[sub, i * EL:(i + 1) * EL] = nv.astype(BF16)
        for p in range(8):
            xx = lax.rem(p // 4 + 1 + xl, 2)
            yy = p % 4
            part[j, xx, yy, 0:n, :] = dot(nrm[rows, :], wall[:, rows_of(yy * 2 + xx, TB)]).astype(BF16)
            if p == 3:
                cross(j).start()
        for step in range(4):
            ring_y(j, step).start()

    def middle_block(j):
        n, xr, h0 = BLOCKS[j][1], BLOCKS[j][2], BLOCKS[j][4]
        h1 = n - xr - h0
        cross(j).wait()
        for yk in range(4):
            both = part[j, xl, yk, 0:xr, :].astype(F32) + rx[j, yk, 0:xr, :].astype(F32)
            qbuf[j, yk, 0:xr, :] = both.astype(BF16)
        for step in range(4):
            ring_x(j, step).start()
        for step in range(2):
            ring_y(j, step).wait()
        for m in range(2):
            both = part[j, m, up, xr:xr + h0, :].astype(F32) + ya[j, m, 0:h0, :].astype(F32)
            yaa[j, m, 0:h0, :] = both.astype(BF16)
            both = part[j, m, down, xr + h0:n, :].astype(F32) + yb[j, m, 0:h1, :].astype(F32)
            yba[j, m, 0:h1, :] = both.astype(BF16)
        for step in range(4, 6):
            ring_y(j, step).start()

    def third_block(j):
        n, xr, h0 = BLOCKS[j][1:4]
        h1 = xr - h0
        for step in range(2):
            ring_x(j, step).wait()
        both = qbuf[j, up, 0:h0, :].astype(F32) + xa[j, 0:h0, :].astype(F32)
        xaa[j, 0:h0, :] = both.astype(BF16)
        both = qbuf[j, down, h0:xr, :].astype(F32) + xb[j, 0:h1, :].astype(F32)
        xba[j, 0:h1, :] = both.astype(BF16)
        for step in range(4, 6):
            ring_x(j, step).start()
        for step in range(2, 6):
            ring_y(j, step).wait()
        sums_ = []
        for m in range(2):
            xx = (xl + 1 + m) % 2
            acc = part[j, xx, y, xr:n, :].astype(F32)
            acc = acc + yprev[j, xx, 0:n - xr, :].astype(F32) + ynext[j, xx, 0:n - xr, :].astype(F32)
            sums_.append(acc)
        abuf[j, 0:n - xr, :] = sums_[0].astype(BF16)
        cross2(j).start()
        return sums_[1]

    def last_block(j, own):
        r0, n, xr = BLOCKS[j][:3]
        for step in range(2, 6):
            ring_x(j, step).wait()
        acc = qbuf[j, y, 0:xr, :].astype(F32)
        acc = acc + xprev[j, 0:xr, :].astype(F32) + xnext[j, 0:xr, :].astype(F32)
        cross2(j).wait()
        low = own + rx2[j, 0:n - xr, :].astype(F32)
        out_ref[:, r0:r0 + n] = jnp.concatenate([acc, low], 0).T

    kept = [None] * len(BLOCKS)
    gated_block(0)
    gated_block(1)
    late_block(3)
    product_block(0)
    gated_block(2)
    product_block(1)
    gated_block(3)
    middle_block(0)
    product_block(2)
    middle_block(1)
    kept[0] = third_block(0)
    product_block(3)
    middle_block(2)
    kept[1] = third_block(1)
    product_block(4)
    last_block(0, kept[0])
    middle_block(3)
    kept[2] = third_block(2)
    middle_block(4)
    last_block(1, kept[1])
    kept[3] = third_block(3)
    kept[4] = third_block(4)
    last_block(2, kept[2])
    last_block(3, kept[3])
    last_block(4, kept[4])


def per_device(
    hidden, ids, table, proj_weight, bc_weight, dt_weight, dt_bias, decay, conv_weight, conv_bias, skip,
    norm_gain, out_weight,
):
    T, D = hidden.shape
    EL = conv_bias.shape[0]
    H = EL // HEADDIM
    NB, NC = T // TB, T // L
    vm = pl.BlockSpec(memory_space=pltpu.VMEM)
    sm = pl.BlockSpec(memory_space=pltpu.SMEM)
    hbm = pl.BlockSpec(memory_space=pl.ANY)
    V = pltpu.VMEM
    dma = pltpu.SemaphoreType.DMA
    scratch = [
        V((T, D), BF16), V((T, D), BF16),
        V((D, 2, EL), BF16), V((D, EL), BF16), V((D, EL), BF16), V((2 * EL, D), BF16),
        V((17, 16, D), BF16), V((TB, TB), BF16),
        V((2, T + 16, EL), F32), V((2, T, EL), BF16), V((2, L, T), BF16), V((2, L, T), BF16), V((2, T, L), BF16),
        V((2, T, EL), F32), V((2, T, EL), F32),
        V((2, NC * H, L), F32), V((NC, L, L), F32), V((T, L), F32), V((2, NC, H, L), F32),
        V((2, NC, L, EL), F32), V((2, L, EL), F32),
        V((2, 16, EL), BF16), V((2, 16, EL), BF16),
        V((2, L + 16, EL), BF16), V((2, L + 16, EL), BF16),
        V((2, L + 16, EL // 2), BF16), V((8, L + 16, EL // 2), BF16),
        V((2, L, EL // 2), BF16), V((2, L, EL // 2), BF16),
        V((NB, 8, 8, TB), F32), V((T, 2 * EL), BF16), V((NR, 2, 4, TB, TB), BF16),
        V((NR, 4, XM, TB), BF16), V((NR, 4, XM, TB), BF16), V((NR, YM, TB), BF16), V((NR, YM, TB), BF16),
        V((NR, XH, TB), BF16), V((NR, XH, TB), BF16), V((NR, XH, TB), BF16), V((NR, XH, TB), BF16),
        V((NR, XM, TB), BF16), V((NR, XM, TB), BF16),
        V((NR, 2, YH, TB), BF16), V((NR, 2, YH, TB), BF16), V((NR, 2, YH, TB), BF16), V((NR, 2, YH, TB), BF16),
        V((NR, 2, YM, TB), BF16), V((NR, 2, YM, TB), BF16),
        dma((NB,)), dma((NB,)), dma, dma, dma((7,)), dma((8,)), dma((2,)), dma((2,)), dma((2,)), dma((2,)), dma, dma, dma((7,)), dma((7,)),
        dma, dma, dma((NB, 7)), dma((NB, 7)),
        dma((NR,)), dma((NR,)), dma((NR,)), dma((NR,)), dma((NR, 6)), dma((NR, 6)), dma((NR, 6)), dma((NR, 6)),
    ]
    return pl.pallas_call(
        kernel,
        out_shape=jax.ShapeDtypeStruct((D // 8, T), F32),
        in_specs=[hbm, vm, vm, hbm, hbm, vm, vm, vm, vm, hbm, sm, sm, sm],
        out_specs=vm,
        scratch_shapes=scratch,
        compiler_params=pltpu.CompilerParams(
            collective_id=0, has_side_effects=True, vmem_limit_bytes=60 * 1024 * 1024
        ),
        cost_estimate=pl.CostEstimate(flops=20_000_000_000, bytes_accessed=16_000_000, transcendentals=4_000_000),
    )(
        hidden, ids.reshape(1, T), table, proj_weight, bc_weight.T.reshape(2, 16, D), dt_weight.T,
        conv_weight, conv_bias.reshape(1, EL), norm_gain.reshape(1, EL), out_weight,
        dt_bias, decay, skip,
    ).astype(BF16)


def solution(mesh):
    in_specs = (
        P("ctx", None), P("ctx"), P(), P(None, None, "shard"), P(None, "shard"), P(None, "shard"), P("shard"),
        P("shard"), P(None, "shard"), P("shard"), P("shard"), P("shard"), P("shard", None),
    )
    return jax.shard_map(
        per_device, mesh=mesh, in_specs=in_specs, out_specs=P("shard", "ctx"), check_vma=False
    )
```

```python
import jax
import jax.numpy as jnp
from jax import lax
from jax.experimental import pallas as pl
from jax.experimental.pallas import tpu as pltpu
from jax.sharding import PartitionSpec as P

E = 4096
L = 128
TB = 256
BLOCKS = (
    (0, 256, 112, 48, 80), (256, 256, 112, 48, 80), (512, 256, 112, 48, 80),
    (768, 128, 64, 32, 32), (896, 128, 64, 32, 32),
)
NR = len(BLOCKS)
XM, XH, YM, YH = 112, 64, 144, 80
HEADDIM = 64
MESH = pl.DeviceIdType.MESH
F32 = jnp.float32
BF16 = jnp.bfloat16
NT = (((1,), (1,)), ((), ()))
TN = (((0,), (0,)), ((), ()))


def dot(a, b, dims=(((1,), (0,)), ((), ())), **kw):
    return lax.dot_general(a, b, dims, preferred_element_type=F32, **kw)


def silu(x):
    half = 0.5 * x
    return half + half * jnp.tanh(half)


def iota(shape, dim):
    return lax.broadcasted_iota(jnp.int32, shape, dim)


def split(x):
    hi = x.astype(BF16).astype(F32)
    return hi, (x - hi).astype(BF16).astype(F32)


def rows_of(k, size):
    return pl.ds(pl.multiple_of(k * size, size), size)


def kernel(
    hid_hbm, ids_ref, table_ref, w_hbm, bcw_hbm, dtw_ref, cw_ref, cb_ref, gain_ref, wo_hbm,
    dtb_ref, decay_ref, skip_ref,
    out_ref,
    u, wraw, wx, wg, wall, bcw, lhs, ob, flip, xin, xc, bt, ct, cm, gate, ybuf, dtraw, rowsbuf, cols, arow, sch, enter,
    halo_out, halo_in, st_out, st_in, ch_out, ch_in, fin_out, fin_in,
    sq, nrm, part, rx, qbuf, abuf, rx2, xa, xb, xaa, xba, xprev, xnext, ya, yb, yaa, yba, yprev, ynext,
    hsem, wsem, wosem, bsem, bgs, bgr, bcs, bcr, hs, hr, sts, stsr, chs, chr_, fis, fir, sqs, sqr,
    rxs, rxr, rx2s, rx2r, osem, xss, xsr, yss, ysr,
):
    T, D = u.shape
    EL = xc.shape[2]
    NB = T // TB
    NC = T // L
    H = EL // HEADDIM
    c = lax.axis_index("ctx")
    s = lax.axis_index("shard")
    z, xh, core = c // 4, (c // 2) % 2, c % 2
    y, xl = s // 2, s % 2

    def remote(src, dst, ss, rs, ctx=None, shard=None):
        return pltpu.make_async_remote_copy(
            src_ref=src, dst_ref=dst, send_sem=ss, recv_sem=rs,
            device_id={"ctx": c if ctx is None else ctx, "shard": s if shard is None else shard},
            device_id_type=MESH,
        )

    WR = D // NB
    hcopies = [
        pltpu.make_async_copy(hid_hbm.at[pl.ds(b * TB, TB)], u.at[pl.ds(b * TB, TB)], hsem.at[b])
        for b in range(NB)
    ]
    wcopies = [
        pltpu.make_async_copy(w_hbm.at[pl.ds(b * WR, WR)], wraw.at[pl.ds(b * WR, WR)], wsem.at[b])
        for b in range(NB)
    ]
    woc = pltpu.make_async_copy(wo_hbm, wall.at[pl.ds(0, EL)], wosem)
    bown = pltpu.make_async_copy(bcw_hbm.at[core], bcw.at[core * 8 + s], bsem)
    for b in range(NB):
        hcopies[b].start()
    for b in range(NB):
        wcopies[b].start()
    bown.start()

    mate = c + 1 - 2 * core
    other = (c + 16 + 2 * core - 1) % 16
    chip = c // 2
    barrier = pltpu.get_barrier_semaphore()
    peers = [(mate, s), (other, s)]
    peers += [((c + 2 * k) % 16, s) for k in range(1, 8)]
    peers += [(c, (s + k) % 8) for k in range(1, 8)]
    for pc, ps in peers:
        pl.semaphore_signal(barrier, inc=1, device_id={"ctx": pc, "shard": ps}, device_id_type=MESH)
    pl.semaphore_wait(barrier, len(peers))

    def gather(k):
        return remote(bcw_hbm.at[core], bcw.at[core * 8 + s], bgs.at[k - 1], bgr.at[s], shard=(s + k) % 8)

    for k in range(1, 8):
        gather(k).start()

    flip[...] = jnp.where(iota((TB, TB), 0) + iota((TB, TB), 1) == TB - 1, 1.0, 0.0).astype(BF16)
    bcw[16] = jnp.concatenate([dtw_ref[...].astype(F32), jnp.zeros((16 - H, D), F32)], 0).astype(BF16)
    nd = D // TB

    def mirror_rows(w, i):
        w[1, (nd - 1 - i) * TB:(nd - i) * TB, :] = dot(flip[...], w[0, i * TB:(i + 1) * TB, :]).astype(BF16)

    def mirror_columns(v):
        parts = [dot(v[:, (nd - 1 - i) * TB:(nd - i) * TB], flip[...]).astype(BF16) for i in range(nd)]
        return jnp.concatenate(parts, 1)

    for b in range(NB):
        rows = slice(b * TB, (b + 1) * TB)
        hcopies[b].wait()
        hot = jnp.where(iota((table_ref.shape[0], TB), 0) == ids_ref[:, rows], 1.0, 0.0).astype(BF16)
        added = dot(hot, table_ref[...], TN)
        u[rows, :] = (u[rows, :].astype(F32) + added).astype(BF16)
    for m in range(NB):
        wcopies[m].wait()
        for k in range(WR // L):
            wr = slice(m * WR + k * L, m * WR + (k + 1) * L)
            pair = jnp.swapaxes(wraw[wr, :, :], 0, 1)
            wg[0, wr, :] = pair[0]
            wx[0, wr, :] = pair[1]
        for i in range(m * WR // TB, (m + 1) * WR // TB):
            mirror_rows(wx, i)
    PB = 512
    for b in range(T // PB):
        rows = slice(b * PB, (b + 1) * PB)
        for i in range(2):
            xv = dot(u[rows, :], wx[i]).astype(BF16)
            xin[i, 8 + b * PB:8 + (b + 1) * PB, :] = xv.astype(F32)
    woc.start()

    halo_out[0] = xin[0, T - 8:T + 8, :].astype(BF16)
    halo_out[1] = xin[1, 8:24, :].astype(BF16)
    nxt, prv = (c + 1) % 16, (c + 15) % 16
    hcf = remote(halo_out.at[0], halo_in.at[0], hs.at[0], hr.at[0], ctx=nxt)
    hcr = remote(halo_out.at[1], halo_in.at[1], hs.at[1], hr.at[1], ctx=prv)
    hcf.start()
    hcr.start()

    def swap(m):
        at = pl.ds(core * 8 + 4 * m, 4)
        return remote(bcw.at[at], bcw.at[at], bcs.at[m], bcr.at[m], ctx=mate)

    bown.wait()
    for m in range(2):
        for src in range(4 * m, 4 * m + 4):
            @pl.when(s != src)
            def _():
                remote(
                    bcw_hbm.at[core], bcw.at[core * 8 + src], bgs.at[0], bgr.at[src], shard=(s + 1) % 8
                ).wait_recv()
        swap(m).start()
    for k in range(1, 8):
        gather(k).wait_send()

    half_w, half_b = 0.5 * cw_ref[...], 0.5 * cb_ref[...]

    def convolve(i, k):
        window = xin[i, k * L:(k + 1) * L + 16, :]
        acc = jnp.zeros((L, EL), F32) + half_b
        for t in range(4):
            at = 8 - 3 + t if i == 0 else 8 + 3 - t
            acc = acc + half_w[t:t + 1, :] * window[at:at + L, :]
        xc[i, k * L:(k + 1) * L, :] = (acc + acc * jnp.tanh(acc)).astype(BF16)

    for k in range(NC):
        if k > 0:
            convolve(0, k)
        if k < NC - 1:
            convolve(1, k)

    def gate_block(j):
        rows = slice(j * TB, (j + 1) * TB)
        for i in range(2):
            gate[i, rows, :] = silu(dot(u[rows, :], wg[i]))

    swap(0).wait()

    wb = jnp.concatenate([bcw[0:4], bcw[8:12], bcw[16:17]], 0).reshape(L + 16, D)
    lhs[0:L + 16, :] = wb
    lhs[L + 16:2 * (L + 16), :] = mirror_columns(wb)
    for b in range(NB):
        rows = slice(b * TB, (b + 1) * TB)
        both = dot(lhs[...], u[rows, :], NT)
        for i in range(2):
            r = both[i * (L + 16):(i + 1) * (L + 16)]
            bt[i, :, rows] = r[0:L].astype(BF16)
            for q in range(TB // L):
                k = b * (TB // L) + q
                dtraw[i, k * H:(k + 1) * H, :] = r[L:L + H, q * L:(q + 1) * L]

    head = iota((NC * H, L), 0) % H
    bias = jnp.zeros((NC * H, L), F32)
    rate = jnp.zeros((NC * H, L), F32)
    for h in range(H):
        bias = jnp.where(head == h, dtb_ref[h], bias)
        rate = jnp.where(head == h, decay_ref[h], rate)
    rowsbuf[...] = jnp.zeros_like(rowsbuf)
    before = iota((L, L), 0) <= iota((L, L), 1)
    after = iota((L, L), 0) >= iota((L, L), 1)
    decs = []
    for i in range(2):
        raw = dtraw[i] + bias
        dt = jnp.maximum(raw, 0.0) + jnp.log1p(jnp.exp(-jnp.abs(raw)))
        tri = jnp.where(before if i == 0 else after, 1.0, 0.0)
        g = dot(-dt * rate, tri, precision=lax.Precision.HIGHEST)
        total = g[:, L - 1:L] if i == 0 else g[:, 0:1]
        whi, wlo = split(jnp.exp(total - g) * dt)
        ehi, elo = split(jnp.exp(g))
        a = g - jnp.log(dt)
        owner = iota((NC * H, EL), 0) % H == iota((NC * H, EL), 1) // HEADDIM
        chunk_of = jnp.where(iota((NC, NC * H), 1) // H == iota((NC, NC * H), 0), 1.0, 0.0).astype(BF16)
        thi, tlo = split(jnp.where(owner, jnp.exp(total), 0.0))
        dec_rows = dot(chunk_of, thi.astype(BF16)) + dot(chunk_of, tlo.astype(BF16))
        decs.append([dec_rows[k:k + 1, :] for k in range(NC)])
        for k in range(NC):
            sl = slice(k * H, (k + 1) * H)
            arow[i, k] = a[sl]
            for j, part_ in enumerate((g, whi, wlo, ehi, elo)):
                at = (5 * i + j) * H
                rowsbuf[k, at:at + H, :] = part_[sl]

    er, ec = iota((L, EL), 0), iota((L, EL), 1)

    def spread(first):
        hit = (er >= first) & (er < first + 2 * H) & (er % H == ec // HEADDIM)
        return jnp.where(hit, 1.0, 0.0).astype(BF16)

    spreads = [spread(5 * H * i + H + 2 * H * j) for i in range(2) for j in range(2)]
    for k in range(NC):
        cols[k * L:(k + 1) * L, :] = rowsbuf[k].T

    hcf.wait()
    hcr.wait()
    xin[0, 0:8, :] = jnp.where(c > 0, halo_in[0, 8:16, :].astype(F32), 0.0)
    xin[1, T + 8:T + 16, :] = jnp.where(c < 15, halo_in[1, 0:8, :].astype(F32), 0.0)

    def chunk_states(i):
        convolve(i, 0 if i == 0 else NC - 1)
        for k in range(NC):
            rows = slice(k * L, (k + 1) * L)
            wexp = dot(cols[rows, :].astype(BF16), spreads[2 * i])
            scaled = (wexp * xc[i, rows, :].astype(F32)).astype(BF16)
            sch[i, k] = dot(bt[i, :, rows], scaled)

    def pack_decay(d):
        hi, lo = split(d)
        wide = (8, d.shape[1])
        return jnp.concatenate([jnp.broadcast_to(hi, wide), jnp.broadcast_to(lo, wide)], 0).astype(BF16)

    def load_state(ref):
        whole = ref[...]
        tail = whole[L:L + 16].astype(F32)
        return whole[:L].astype(F32), tail[0:1] + tail[8:9]

    reach = [[None] * NC, [None] * NC]

    def device_state(i):
        state, dec = jnp.zeros((L, EL), F32), jnp.ones((1, EL), F32)
        for k in (range(NC) if i == 0 else range(NC - 1, -1, -1)):
            reach[i][k] = dec
            own = sch[i, k]
            sch[i, k] = state
            state = decs[i][k] * state + own
            dec = dec * decs[i][k]
        st_out[i, 0:L, :] = state.astype(BF16)
        st_out[i, L:L + 16, :] = pack_decay(dec)

    def mates(i):
        return remote(st_out.at[i], st_in.at[i], sts.at[i], stsr.at[i], ctx=mate)

    HC = EL // 2
    half = pl.ds(pl.multiple_of(core * HC, HC), HC)

    def chips(k, i):
        return remote(ch_out.at[i], ch_in.at[chip], chs.at[k - 1], chr_.at[k - 1], ctx=(c + 2 * k) % 16)

    def chip_state(i):
        mates(i).wait()
        ms, md = load_state(st_out.at[i, :, half])
        ts, td = load_state(st_in.at[i, :, half])
        state = jnp.where(core == i, td * ms + ts, md * ts + ms)
        ch_out[i, 0:L, :] = state.astype(BF16)
        ch_out[i, L:L + 16, :] = pack_decay(md * td)
        for k in range(1, 8):
            @pl.when((chip + k) // 8 == i)
            def _():
                chips(k, i).start()

    chunk_states(0)
    device_state(0)
    mates(0).start()
    chunk_states(1)
    chip_state(0)
    device_state(1)
    mates(1).start()

    lane = iota((L, L), 1)
    sk = jnp.zeros((1, EL), F32)
    for h in range(H):
        sk = jnp.where(iota((1, EL), 1) // HEADDIM == h, skip_ref[h], sk)

    def late_block(j):
        gate_block(j)
        for k in range(j * (TB // L), (j + 1) * (TB // L)):
            rows = slice(k * L, (k + 1) * L)
            for i in range(2):
                cv = ct[i, :, rows].astype(F32).T.astype(BF16)
                cm[i, rows, :] = cv
                cb = dot(cv, bt[i, :, rows])
                keep = iota((L, L), 0) >= lane if i == 0 else iota((L, L), 0) <= lane
                ar = arow[i, k]
                for q in range(H // 2):
                    ms = []
                    for h in (2 * q, 2 * q + 1):
                        at = 5 * H * i + h
                        d = cols[rows, at:at + 1] - ar[h:h + 1, :]
                        ms.append((jnp.exp(jnp.where(keep, d, -1e30)) * cb).astype(BF16))
                    xp = xc[i, rows, q * L:(q + 1) * L]
                    zero = jnp.zeros_like(xp)
                    left = jnp.where(lane < HEADDIM, xp, zero)
                    right = jnp.where(lane < HEADDIM, zero, xp)
                    yq = dot(jnp.concatenate(ms, 1), jnp.concatenate([left, right], 0))
                    ybuf[i, rows, q * L:(q + 1) * L] = yq + sk[:, q * L:(q + 1) * L] * xp.astype(F32)

    swap(1).wait()
    wc = jnp.concatenate([bcw[4:8], bcw[12:16]], 0).reshape(L, D)
    lhs[0:L, :] = wc
    lhs[L:2 * L, :] = mirror_columns(wc)
    for i in range(nd):
        mirror_rows(wg, i)
    chip_state(1)
    ch_in[chip] = ch_out[0]
    for b in range(NB):
        rows = slice(b * TB, (b + 1) * TB)
        both = dot(lhs[0:2 * L, :], u[rows, :], NT)
        for i in range(2):
            ct[i, :, rows] = both[i * L:(i + 1) * L].astype(BF16)

    woc.wait()
    for i in range(nd):
        wall[EL:2 * EL, i * TB:(i + 1) * TB] = dot(
            wall[0:EL, (nd - 1 - i) * TB:(nd - i) * TB], flip[...]
        ).astype(BF16)

    late_block(0)

    late_block(1)
    late_block(2)

    for k in range(1, 8):
        chips(k, 0).wait_send()
        pltpu.make_async_remote_copy(
            src_ref=ch_out.at[0], dst_ref=ch_in.at[(chip + 8 - k) % 8], send_sem=chs.at[k - 1],
            recv_sem=chr_.at[k - 1], device_id={"ctx": (c + 2 * k) % 16, "shard": s}, device_id_type=MESH,
        ).wait_recv()
    entries = [jnp.zeros((L, HC), F32), jnp.zeros((L, HC), F32)]
    for pp in range(7):
        ps, pd = load_state(ch_in.at[pp])
        entries[0] = jnp.where(pp < chip, pd * entries[0] + ps, entries[0])
    for pp in range(7, 0, -1):
        ps, pd = load_state(ch_in.at[pp])
        entries[1] = jnp.where(pp > chip, pd * entries[1] + ps, entries[1])
    for i in range(2):
        fin_out[i] = entries[i].astype(BF16)
    fina = remote(fin_out, fin_in, fis, fir, ctx=mate)
    fina.start()
    fina.wait()

    for i in range(2):
        mine, theirs = fin_out[i].astype(F32), fin_in[i].astype(F32)
        entering = jnp.where(
            core == 0, jnp.concatenate([mine, theirs], 1), jnp.concatenate([theirs, mine], 1)
        )
        ts, td = load_state(st_in.at[i])
        enter[i] = jnp.where(core != i, td * entering + ts, entering)

    def sums(j, k):
        return remote(sq.at[j, s], sq.at[j, s], sqs.at[j, k - 1], sqr.at[j, k - 1], shard=(s + k) % 8)

    def gated_block(j):
        total = jnp.zeros((8, TB), F32)
        for i in range(2):
            pick = jnp.where(iota((8, EL), 0) // 4 == i, 1.0, 0.0).astype(BF16)
            for q in range(TB // L):
                k = j * (TB // L) + q
                rows = slice(k * L, (k + 1) * L)
                eexp = dot(cols[rows, :].astype(BF16), spreads[2 * i + 1])
                yv = ybuf[i, rows, :] + eexp * dot(cm[i, rows, :], (sch[i, k] + reach[i][k] * enter[i]).astype(BF16))
                ybuf[i, rows, :] = yv * gate[i, rows, :]
            rows = slice(j * TB, (j + 1) * TB)
            gv = ybuf[i, rows, :]
            total = total + dot(pick, (gv * gv).astype(BF16), NT)
        sq[j, s] = total
        for k in range(1, 8):
            sums(j, k).start()

    def wait_sums(j):
        for k in range(1, 8):
            sums(j, k).wait_send()
            pltpu.make_async_remote_copy(
                src_ref=sq.at[j, s], dst_ref=sq.at[j, (s + 8 - k) % 8], send_sem=sqs.at[j, k - 1],
                recv_sem=sqr.at[j, k - 1], device_id={"ctx": c, "shard": (s + k) % 8}, device_id_type=MESH,
            ).wait_recv()

    xs = s + 1 - 2 * xl
    up, down, across = (y + 1) % 4, (y + 3) % 4, (y + 2) % 4

    def cross(j):
        xr = BLOCKS[j][2]
        return remote(
            part.at[j, 1 - xl, :, pl.ds(0, xr), :], rx.at[j, :, pl.ds(0, xr), :], rxs.at[j], rxr.at[j], shard=xs
        )

    def cross2(j):
        n = BLOCKS[j][1] - BLOCKS[j][2]
        return remote(abuf.at[j, pl.ds(0, n)], rx2.at[j, pl.ds(0, n)], rx2s.at[j], rx2r.at[j], shard=xs)

    def ring_y(j, step):
        n, xr, h0 = BLOCKS[j][1], BLOCKS[j][2], BLOCKS[j][4]
        h1 = n - xr - h0
        lo, hi = pl.ds(0, h0), pl.ds(h0, h1)
        plo, phi = pl.ds(xr, h0), pl.ds(xr + h0, h1)
        src, dst, to = [
            (part.at[j, :, across, plo, :], ya.at[j, :, lo, :], up),
            (part.at[j, :, across, phi, :], yb.at[j, :, pl.ds(0, h1), :], down),
            (part.at[j, :, up, phi, :], yprev.at[j, :, hi, :], up),
            (part.at[j, :, down, plo, :], ynext.at[j, :, lo, :], down),
            (yaa.at[j, :, lo, :], yprev.at[j, :, lo, :], up),
            (yba.at[j, :, pl.ds(0, h1), :], ynext.at[j, :, hi, :], down),
        ][step]
        return remote(src, dst, yss.at[j, step], ysr.at[j, step], shard=to * 2 + xl)

    def ring_x(j, step):
        xr, h0 = BLOCKS[j][2], BLOCKS[j][3]
        h1 = xr - h0
        lo, hi = pl.ds(0, h0), pl.ds(h0, h1)
        src, dst, to = [
            (qbuf.at[j, across, lo, :], xa.at[j, lo, :], up),
            (qbuf.at[j, across, hi, :], xb.at[j, pl.ds(0, h1), :], down),
            (qbuf.at[j, up, hi, :], xprev.at[j, hi, :], up),
            (qbuf.at[j, down, lo, :], xnext.at[j, lo, :], down),
            (xaa.at[j, lo, :], xprev.at[j, lo, :], up),
            (xba.at[j, pl.ds(0, h1), :], xnext.at[j, hi, :], down),
        ][step]
        return remote(src, dst, xss.at[j, step], xsr.at[j, step], shard=to * 2 + xl)

    def product_block(j):
        r0, n, xr = BLOCKS[j][:3]
        tb = r0 // TB
        if r0 % TB == 0:
            wait_sums(tb)
        total = sq[tb, 0]
        for k in range(1, 8):
            total = total + sq[tb, k]
        scale = lax.rsqrt(total / E + 1e-05)
        rows = slice(r0, r0 + n)
        for q in range(r0, r0 + n, L):
            at = q % TB
            col = jnp.concatenate([scale[:, at:at + L]] * (L // 8), 0).T
            sub = slice(q, q + L)
            for i in range(2):
                nv = ybuf[i, sub, :] * col[:, 4 * i:4 * i + 1] * gain_ref[...]
                nrm[sub, i * EL:(i + 1) * EL] = nv.astype(BF16)
        for p in range(8):
            xx = lax.rem(p // 4 + 1 + xl, 2)
            yy = p % 4
            part[j, xx, yy, 0:n, :] = dot(nrm[rows, :], wall[:, rows_of(yy * 2 + xx, TB)]).astype(BF16)
            if p == 3:
                cross(j).start()
        for step in range(4):
            ring_y(j, step).start()

    def middle_block(j):
        n, xr, h0 = BLOCKS[j][1], BLOCKS[j][2], BLOCKS[j][4]
        h1 = n - xr - h0
        cross(j).wait()
        for yk in range(4):
            both = part[j, xl, yk, 0:xr, :].astype(F32) + rx[j, yk, 0:xr, :].astype(F32)
            qbuf[j, yk, 0:xr, :] = both.astype(BF16)
        for step in range(4):
            ring_x(j, step).start()
        for step in range(2):
            ring_y(j, step).wait()
        for m in range(2):
            both = part[j, m, up, xr:xr + h0, :].astype(F32) + ya[j, m, 0:h0, :].astype(F32)
            yaa[j, m, 0:h0, :] = both.astype(BF16)
            both = part[j, m, down, xr + h0:n, :].astype(F32) + yb[j, m, 0:h1, :].astype(F32)
            yba[j, m, 0:h1, :] = both.astype(BF16)
        for step in range(4, 6):
            ring_y(j, step).start()

    def third_block(j):
        n, xr, h0 = BLOCKS[j][1:4]
        h1 = xr - h0
        for step in range(2):
            ring_x(j, step).wait()
        both = qbuf[j, up, 0:h0, :].astype(F32) + xa[j, 0:h0, :].astype(F32)
        xaa[j, 0:h0, :] = both.astype(BF16)
        both = qbuf[j, down, h0:xr, :].astype(F32) + xb[j, 0:h1, :].astype(F32)
        xba[j, 0:h1, :] = both.astype(BF16)
        for step in range(4, 6):
            ring_x(j, step).start()
        for step in range(2, 6):
            ring_y(j, step).wait()
        sums_ = []
        for m in range(2):
            xx = (xl + 1 + m) % 2
            acc = part[j, xx, y, xr:n, :].astype(F32)
            acc = acc + yprev[j, xx, 0:n - xr, :].astype(F32) + ynext[j, xx, 0:n - xr, :].astype(F32)
            sums_.append(acc)
        abuf[j, 0:n - xr, :] = sums_[0].astype(BF16)
        cross2(j).start()
        return sums_[1]

    def last_block(j, own):
        r0, n, xr = BLOCKS[j][:3]
        for step in range(2, 6):
            ring_x(j, step).wait()
        acc = qbuf[j, y, 0:xr, :].astype(F32)
        acc = acc + xprev[j, 0:xr, :].astype(F32) + xnext[j, 0:xr, :].astype(F32)
        cross2(j).wait()
        low = own + rx2[j, 0:n - xr, :].astype(F32)
        ob[:, r0:r0 + n] = jnp.concatenate([acc, low], 0).T.astype(BF16)
        leave(j).start()

    def leave(j):
        at = pl.ds(BLOCKS[j][0], BLOCKS[j][1])
        return pltpu.make_async_copy(ob.at[:, at], out_ref.at[:, at], osem.at[j])

    kept = [None] * len(BLOCKS)
    gated_block(0)
    gated_block(1)
    late_block(3)
    product_block(0)
    gated_block(2)
    product_block(1)
    gated_block(3)
    middle_block(0)
    product_block(2)
    middle_block(1)
    kept[0] = third_block(0)
    product_block(3)
    middle_block(2)
    kept[1] = third_block(1)
    product_block(4)
    last_block(0, kept[0])
    middle_block(3)
    kept[2] = third_block(2)
    middle_block(4)
    last_block(1, kept[1])
    kept[3] = third_block(3)
    kept[4] = third_block(4)
    last_block(2, kept[2])
    last_block(3, kept[3])
    last_block(4, kept[4])
    for j in range(NR):
        leave(j).wait()


def per_device(
    hidden, ids, table, proj_weight, bc_weight, dt_weight, dt_bias, decay, conv_weight, conv_bias, skip,
    norm_gain, out_weight,
):
    T, D = hidden.shape
    EL = conv_bias.shape[0]
    H = EL // HEADDIM
    NB, NC = T // TB, T // L
    vm = pl.BlockSpec(memory_space=pltpu.VMEM)
    sm = pl.BlockSpec(memory_space=pltpu.SMEM)
    hbm = pl.BlockSpec(memory_space=pl.ANY)
    V = pltpu.VMEM
    dma = pltpu.SemaphoreType.DMA
    scratch = [
        V((T, D), BF16),
        V((D, 2, EL), BF16), V((2, D, EL), BF16), V((2, D, EL), BF16), V((2 * EL, D), BF16),
        V((17, 16, D), BF16), V((2 * (L + 16), D), BF16), V((D // 8, T), BF16), V((TB, TB), BF16),
        V((2, T + 16, EL), F32), V((2, T, EL), BF16), V((2, L, T), BF16), V((2, L, T), BF16), V((2, T, L), BF16),
        V((2, T, EL), F32), V((2, T, EL), F32),
        V((2, NC * H, L), F32), V((NC, L, L), F32), V((T, L), F32), V((2, NC, H, L), F32),
        V((2, NC, L, EL), F32), V((2, L, EL), F32),
        V((2, 16, EL), BF16), V((2, 16, EL), BF16),
        V((2, L + 16, EL), BF16), V((2, L + 16, EL), BF16),
        V((2, L + 16, EL // 2), BF16), V((8, L + 16, EL // 2), BF16),
        V((2, L, EL // 2), BF16), V((2, L, EL // 2), BF16),
        V((NB, 8, 8, TB), F32), V((T, 2 * EL), BF16), V((NR, 2, 4, TB, TB), BF16),
        V((NR, 4, XM, TB), BF16), V((NR, 4, XM, TB), BF16), V((NR, YM, TB), BF16), V((NR, YM, TB), BF16),
        V((NR, XH, TB), BF16), V((NR, XH, TB), BF16), V((NR, XH, TB), BF16), V((NR, XH, TB), BF16),
        V((NR, XM, TB), BF16), V((NR, XM, TB), BF16),
        V((NR, 2, YH, TB), BF16), V((NR, 2, YH, TB), BF16), V((NR, 2, YH, TB), BF16), V((NR, 2, YH, TB), BF16),
        V((NR, 2, YM, TB), BF16), V((NR, 2, YM, TB), BF16),
        dma((NB,)), dma((NB,)), dma, dma, dma((7,)), dma((8,)), dma((2,)), dma((2,)), dma((2,)), dma((2,)), dma((2,)), dma((2,)), dma((7,)), dma((7,)),
        dma, dma, dma((NB, 7)), dma((NB, 7)),
        dma((NR,)), dma((NR,)), dma((NR,)), dma((NR,)), dma((NR,)), dma((NR, 6)), dma((NR, 6)), dma((NR, 6)), dma((NR, 6)),
    ]
    return pl.pallas_call(
        kernel,
        out_shape=jax.ShapeDtypeStruct((D // 8, T), BF16),
        in_specs=[hbm, vm, vm, hbm, hbm, vm, vm, vm, vm, hbm, sm, sm, sm],
        out_specs=hbm,
        scratch_shapes=scratch,
        compiler_params=pltpu.CompilerParams(
            collective_id=0, has_side_effects=True, vmem_limit_bytes=60 * 1024 * 1024
        ),
        cost_estimate=pl.CostEstimate(flops=20_000_000_000, bytes_accessed=16_000_000, transcendentals=4_000_000),
    )(
        hidden, ids.reshape(1, T), table, proj_weight, bc_weight.T.reshape(2, 16, D), dt_weight.T,
        conv_weight, conv_bias.reshape(1, EL), norm_gain.reshape(1, EL), out_weight,
        dt_bias, decay, skip,
    )


def solution(mesh):
    in_specs = (
        P("ctx", None), P("ctx"), P(), P(None, None, "shard"), P(None, "shard"), P(None, "shard"), P("shard"),
        P("shard"), P(None, "shard"), P("shard"), P("shard"), P("shard"), P("shard", None),
    )
    return jax.shard_map(
        per_device, mesh=mesh, in_specs=in_specs, out_specs=P("shard", "ctx"), check_vma=False
    )
```

```python
import jax
import jax.numpy as jnp
from jax import lax
from jax.experimental import pallas as pl
from jax.experimental.pallas import tpu as pltpu
from jax.sharding import PartitionSpec as P

E = 4096
L = 128
TB = 256
BLOCKS = (
    (0, 256, 112, 48, 80), (256, 256, 112, 48, 80), (512, 256, 112, 48, 80),
    (768, 128, 64, 32, 32), (896, 128, 64, 64, 64),
)
NR = len(BLOCKS)
XM, XH, YM, YH = 112, 64, 144, 80
HEADDIM = 64
MESH = pl.DeviceIdType.MESH
F32 = jnp.float32
BF16 = jnp.bfloat16
NT = (((1,), (1,)), ((), ()))
TN = (((0,), (0,)), ((), ()))


def dot(a, b, dims=(((1,), (0,)), ((), ())), **kw):
    return lax.dot_general(a, b, dims, preferred_element_type=F32, **kw)


def silu(x):
    half = 0.5 * x
    return half + half * jnp.tanh(half)


def iota(shape, dim):
    return lax.broadcasted_iota(jnp.int32, shape, dim)


def split(x):
    hi = x.astype(BF16).astype(F32)
    return hi, (x - hi).astype(BF16).astype(F32)


def rows_of(k, size):
    return pl.ds(pl.multiple_of(k * size, size), size)


def kernel(
    hid_hbm, ids_ref, table_ref, w_hbm, bcw_ref, dtw_ref, cw_ref, cb_ref, gain_ref, wo_hbm,
    dtb_ref, decay_ref, skip_ref,
    out_ref,
    u, wraw, wx, wg, wall, bcw, lhs, ob, flip, xin, xc, bt, ct, cm, gate, ybuf, dtraw, rowsbuf, cols, arow, sch, enter,
    halo_out, halo_in, st_out, st_in, ch_out, ch_in, fin_out, fin_in,
    sq, nrm, part, rx, qbuf, abuf, rx2, xa, xb, xaa, xba, xprev, xnext, ya, yb, yaa, yba, yprev, ynext,
    hsem, wsem, wosem, bgs, bgr, bcs, bcr, hs, hr, sts, stsr, chs, chr_, fis, fir, sqs, sqr,
    rxs, rxr, rx2s, rx2r, osem, xss, xsr, yss, ysr,
):
    T, D = u.shape
    EL = xc.shape[2]
    NB = T // TB
    NC = T // L
    H = EL // HEADDIM
    c = lax.axis_index("ctx")
    s = lax.axis_index("shard")
    z, xh, core = c // 4, (c // 2) % 2, c % 2
    y, xl = s // 2, s % 2

    def remote(src, dst, ss, rs, ctx=None, shard=None):
        return pltpu.make_async_remote_copy(
            src_ref=src, dst_ref=dst, send_sem=ss, recv_sem=rs,
            device_id={"ctx": c if ctx is None else ctx, "shard": s if shard is None else shard},
            device_id_type=MESH,
        )

    mate = c + 1 - 2 * core
    other = (c + 16 + 2 * core - 1) % 16
    chip = c // 2
    barrier = pltpu.get_barrier_semaphore()
    peers = [(mate, s), (other, s)]
    peers += [((c + 2 * k) % 16, s) for k in range(1, 8)]
    peers += [(c, (s + k) % 8) for k in range(1, 8)]
    for pc, ps in peers:
        pl.semaphore_signal(barrier, inc=1, device_id={"ctx": pc, "shard": ps}, device_id_type=MESH)

    WR = D // NB
    hcopies = [
        pltpu.make_async_copy(hid_hbm.at[pl.ds(b * TB, TB)], u.at[pl.ds(b * TB, TB)], hsem.at[b])
        for b in range(NB)
    ]
    wcopies = [
        pltpu.make_async_copy(w_hbm.at[pl.ds(b * WR, WR)], wraw.at[pl.ds(b * WR, WR)], wsem.at[b])
        for b in range(NB)
    ]
    woc = pltpu.make_async_copy(wo_hbm, wall.at[pl.ds(0, EL)], wosem)
    for b in range(NB):
        hcopies[b].start()
    for b in range(NB):
        wcopies[b].start()

    pl.semaphore_wait(barrier, len(peers))

    bcw[pl.ds(core * 8 + s, 1)] = bcw_ref[pl.ds(core, 1)]

    def gather(k):
        return remote(bcw_ref.at[core], bcw.at[core * 8 + s], bgs.at[k - 1], bgr.at[s], shard=(s + k) % 8)

    for k in range(1, 8):
        gather(k).start()

    flip[...] = jnp.where(iota((TB, TB), 0) + iota((TB, TB), 1) == TB - 1, 1.0, 0.0).astype(BF16)
    bcw[16] = jnp.concatenate([dtw_ref[...].astype(F32), jnp.zeros((16 - H, D), F32)], 0).astype(BF16)
    nd = D // TB

    def mirror_rows(w, i):
        w[1, (nd - 1 - i) * TB:(nd - i) * TB, :] = dot(flip[...], w[0, i * TB:(i + 1) * TB, :]).astype(BF16)

    def mirror_columns(v):
        parts = [dot(v[:, (nd - 1 - i) * TB:(nd - i) * TB], flip[...]).astype(BF16) for i in range(nd)]
        return jnp.concatenate(parts, 1)

    for b in range(NB):
        rows = slice(b * TB, (b + 1) * TB)
        hcopies[b].wait()
        hot = jnp.where(iota((table_ref.shape[0], TB), 0) == ids_ref[:, rows], 1.0, 0.0).astype(BF16)
        added = dot(hot, table_ref[...], TN)
        u[rows, :] = (u[rows, :].astype(F32) + added).astype(BF16)
    for m in range(NB):
        wcopies[m].wait()
        for k in range(WR // L):
            wr = slice(m * WR + k * L, m * WR + (k + 1) * L)
            pair = jnp.swapaxes(wraw[wr, :, :], 0, 1)
            wg[0, wr, :] = pair[0]
            wx[0, wr, :] = pair[1]
        for i in range(m * WR // TB, (m + 1) * WR // TB):
            mirror_rows(wx, i)
    PB = 512
    for b in range(T // PB):
        rows = slice(b * PB, (b + 1) * PB)
        for i in range(2):
            xv = dot(u[rows, :], wx[i]).astype(BF16)
            xin[i, 8 + b * PB:8 + (b + 1) * PB, :] = xv.astype(F32)
    woc.start()

    halo_out[0] = xin[0, T - 8:T + 8, :].astype(BF16)
    halo_out[1] = xin[1, 8:24, :].astype(BF16)
    nxt, prv = (c + 1) % 16, (c + 15) % 16
    hcf = remote(halo_out.at[0], halo_in.at[0], hs.at[0], hr.at[0], ctx=nxt)
    hcr = remote(halo_out.at[1], halo_in.at[1], hs.at[1], hr.at[1], ctx=prv)
    hcf.start()
    hcr.start()

    def swap(m):
        at = pl.ds(core * 8 + 4 * m, 4)
        return remote(bcw.at[at], bcw.at[at], bcs.at[m], bcr.at[m], ctx=mate)

    for m in range(2):
        for src in range(4 * m, 4 * m + 4):
            @pl.when(s != src)
            def _():
                remote(
                    bcw_ref.at[core], bcw.at[core * 8 + src], bgs.at[0], bgr.at[src], shard=(s + 1) % 8
                ).wait_recv()
        swap(m).start()
    for k in range(1, 8):
        gather(k).wait_send()

    half_w, half_b = 0.5 * cw_ref[...], 0.5 * cb_ref[...]

    def convolve(i, k):
        window = xin[i, k * L:(k + 1) * L + 16, :]
        acc = jnp.zeros((L, EL), F32) + half_b
        for t in range(4):
            at = 8 - 3 + t if i == 0 else 8 + 3 - t
            acc = acc + half_w[t:t + 1, :] * window[at:at + L, :]
        xc[i, k * L:(k + 1) * L, :] = (acc + acc * jnp.tanh(acc)).astype(BF16)

    for k in range(NC):
        if k > 0:
            convolve(0, k)
        if k < NC - 1:
            convolve(1, k)

    def gate_block(j):
        rows = slice(j * TB, (j + 1) * TB)
        for i in range(2):
            gate[i, rows, :] = silu(dot(u[rows, :], wg[i]))

    hcf.wait()
    hcr.wait()
    xin[0, 0:8, :] = jnp.where(c > 0, halo_in[0, 8:16, :].astype(F32), 0.0)
    xin[1, T + 8:T + 16, :] = jnp.where(c < 15, halo_in[1, 0:8, :].astype(F32), 0.0)
    convolve(0, 0)
    convolve(1, NC - 1)
    swap(0).wait()

    wb = jnp.concatenate([bcw[0:4], bcw[8:12], bcw[16:17]], 0).reshape(L + 16, D)
    lhs[0:L + 16, :] = wb
    lhs[L + 16:2 * (L + 16), :] = mirror_columns(wb)
    for b in range(NB):
        rows = slice(b * TB, (b + 1) * TB)
        both = dot(lhs[...], u[rows, :], NT)
        for i in range(2):
            r = both[i * (L + 16):(i + 1) * (L + 16)]
            bt[i, :, rows] = r[0:L].astype(BF16)
            for q in range(TB // L):
                k = b * (TB // L) + q
                dtraw[i, k * H:(k + 1) * H, :] = r[L:L + H, q * L:(q + 1) * L]

    head = iota((NC * H, L), 0) % H
    bias = jnp.zeros((NC * H, L), F32)
    rate = jnp.zeros((NC * H, L), F32)
    for h in range(H):
        bias = jnp.where(head == h, dtb_ref[h], bias)
        rate = jnp.where(head == h, decay_ref[h], rate)
    rowsbuf[...] = jnp.zeros_like(rowsbuf)
    before = iota((L, L), 0) <= iota((L, L), 1)
    after = iota((L, L), 0) >= iota((L, L), 1)
    decs = []
    for i in range(2):
        raw = dtraw[i] + bias
        dt = jnp.maximum(raw, 0.0) + jnp.log1p(jnp.exp(-jnp.abs(raw)))
        tri = jnp.where(before if i == 0 else after, 1.0, 0.0)
        g = dot(-dt * rate, tri, precision=lax.Precision.HIGHEST)
        total = g[:, L - 1:L] if i == 0 else g[:, 0:1]
        whi, wlo = split(jnp.exp(total - g) * dt)
        ehi, elo = split(jnp.exp(g))
        a = g - jnp.log(dt)
        owner = iota((NC * H, EL), 0) % H == iota((NC * H, EL), 1) // HEADDIM
        chunk_of = jnp.where(iota((NC, NC * H), 1) // H == iota((NC, NC * H), 0), 1.0, 0.0).astype(BF16)
        thi, tlo = split(jnp.where(owner, jnp.exp(total), 0.0))
        dec_rows = dot(chunk_of, thi.astype(BF16)) + dot(chunk_of, tlo.astype(BF16))
        decs.append([dec_rows[k:k + 1, :] for k in range(NC)])
        for k in range(NC):
            sl = slice(k * H, (k + 1) * H)
            arow[i, k] = a[sl]
            for j, part_ in enumerate((g, whi, wlo, ehi, elo)):
                at = (5 * i + j) * H
                rowsbuf[k, at:at + H, :] = part_[sl]

    er, ec = iota((L, EL), 0), iota((L, EL), 1)

    def spread(first):
        hit = (er >= first) & (er < first + 2 * H) & (er % H == ec // HEADDIM)
        return jnp.where(hit, 1.0, 0.0).astype(BF16)

    spreads = [spread(5 * H * i + H + 2 * H * j) for i in range(2) for j in range(2)]
    for k in range(NC):
        cols[k * L:(k + 1) * L, :] = rowsbuf[k].T

    def chunk_states(i):
        for k in range(NC):
            rows = slice(k * L, (k + 1) * L)
            wexp = dot(cols[rows, :].astype(BF16), spreads[2 * i])
            scaled = (wexp * xc[i, rows, :].astype(F32)).astype(BF16)
            sch[i, k] = dot(bt[i, :, rows], scaled)

    def pack_decay(d):
        hi, lo = split(d)
        wide = (8, d.shape[1])
        return jnp.concatenate([jnp.broadcast_to(hi, wide), jnp.broadcast_to(lo, wide)], 0).astype(BF16)

    def load_state(ref):
        whole = ref[...]
        tail = whole[L:L + 16].astype(F32)
        return whole[:L].astype(F32), tail[0:1] + tail[8:9]

    reach = [[None] * NC, [None] * NC]

    def device_state(i):
        state, dec = jnp.zeros((L, EL), F32), jnp.ones((1, EL), F32)
        for k in (range(NC) if i == 0 else range(NC - 1, -1, -1)):
            reach[i][k] = dec
            own = sch[i, k]
            sch[i, k] = state
            state = decs[i][k] * state + own
            dec = dec * decs[i][k]
        st_out[i, 0:L, :] = state.astype(BF16)
        st_out[i, L:L + 16, :] = pack_decay(dec)

    def mates(i):
        return remote(st_out.at[i], st_in.at[i], sts.at[i], stsr.at[i], ctx=mate)

    HC = EL // 2
    half = pl.ds(pl.multiple_of(core * HC, HC), HC)

    def chips(k, i):
        return remote(ch_out.at[i], ch_in.at[chip], chs.at[k - 1], chr_.at[k - 1], ctx=(c + 2 * k) % 16)

    def chip_state(i):
        mates(i).wait()
        ms, md = load_state(st_out.at[i, :, half])
        ts, td = load_state(st_in.at[i, :, half])
        state = jnp.where(core == i, td * ms + ts, md * ts + ms)
        ch_out[i, 0:L, :] = state.astype(BF16)
        ch_out[i, L:L + 16, :] = pack_decay(md * td)
        for k in range(1, 8):
            @pl.when((chip + k) // 8 == i)
            def _():
                chips(k, i).start()

    chunk_states(0)
    device_state(0)
    mates(0).start()
    chunk_states(1)
    chip_state(0)
    device_state(1)
    mates(1).start()

    lane = iota((L, L), 1)
    sk = jnp.zeros((1, EL), F32)
    for h in range(H):
        sk = jnp.where(iota((1, EL), 1) // HEADDIM == h, skip_ref[h], sk)

    def late_block(j):
        gate_block(j)
        for k in range(j * (TB // L), (j + 1) * (TB // L)):
            rows = slice(k * L, (k + 1) * L)
            for i in range(2):
                cv = ct[i, :, rows].astype(F32).T.astype(BF16)
                cm[i, rows, :] = cv
                cb = dot(cv, bt[i, :, rows])
                keep = iota((L, L), 0) >= lane if i == 0 else iota((L, L), 0) <= lane
                ar = arow[i, k]
                for q in range(H // 2):
                    ms = []
                    for h in (2 * q, 2 * q + 1):
                        at = 5 * H * i + h
                        d = cols[rows, at:at + 1] - ar[h:h + 1, :]
                        ms.append((jnp.exp(jnp.where(keep, d, -1e30)) * cb).astype(BF16))
                    xp = xc[i, rows, q * L:(q + 1) * L]
                    zero = jnp.zeros_like(xp)
                    left = jnp.where(lane < HEADDIM, xp, zero)
                    right = jnp.where(lane < HEADDIM, zero, xp)
                    yq = dot(jnp.concatenate(ms, 1), jnp.concatenate([left, right], 0))
                    ybuf[i, rows, q * L:(q + 1) * L] = yq + sk[:, q * L:(q + 1) * L] * xp.astype(F32)

    swap(1).wait()
    wc = jnp.concatenate([bcw[4:8], bcw[12:16]], 0).reshape(L, D)
    lhs[0:L, :] = wc
    lhs[L:2 * L, :] = mirror_columns(wc)
    for i in range(nd):
        mirror_rows(wg, i)
    chip_state(1)
    ch_in[chip] = ch_out[0]
    for b in range(NB):
        rows = slice(b * TB, (b + 1) * TB)
        both = dot(lhs[0:2 * L, :], u[rows, :], NT)
        for i in range(2):
            ct[i, :, rows] = both[i * L:(i + 1) * L].astype(BF16)

    woc.wait()
    for i in range(nd):
        wall[EL:2 * EL, i * TB:(i + 1) * TB] = dot(
            wall[0:EL, (nd - 1 - i) * TB:(nd - i) * TB], flip[...]
        ).astype(BF16)

    late_block(0)

    late_block(1)
    late_block(2)

    for k in range(1, 8):
        chips(k, 0).wait_send()
        pltpu.make_async_remote_copy(
            src_ref=ch_out.at[0], dst_ref=ch_in.at[(chip + 8 - k) % 8], send_sem=chs.at[k - 1],
            recv_sem=chr_.at[k - 1], device_id={"ctx": (c + 2 * k) % 16, "shard": s}, device_id_type=MESH,
        ).wait_recv()
    entries = [jnp.zeros((L, HC), F32), jnp.zeros((L, HC), F32)]
    for pp in range(7):
        ps, pd = load_state(ch_in.at[pp])
        entries[0] = jnp.where(pp < chip, pd * entries[0] + ps, entries[0])
    for pp in range(7, 0, -1):
        ps, pd = load_state(ch_in.at[pp])
        entries[1] = jnp.where(pp > chip, pd * entries[1] + ps, entries[1])
    for i in range(2):
        fin_out[i] = entries[i].astype(BF16)
    fina = remote(fin_out, fin_in, fis, fir, ctx=mate)
    fina.start()
    fina.wait()

    for i in range(2):
        mine, theirs = fin_out[i].astype(F32), fin_in[i].astype(F32)
        entering = jnp.where(
            core == 0, jnp.concatenate([mine, theirs], 1), jnp.concatenate([theirs, mine], 1)
        )
        ts, td = load_state(st_in.at[i])
        enter[i] = jnp.where(core != i, td * entering + ts, entering)

    def sums(j, k):
        return remote(sq.at[j, s], sq.at[j, s], sqs.at[j, k - 1], sqr.at[j, k - 1], shard=(s + k) % 8)

    def gated_block(j):
        total = jnp.zeros((8, TB), F32)
        for i in range(2):
            pick = jnp.where(iota((8, EL), 0) // 4 == i, 1.0, 0.0).astype(BF16)
            for q in range(TB // L):
                k = j * (TB // L) + q
                rows = slice(k * L, (k + 1) * L)
                eexp = dot(cols[rows, :].astype(BF16), spreads[2 * i + 1])
                yv = ybuf[i, rows, :] + eexp * dot(cm[i, rows, :], (sch[i, k] + reach[i][k] * enter[i]).astype(BF16))
                ybuf[i, rows, :] = yv * gate[i, rows, :]
            rows = slice(j * TB, (j + 1) * TB)
            gv = ybuf[i, rows, :]
            total = total + dot(pick, (gv * gv).astype(BF16), NT)
        sq[j, s] = total
        for k in range(1, 8):
            sums(j, k).start()

    def wait_sums(j):
        for k in range(1, 8):
            sums(j, k).wait_send()
            pltpu.make_async_remote_copy(
                src_ref=sq.at[j, s], dst_ref=sq.at[j, (s + 8 - k) % 8], send_sem=sqs.at[j, k - 1],
                recv_sem=sqr.at[j, k - 1], device_id={"ctx": c, "shard": (s + k) % 8}, device_id_type=MESH,
            ).wait_recv()

    xs = s + 1 - 2 * xl
    up, down, across = (y + 1) % 4, (y + 3) % 4, (y + 2) % 4

    def cross(j):
        xr = BLOCKS[j][2]
        return remote(
            part.at[j, 1 - xl, :, pl.ds(0, xr), :], rx.at[j, :, pl.ds(0, xr), :], rxs.at[j], rxr.at[j], shard=xs
        )

    def cross2(j):
        n = BLOCKS[j][1] - BLOCKS[j][2]
        return remote(abuf.at[j, pl.ds(0, n)], rx2.at[j, pl.ds(0, n)], rx2s.at[j], rx2r.at[j], shard=xs)

    def straight(j):
        return BLOCKS[j][2] == BLOCKS[j][3]

    def first_steps(j):
        return range(3) if straight(j) else range(4)

    def final_steps(j):
        return range(3) if straight(j) else range(2, 6)

    def ring_y(j, step):
        n, xr, h0 = BLOCKS[j][1], BLOCKS[j][2], BLOCKS[j][4]
        h1 = n - xr - h0
        if straight(j):
            to, buf = [(up, yprev), (down, ynext), (across, ya)][step]
            return remote(
                part.at[j, :, to, pl.ds(xr, h0), :], buf.at[j, :, pl.ds(0, h0), :],
                yss.at[j, step], ysr.at[j, step], shard=to * 2 + xl,
            )
        lo, hi = pl.ds(0, h0), pl.ds(h0, h1)
        plo, phi = pl.ds(xr, h0), pl.ds(xr + h0, h1)
        src, dst, to = [
            (part.at[j, :, across, plo, :], ya.at[j, :, lo, :], up),
            (part.at[j, :, across, phi, :], yb.at[j, :, pl.ds(0, h1), :], down),
            (part.at[j, :, up, phi, :], yprev.at[j, :, hi, :], up),
            (part.at[j, :, down, plo, :], ynext.at[j, :, lo, :], down),
            (yaa.at[j, :, lo, :], yprev.at[j, :, lo, :], up),
            (yba.at[j, :, pl.ds(0, h1), :], ynext.at[j, :, hi, :], down),
        ][step]
        return remote(src, dst, yss.at[j, step], ysr.at[j, step], shard=to * 2 + xl)

    def ring_x(j, step):
        xr, h0 = BLOCKS[j][2], BLOCKS[j][3]
        h1 = xr - h0
        if straight(j):
            to, buf = [(up, xprev), (down, xnext), (across, xa)][step]
            return remote(
                qbuf.at[j, to, pl.ds(0, xr), :], buf.at[j, pl.ds(0, xr), :],
                xss.at[j, step], xsr.at[j, step], shard=to * 2 + xl,
            )
        lo, hi = pl.ds(0, h0), pl.ds(h0, h1)
        src, dst, to = [
            (qbuf.at[j, across, lo, :], xa.at[j, lo, :], up),
            (qbuf.at[j, across, hi, :], xb.at[j, pl.ds(0, h1), :], down),
            (qbuf.at[j, up, hi, :], xprev.at[j, hi, :], up),
            (qbuf.at[j, down, lo, :], xnext.at[j, lo, :], down),
            (xaa.at[j, lo, :], xprev.at[j, lo, :], up),
            (xba.at[j, pl.ds(0, h1), :], xnext.at[j, hi, :], down),
        ][step]
        return remote(src, dst, xss.at[j, step], xsr.at[j, step], shard=to * 2 + xl)

    def product_block(j):
        r0, n, xr = BLOCKS[j][:3]
        tb = r0 // TB
        if r0 % TB == 0:
            wait_sums(tb)
        total = sq[tb, 0]
        for k in range(1, 8):
            total = total + sq[tb, k]
        scale = lax.rsqrt(total / E + 1e-05)
        rows = slice(r0, r0 + n)
        for q in range(r0, r0 + n, L):
            at = q % TB
            col = jnp.concatenate([scale[:, at:at + L]] * (L // 8), 0).T
            sub = slice(q, q + L)
            for i in range(2):
                nv = ybuf[i, sub, :] * col[:, 4 * i:4 * i + 1] * gain_ref[...]
                nrm[sub, i * EL:(i + 1) * EL] = nv.astype(BF16)
        for p in range(8):
            xx = lax.rem(p // 4 + 1 + xl, 2)
            yy = p % 4
            part[j, xx, yy, 0:n, :] = dot(nrm[rows, :], wall[:, rows_of(yy * 2 + xx, TB)]).astype(BF16)
            if p == 3:
                cross(j).start()
        for step in first_steps(j):
            ring_y(j, step).start()

    def middle_x(j):
        xr = BLOCKS[j][2]
        cross(j).wait()
        for yk in range(4):
            both = part[j, xl, yk, 0:xr, :].astype(F32) + rx[j, yk, 0:xr, :].astype(F32)
            qbuf[j, yk, 0:xr, :] = both.astype(BF16)
        for step in first_steps(j):
            ring_x(j, step).start()

    def middle_y(j):
        n, xr, h0 = BLOCKS[j][1], BLOCKS[j][2], BLOCKS[j][4]
        h1 = n - xr - h0
        for step in range(2):
            ring_y(j, step).wait()
        for m in range(2):
            both = part[j, m, up, xr:xr + h0, :].astype(F32) + ya[j, m, 0:h0, :].astype(F32)
            yaa[j, m, 0:h0, :] = both.astype(BF16)
            both = part[j, m, down, xr + h0:n, :].astype(F32) + yb[j, m, 0:h1, :].astype(F32)
            yba[j, m, 0:h1, :] = both.astype(BF16)
        for step in range(4, 6):
            ring_y(j, step).start()

    def third_x(j):
        xr, h0 = BLOCKS[j][2:4]
        h1 = xr - h0
        for step in range(2):
            ring_x(j, step).wait()
        both = qbuf[j, up, 0:h0, :].astype(F32) + xa[j, 0:h0, :].astype(F32)
        xaa[j, 0:h0, :] = both.astype(BF16)
        both = qbuf[j, down, h0:xr, :].astype(F32) + xb[j, 0:h1, :].astype(F32)
        xba[j, 0:h1, :] = both.astype(BF16)
        for step in range(4, 6):
            ring_x(j, step).start()

    def third_y(j):
        n, xr = BLOCKS[j][1:3]
        for step in final_steps(j):
            ring_y(j, step).wait()
        sums_ = []
        for m in range(2):
            xx = (xl + 1 + m) % 2
            acc = part[j, xx, y, xr:n, :].astype(F32)
            acc = acc + yprev[j, xx, 0:n - xr, :].astype(F32) + ynext[j, xx, 0:n - xr, :].astype(F32)
            if straight(j):
                acc = acc + ya[j, xx, 0:n - xr, :].astype(F32)
            sums_.append(acc)
        abuf[j, 0:n - xr, :] = sums_[0].astype(BF16)
        cross2(j).start()
        kept[j] = sums_[1]

    def last_block(j):
        r0, n, xr = BLOCKS[j][:3]
        for step in final_steps(j):
            ring_x(j, step).wait()
        acc = qbuf[j, y, 0:xr, :].astype(F32)
        acc = acc + xprev[j, 0:xr, :].astype(F32) + xnext[j, 0:xr, :].astype(F32)
        if straight(j):
            acc = acc + xa[j, 0:xr, :].astype(F32)
        cross2(j).wait()
        low = kept[j] + rx2[j, 0:n - xr, :].astype(F32)
        ob[:, r0:r0 + n] = jnp.concatenate([acc, low], 0).T.astype(BF16)
        leave(j).start()

    def leave(j):
        at = pl.ds(BLOCKS[j][0], BLOCKS[j][1])
        return pltpu.make_async_copy(ob.at[:, at], out_ref.at[:, at], osem.at[j])

    kept = [None] * len(BLOCKS)
    gated_block(0)
    gated_block(1)
    gated_block(2)
    late_block(3)
    product_block(0)
    product_block(1)
    gated_block(3)
    middle_y(0)
    product_block(2)
    middle_y(1)
    middle_x(0)
    product_block(3)
    middle_y(2)
    product_block(4)
    middle_x(1)
    third_y(0)
    third_x(0)
    middle_y(3)
    middle_x(2)
    third_y(1)
    third_x(1)
    last_block(0)
    middle_x(3)
    third_y(2)
    third_x(2)
    middle_x(4)
    third_y(3)
    third_x(3)
    third_y(4)
    last_block(1)
    last_block(2)
    last_block(3)
    last_block(4)
    for j in range(NR):
        leave(j).wait()


def per_device(
    hidden, ids, table, proj_weight, bc_weight, dt_weight, dt_bias, decay, conv_weight, conv_bias, skip,
    norm_gain, out_weight,
):
    T, D = hidden.shape
    EL = conv_bias.shape[0]
    H = EL // HEADDIM
    NB, NC = T // TB, T // L
    vm = pl.BlockSpec(memory_space=pltpu.VMEM)
    sm = pl.BlockSpec(memory_space=pltpu.SMEM)
    hbm = pl.BlockSpec(memory_space=pl.ANY)
    V = pltpu.VMEM
    dma = pltpu.SemaphoreType.DMA
    scratch = [
        V((T, D), BF16),
        V((D, 2, EL), BF16), V((2, D, EL), BF16), V((2, D, EL), BF16), V((2 * EL, D), BF16),
        V((17, 16, D), BF16), V((2 * (L + 16), D), BF16), V((D // 8, T), BF16), V((TB, TB), BF16),
        V((2, T + 16, EL), F32), V((2, T, EL), BF16), V((2, L, T), BF16), V((2, L, T), BF16), V((2, T, L), BF16),
        V((2, T, EL), F32), V((2, T, EL), F32),
        V((2, NC * H, L), F32), V((NC, L, L), F32), V((T, L), F32), V((2, NC, H, L), F32),
        V((2, NC, L, EL), F32), V((2, L, EL), F32),
        V((2, 16, EL), BF16), V((2, 16, EL), BF16),
        V((2, L + 16, EL), BF16), V((2, L + 16, EL), BF16),
        V((2, L + 16, EL // 2), BF16), V((8, L + 16, EL // 2), BF16),
        V((2, L, EL // 2), BF16), V((2, L, EL // 2), BF16),
        V((NB, 8, 8, TB), F32), V((T, 2 * EL), BF16), V((NR, 2, 4, TB, TB), BF16),
        V((NR, 4, XM, TB), BF16), V((NR, 4, XM, TB), BF16), V((NR, YM, TB), BF16), V((NR, YM, TB), BF16),
        V((NR, XH, TB), BF16), V((NR, XH, TB), BF16), V((NR, XH, TB), BF16), V((NR, XH, TB), BF16),
        V((NR, XM, TB), BF16), V((NR, XM, TB), BF16),
        V((NR, 2, YH, TB), BF16), V((NR, 2, YH, TB), BF16), V((NR, 2, YH, TB), BF16), V((NR, 2, YH, TB), BF16),
        V((NR, 2, YM, TB), BF16), V((NR, 2, YM, TB), BF16),
        dma((NB,)), dma((NB,)), dma, dma((7,)), dma((8,)), dma((2,)), dma((2,)), dma((2,)), dma((2,)), dma((2,)), dma((2,)), dma((7,)), dma((7,)),
        dma, dma, dma((NB, 7)), dma((NB, 7)),
        dma((NR,)), dma((NR,)), dma((NR,)), dma((NR,)), dma((NR,)), dma((NR, 6)), dma((NR, 6)), dma((NR, 6)), dma((NR, 6)),
    ]
    return pl.pallas_call(
        kernel,
        out_shape=jax.ShapeDtypeStruct((D // 8, T), BF16),
        in_specs=[hbm, vm, vm, hbm, vm, vm, vm, vm, vm, hbm, sm, sm, sm],
        out_specs=hbm,
        scratch_shapes=scratch,
        compiler_params=pltpu.CompilerParams(
            collective_id=0, has_side_effects=True, vmem_limit_bytes=60 * 1024 * 1024
        ),
        cost_estimate=pl.CostEstimate(flops=20_000_000_000, bytes_accessed=16_000_000, transcendentals=4_000_000),
    )(
        hidden, ids.reshape(1, T), table, proj_weight, bc_weight.T.reshape(2, 16, D), dt_weight.T,
        conv_weight, conv_bias.reshape(1, EL), norm_gain.reshape(1, EL), out_weight,
        dt_bias, decay, skip,
    )


def solution(mesh):
    in_specs = (
        P("ctx", None), P("ctx"), P(), P(None, None, "shard"), P(None, "shard"), P(None, "shard"), P("shard"),
        P("shard"), P(None, "shard"), P("shard"), P("shard"), P("shard"), P("shard", None),
    )
    return jax.shard_map(
        per_device, mesh=mesh, in_specs=in_specs, out_specs=P("shard", "ctx"), check_vma=False
    )
```

```python
import jax
import jax.numpy as jnp
from jax import lax
from jax.experimental import pallas as pl
from jax.experimental.pallas import tpu as pltpu
from jax.sharding import PartitionSpec as P

E = 4096
L = 128
TB = 256
BLOCKS = (
    (0, 256, 112, 48, 80), (256, 256, 112, 48, 80), (512, 256, 112, 48, 80),
    (768, 128, 64, 32, 32), (896, 128, 64, 32, 32),
)
NR = len(BLOCKS)
XM, XH, YM, YH = 112, 64, 144, 80
HEADDIM = 64
MESH = pl.DeviceIdType.MESH
F32 = jnp.float32
BF16 = jnp.bfloat16
NT = (((1,), (1,)), ((), ()))
TN = (((0,), (0,)), ((), ()))


def dot(a, b, dims=(((1,), (0,)), ((), ())), **kw):
    return lax.dot_general(a, b, dims, preferred_element_type=F32, **kw)


def silu(x):
    half = 0.5 * x
    return half + half * jnp.tanh(half)


def iota(shape, dim):
    return lax.broadcasted_iota(jnp.int32, shape, dim)


def split(x):
    hi = x.astype(BF16).astype(F32)
    return hi, (x - hi).astype(BF16).astype(F32)


def rows_of(k, size):
    return pl.ds(pl.multiple_of(k * size, size), size)


def kernel(
    hid_hbm, ids_ref, table_ref, w_hbm, bcw_hbm, dtw_ref, cw_ref, cb_ref, gain_ref, wo_hbm,
    dtb_ref, decay_ref, skip_ref,
    out_ref,
    u, wraw, wx, wg, wall, bcw, lhs, ob, flip, xin, xc, bt, ct, cm, gate, ybuf, dtraw, rowsbuf, cols, arow, sch, enter,
    halo_out, halo_in, st_out, st_in, ch_out, ch_in, fin_out, fin_in,
    sq, nrm, part, rx, qbuf, abuf, rx2, xa, xb, xaa, xba, xprev, xnext, ya, yb, yaa, yba, yprev, ynext,
    hsem, wsem, wosem, bsem, bgs, bgr, bcs, bcr, hs, hr, sts, stsr, chs, chr_, fis, fir, sqs, sqr,
    rxs, rxr, rx2s, rx2r, osem, xss, xsr, yss, ysr,
):
    T, D = u.shape
    EL = xc.shape[2]
    NB = T // TB
    NC = T // L
    H = EL // HEADDIM
    c = lax.axis_index("ctx")
    s = lax.axis_index("shard")
    z, xh, core = c // 4, (c // 2) % 2, c % 2
    y, xl = s // 2, s % 2

    def remote(src, dst, ss, rs, ctx=None, shard=None):
        return pltpu.make_async_remote_copy(
            src_ref=src, dst_ref=dst, send_sem=ss, recv_sem=rs,
            device_id={"ctx": c if ctx is None else ctx, "shard": s if shard is None else shard},
            device_id_type=MESH,
        )

    WR = D // NB
    hcopies = [
        pltpu.make_async_copy(hid_hbm.at[pl.ds(b * TB, TB)], u.at[pl.ds(b * TB, TB)], hsem.at[b])
        for b in range(NB)
    ]
    wcopies = [
        pltpu.make_async_copy(w_hbm.at[pl.ds(b * WR, WR)], wraw.at[pl.ds(b * WR, WR)], wsem.at[b])
        for b in range(NB)
    ]
    woc = pltpu.make_async_copy(wo_hbm, wall.at[pl.ds(0, EL)], wosem)
    bown = pltpu.make_async_copy(bcw_hbm.at[core], bcw.at[core * 8 + s], bsem)
    for b in range(NB):
        hcopies[b].start()
    for b in range(NB):
        wcopies[b].start()
    bown.start()

    mate = c + 1 - 2 * core
    other = (c + 16 + 2 * core - 1) % 16
    chip = c // 2
    barrier = pltpu.get_barrier_semaphore()
    peers = [(mate, s), (other, s)]
    peers += [((c + 2 * k) % 16, s) for k in range(1, 8)]
    peers += [(c, (s + k) % 8) for k in range(1, 8)]
    for pc, ps in peers:
        pl.semaphore_signal(barrier, inc=1, device_id={"ctx": pc, "shard": ps}, device_id_type=MESH)
    pl.semaphore_wait(barrier, len(peers))

    def gather(k):
        return remote(bcw_hbm.at[core], bcw.at[core * 8 + s], bgs.at[k - 1], bgr.at[s], shard=(s + k) % 8)

    for k in range(1, 8):
        gather(k).start()

    flip[...] = jnp.where(iota((TB, TB), 0) + iota((TB, TB), 1) == TB - 1, 1.0, 0.0).astype(BF16)
    bcw[16] = jnp.concatenate([dtw_ref[...].astype(F32), jnp.zeros((16 - H, D), F32)], 0).astype(BF16)
    nd = D // TB

    def mirror_rows(w, i):
        w[1, (nd - 1 - i) * TB:(nd - i) * TB, :] = dot(flip[...], w[0, i * TB:(i + 1) * TB, :]).astype(BF16)

    def mirror_columns(v):
        parts = [dot(v[:, (nd - 1 - i) * TB:(nd - i) * TB], flip[...]).astype(BF16) for i in range(nd)]
        return jnp.concatenate(parts, 1)

    for b in range(NB):
        rows = slice(b * TB, (b + 1) * TB)
        hcopies[b].wait()
        hot = jnp.where(iota((table_ref.shape[0], TB), 0) == ids_ref[:, rows], 1.0, 0.0).astype(BF16)
        added = dot(hot, table_ref[...], TN)
        u[rows, :] = (u[rows, :].astype(F32) + added).astype(BF16)
    for m in range(NB):
        wcopies[m].wait()
        for k in range(WR // L):
            wr = slice(m * WR + k * L, m * WR + (k + 1) * L)
            pair = jnp.swapaxes(wraw[wr, :, :], 0, 1)
            wg[0, wr, :] = pair[0]
            wx[0, wr, :] = pair[1]
        for i in range(m * WR // TB, (m + 1) * WR // TB):
            mirror_rows(wx, i)
    PB = 512
    for b in range(T // PB):
        rows = slice(b * PB, (b + 1) * PB)
        for i in range(2):
            xv = dot(u[rows, :], wx[i]).astype(BF16)
            xin[i, 8 + b * PB:8 + (b + 1) * PB, :] = xv.astype(F32)
    woc.start()

    halo_out[0] = xin[0, T - 8:T + 8, :].astype(BF16)
    halo_out[1] = xin[1, 8:24, :].astype(BF16)
    nxt, prv = (c + 1) % 16, (c + 15) % 16
    hcf = remote(halo_out.at[0], halo_in.at[0], hs.at[0], hr.at[0], ctx=nxt)
    hcr = remote(halo_out.at[1], halo_in.at[1], hs.at[1], hr.at[1], ctx=prv)
    hcf.start()
    hcr.start()

    def swap(m):
        at = pl.ds(core * 8 + 4 * m, 4)
        return remote(bcw.at[at], bcw.at[at], bcs.at[m], bcr.at[m], ctx=mate)

    bown.wait()
    for m in range(2):
        for src in range(4 * m, 4 * m + 4):
            @pl.when(s != src)
            def _():
                remote(
                    bcw_hbm.at[core], bcw.at[core * 8 + src], bgs.at[0], bgr.at[src], shard=(s + 1) % 8
                ).wait_recv()
        swap(m).start()
    for k in range(1, 8):
        gather(k).wait_send()

    half_w, half_b = 0.5 * cw_ref[...], 0.5 * cb_ref[...]

    def convolve(i, k):
        window = xin[i, k * L:(k + 1) * L + 16, :]
        acc = jnp.zeros((L, EL), F32) + half_b
        for t in range(4):
            at = 8 - 3 + t if i == 0 else 8 + 3 - t
            acc = acc + half_w[t:t + 1, :] * window[at:at + L, :]
        xc[i, k * L:(k + 1) * L, :] = (acc + acc * jnp.tanh(acc)).astype(BF16)

    for k in range(NC):
        if k > 0:
            convolve(0, k)
        if k < NC - 1:
            convolve(1, k)

    def gate_block(j):
        rows = slice(j * TB, (j + 1) * TB)
        for i in range(2):
            gate[i, rows, :] = silu(dot(u[rows, :], wg[i]))

    swap(0).wait()

    wb = jnp.concatenate([bcw[0:4], bcw[8:12], bcw[16:17]], 0).reshape(L + 16, D)
    lhs[0:L + 16, :] = wb
    lhs[L + 16:2 * (L + 16), :] = mirror_columns(wb)
    for b in range(NB):
        rows = slice(b * TB, (b + 1) * TB)
        both = dot(lhs[...], u[rows, :], NT)
        for i in range(2):
            r = both[i * (L + 16):(i + 1) * (L + 16)]
            bt[i, :, rows] = r[0:L].astype(BF16)
            for q in range(TB // L):
                k = b * (TB // L) + q
                dtraw[i, k * H:(k + 1) * H, :] = r[L:L + H, q * L:(q + 1) * L]

    head = iota((NC * H, L), 0) % H
    bias = jnp.zeros((NC * H, L), F32)
    rate = jnp.zeros((NC * H, L), F32)
    for h in range(H):
        bias = jnp.where(head == h, dtb_ref[h], bias)
        rate = jnp.where(head == h, decay_ref[h], rate)
    rowsbuf[...] = jnp.zeros_like(rowsbuf)
    before = iota((L, L), 0) <= iota((L, L), 1)
    after = iota((L, L), 0) >= iota((L, L), 1)
    decs = []
    for i in range(2):
        raw = dtraw[i] + bias
        dt = jnp.maximum(raw, 0.0) + jnp.log1p(jnp.exp(-jnp.abs(raw)))
        tri = jnp.where(before if i == 0 else after, 1.0, 0.0)
        g = dot(-dt * rate, tri, precision=lax.Precision.HIGHEST)
        total = g[:, L - 1:L] if i == 0 else g[:, 0:1]
        whi, wlo = split(jnp.exp(total - g) * dt)
        ehi, elo = split(jnp.exp(g))
        a = g - jnp.log(dt)
        owner = iota((NC * H, EL), 0) % H == iota((NC * H, EL), 1) // HEADDIM
        chunk_of = jnp.where(iota((NC, NC * H), 1) // H == iota((NC, NC * H), 0), 1.0, 0.0).astype(BF16)
        thi, tlo = split(jnp.where(owner, jnp.exp(total), 0.0))
        dec_rows = dot(chunk_of, thi.astype(BF16)) + dot(chunk_of, tlo.astype(BF16))
        decs.append([dec_rows[k:k + 1, :] for k in range(NC)])
        for k in range(NC):
            sl = slice(k * H, (k + 1) * H)
            arow[i, k] = a[sl]
            for j, part_ in enumerate((g, whi, wlo, ehi, elo)):
                at = (5 * i + j) * H
                rowsbuf[k, at:at + H, :] = part_[sl]

    er, ec = iota((L, EL), 0), iota((L, EL), 1)

    def spread(first):
        hit = (er >= first) & (er < first + 2 * H) & (er % H == ec // HEADDIM)
        return jnp.where(hit, 1.0, 0.0).astype(BF16)

    spreads = [spread(5 * H * i + H + 2 * H * j) for i in range(2) for j in range(2)]
    for k in range(NC):
        cols[k * L:(k + 1) * L, :] = rowsbuf[k].T

    hcf.wait()
    hcr.wait()
    xin[0, 0:8, :] = jnp.where(c > 0, halo_in[0, 8:16, :].astype(F32), 0.0)
    xin[1, T + 8:T + 16, :] = jnp.where(c < 15, halo_in[1, 0:8, :].astype(F32), 0.0)

    def chunk_states(i):
        convolve(i, 0 if i == 0 else NC - 1)
        for k in range(NC):
            rows = slice(k * L, (k + 1) * L)
            wexp = dot(cols[rows, :].astype(BF16), spreads[2 * i])
            scaled = (wexp * xc[i, rows, :].astype(F32)).astype(BF16)
            sch[i, k] = dot(bt[i, :, rows], scaled)

    def pack_decay(d):
        hi, lo = split(d)
        wide = (8, d.shape[1])
        return jnp.concatenate([jnp.broadcast_to(hi, wide), jnp.broadcast_to(lo, wide)], 0).astype(BF16)

    def load_state(ref):
        whole = ref[...]
        tail = whole[L:L + 16].astype(F32)
        return whole[:L].astype(F32), tail[0:1] + tail[8:9]

    reach = [[None] * NC, [None] * NC]

    def device_state(i):
        state, dec = jnp.zeros((L, EL), F32), jnp.ones((1, EL), F32)
        for k in (range(NC) if i == 0 else range(NC - 1, -1, -1)):
            reach[i][k] = dec
            own = sch[i, k]
            sch[i, k] = state
            state = decs[i][k] * state + own
            dec = dec * decs[i][k]
        st_out[i, 0:L, :] = state.astype(BF16)
        st_out[i, L:L + 16, :] = pack_decay(dec)

    def mates(i):
        return remote(st_out.at[i], st_in.at[i], sts.at[i], stsr.at[i], ctx=mate)

    HC = EL // 2
    half = pl.ds(pl.multiple_of(core * HC, HC), HC)

    def chips(k, i):
        return remote(ch_out.at[i], ch_in.at[chip], chs.at[k - 1], chr_.at[k - 1], ctx=(c + 2 * k) % 16)

    def chip_state(i):
        mates(i).wait()
        ms, md = load_state(st_out.at[i, :, half])
        ts, td = load_state(st_in.at[i, :, half])
        state = jnp.where(core == i, td * ms + ts, md * ts + ms)
        ch_out[i, 0:L, :] = state.astype(BF16)
        ch_out[i, L:L + 16, :] = pack_decay(md * td)
        for k in range(1, 8):
            @pl.when((chip + k) // 8 == i)
            def _():
                chips(k, i).start()

    chunk_states(0)
    device_state(0)
    mates(0).start()
    chunk_states(1)
    chip_state(0)
    device_state(1)
    mates(1).start()

    lane = iota((L, L), 1)
    sk = jnp.zeros((1, EL), F32)
    for h in range(H):
        sk = jnp.where(iota((1, EL), 1) // HEADDIM == h, skip_ref[h], sk)

    def late_block(j):
        gate_block(j)
        for k in range(j * (TB // L), (j + 1) * (TB // L)):
            rows = slice(k * L, (k + 1) * L)
            for i in range(2):
                cv = ct[i, :, rows].astype(F32).T.astype(BF16)
                cm[i, rows, :] = cv
                cb = dot(cv, bt[i, :, rows])
                keep = iota((L, L), 0) >= lane if i == 0 else iota((L, L), 0) <= lane
                ar = arow[i, k]
                for q in range(H // 2):
                    ms = []
                    for h in (2 * q, 2 * q + 1):
                        at = 5 * H * i + h
                        d = cols[rows, at:at + 1] - ar[h:h + 1, :]
                        ms.append((jnp.exp(jnp.where(keep, d, -1e30)) * cb).astype(BF16))
                    xp = xc[i, rows, q * L:(q + 1) * L]
                    zero = jnp.zeros_like(xp)
                    left = jnp.where(lane < HEADDIM, xp, zero)
                    right = jnp.where(lane < HEADDIM, zero, xp)
                    yq = dot(jnp.concatenate(ms, 1), jnp.concatenate([left, right], 0))
                    ybuf[i, rows, q * L:(q + 1) * L] = yq + sk[:, q * L:(q + 1) * L] * xp.astype(F32)

    swap(1).wait()
    wc = jnp.concatenate([bcw[4:8], bcw[12:16]], 0).reshape(L, D)
    lhs[0:L, :] = wc
    lhs[L:2 * L, :] = mirror_columns(wc)
    for i in range(nd):
        mirror_rows(wg, i)
    chip_state(1)
    ch_in[chip] = ch_out[0]
    for b in range(NB):
        rows = slice(b * TB, (b + 1) * TB)
        both = dot(lhs[0:2 * L, :], u[rows, :], NT)
        for i in range(2):
            ct[i, :, rows] = both[i * L:(i + 1) * L].astype(BF16)

    woc.wait()
    for i in range(nd):
        wall[EL:2 * EL, i * TB:(i + 1) * TB] = dot(
            wall[0:EL, (nd - 1 - i) * TB:(nd - i) * TB], flip[...]
        ).astype(BF16)

    late_block(0)

    late_block(1)
    late_block(2)

    for k in range(1, 8):
        chips(k, 0).wait_send()
        pltpu.make_async_remote_copy(
            src_ref=ch_out.at[0], dst_ref=ch_in.at[(chip + 8 - k) % 8], send_sem=chs.at[k - 1],
            recv_sem=chr_.at[k - 1], device_id={"ctx": (c + 2 * k) % 16, "shard": s}, device_id_type=MESH,
        ).wait_recv()
    entries = [jnp.zeros((L, HC), F32), jnp.zeros((L, HC), F32)]
    for pp in range(7):
        ps, pd = load_state(ch_in.at[pp])
        entries[0] = jnp.where(pp < chip, pd * entries[0] + ps, entries[0])
    for pp in range(7, 0, -1):
        ps, pd = load_state(ch_in.at[pp])
        entries[1] = jnp.where(pp > chip, pd * entries[1] + ps, entries[1])
    for i in range(2):
        fin_out[i] = entries[i].astype(BF16)
    fina = remote(fin_out, fin_in, fis, fir, ctx=mate)
    fina.start()
    fina.wait()

    for i in range(2):
        mine, theirs = fin_out[i].astype(F32), fin_in[i].astype(F32)
        entering = jnp.where(
            core == 0, jnp.concatenate([mine, theirs], 1), jnp.concatenate([theirs, mine], 1)
        )
        ts, td = load_state(st_in.at[i])
        enter[i] = jnp.where(core != i, td * entering + ts, entering)

    def sums(j, k):
        return remote(sq.at[j, s], sq.at[j, s], sqs.at[j, k - 1], sqr.at[j, k - 1], shard=(s + k) % 8)

    def gated_block(j):
        total = jnp.zeros((8, TB), F32)
        for i in range(2):
            pick = jnp.where(iota((8, EL), 0) // 4 == i, 1.0, 0.0).astype(BF16)
            for q in range(TB // L):
                k = j * (TB // L) + q
                rows = slice(k * L, (k + 1) * L)
                eexp = dot(cols[rows, :].astype(BF16), spreads[2 * i + 1])
                yv = ybuf[i, rows, :] + eexp * dot(cm[i, rows, :], (sch[i, k] + reach[i][k] * enter[i]).astype(BF16))
                ybuf[i, rows, :] = yv * gate[i, rows, :]
            rows = slice(j * TB, (j + 1) * TB)
            gv = ybuf[i, rows, :]
            total = total + dot(pick, (gv * gv).astype(BF16), NT)
        sq[j, s] = total
        for k in range(1, 8):
            sums(j, k).start()

    def wait_sums(j):
        for k in range(1, 8):
            sums(j, k).wait_send()
            pltpu.make_async_remote_copy(
                src_ref=sq.at[j, s], dst_ref=sq.at[j, (s + 8 - k) % 8], send_sem=sqs.at[j, k - 1],
                recv_sem=sqr.at[j, k - 1], device_id={"ctx": c, "shard": (s + k) % 8}, device_id_type=MESH,
            ).wait_recv()

    xs = s + 1 - 2 * xl
    up, down, across = (y + 1) % 4, (y + 3) % 4, (y + 2) % 4

    def cross(j):
        xr = BLOCKS[j][2]
        return remote(
            part.at[j, 1 - xl, :, pl.ds(0, xr), :], rx.at[j, :, pl.ds(0, xr), :], rxs.at[j], rxr.at[j], shard=xs
        )

    def cross2(j):
        n = BLOCKS[j][1] - BLOCKS[j][2]
        return remote(abuf.at[j, pl.ds(0, n)], rx2.at[j, pl.ds(0, n)], rx2s.at[j], rx2r.at[j], shard=xs)

    def ring_y(j, step):
        n, xr, h0 = BLOCKS[j][1], BLOCKS[j][2], BLOCKS[j][4]
        h1 = n - xr - h0
        lo, hi = pl.ds(0, h0), pl.ds(h0, h1)
        plo, phi = pl.ds(xr, h0), pl.ds(xr + h0, h1)
        src, dst, to = [
            (part.at[j, :, across, plo, :], ya.at[j, :, lo, :], up),
            (part.at[j, :, across, phi, :], yb.at[j, :, pl.ds(0, h1), :], down),
            (part.at[j, :, up, phi, :], yprev.at[j, :, hi, :], up),
            (part.at[j, :, down, plo, :], ynext.at[j, :, lo, :], down),
            (yaa.at[j, :, lo, :], yprev.at[j, :, lo, :], up),
            (yba.at[j, :, pl.ds(0, h1), :], ynext.at[j, :, hi, :], down),
        ][step]
        return remote(src, dst, yss.at[j, step], ysr.at[j, step], shard=to * 2 + xl)

    def ring_x(j, step):
        xr, h0 = BLOCKS[j][2], BLOCKS[j][3]
        h1 = xr - h0
        lo, hi = pl.ds(0, h0), pl.ds(h0, h1)
        src, dst, to = [
            (qbuf.at[j, across, lo, :], xa.at[j, lo, :], up),
            (qbuf.at[j, across, hi, :], xb.at[j, pl.ds(0, h1), :], down),
            (qbuf.at[j, up, hi, :], xprev.at[j, hi, :], up),
            (qbuf.at[j, down, lo, :], xnext.at[j, lo, :], down),
            (xaa.at[j, lo, :], xprev.at[j, lo, :], up),
            (xba.at[j, pl.ds(0, h1), :], xnext.at[j, hi, :], down),
        ][step]
        return remote(src, dst, xss.at[j, step], xsr.at[j, step], shard=to * 2 + xl)

    def product_block(j):
        r0, n, xr = BLOCKS[j][:3]
        tb = r0 // TB
        if r0 % TB == 0:
            wait_sums(tb)
        total = sq[tb, 0]
        for k in range(1, 8):
            total = total + sq[tb, k]
        scale = lax.rsqrt(total / E + 1e-05)
        rows = slice(r0, r0 + n)
        for q in range(r0, r0 + n, L):
            at = q % TB
            col = jnp.concatenate([scale[:, at:at + L]] * (L // 8), 0).T
            sub = slice(q, q + L)
            for i in range(2):
                nv = ybuf[i, sub, :] * col[:, 4 * i:4 * i + 1] * gain_ref[...]
                nrm[sub, i * EL:(i + 1) * EL] = nv.astype(BF16)
        for p in range(8):
            xx = lax.rem(p // 4 + 1 + xl, 2)
            yy = p % 4
            part[j, xx, yy, 0:n, :] = dot(nrm[rows, :], wall[:, rows_of(yy * 2 + xx, TB)]).astype(BF16)
            if p == 3:
                cross(j).start()
        for step in range(4):
            ring_y(j, step).start()

    def middle_x(j):
        xr = BLOCKS[j][2]
        cross(j).wait()
        for yk in range(4):
            both = part[j, xl, yk, 0:xr, :].astype(F32) + rx[j, yk, 0:xr, :].astype(F32)
            qbuf[j, yk, 0:xr, :] = both.astype(BF16)
        for step in range(4):
            ring_x(j, step).start()

    def middle_y(j):
        n, xr, h0 = BLOCKS[j][1], BLOCKS[j][2], BLOCKS[j][4]
        h1 = n - xr - h0
        for step in range(2):
            ring_y(j, step).wait()
        for m in range(2):
            both = part[j, m, up, xr:xr + h0, :].astype(F32) + ya[j, m, 0:h0, :].astype(F32)
            yaa[j, m, 0:h0, :] = both.astype(BF16)
            both = part[j, m, down, xr + h0:n, :].astype(F32) + yb[j, m, 0:h1, :].astype(F32)
            yba[j, m, 0:h1, :] = both.astype(BF16)
        for step in range(4, 6):
            ring_y(j, step).start()

    def third_x(j):
        xr, h0 = BLOCKS[j][2:4]
        h1 = xr - h0
        for step in range(2):
            ring_x(j, step).wait()
        both = qbuf[j, up, 0:h0, :].astype(F32) + xa[j, 0:h0, :].astype(F32)
        xaa[j, 0:h0, :] = both.astype(BF16)
        both = qbuf[j, down, h0:xr, :].astype(F32) + xb[j, 0:h1, :].astype(F32)
        xba[j, 0:h1, :] = both.astype(BF16)
        for step in range(4, 6):
            ring_x(j, step).start()

    def third_y(j):
        n, xr = BLOCKS[j][1:3]
        for step in range(2, 6):
            ring_y(j, step).wait()
        sums_ = []
        for m in range(2):
            xx = (xl + 1 + m) % 2
            acc = part[j, xx, y, xr:n, :].astype(F32)
            acc = acc + yprev[j, xx, 0:n - xr, :].astype(F32) + ynext[j, xx, 0:n - xr, :].astype(F32)
            sums_.append(acc)
        abuf[j, 0:n - xr, :] = sums_[0].astype(BF16)
        cross2(j).start()
        kept[j] = sums_[1]

    def last_block(j):
        r0, n, xr = BLOCKS[j][:3]
        for step in range(2, 6):
            ring_x(j, step).wait()
        acc = qbuf[j, y, 0:xr, :].astype(F32)
        acc = acc + xprev[j, 0:xr, :].astype(F32) + xnext[j, 0:xr, :].astype(F32)
        cross2(j).wait()
        low = kept[j] + rx2[j, 0:n - xr, :].astype(F32)
        ob[:, r0:r0 + n] = jnp.concatenate([acc, low], 0).T.astype(BF16)
        leave(j).start()

    def leave(j):
        at = pl.ds(BLOCKS[j][0], BLOCKS[j][1])
        return pltpu.make_async_copy(ob.at[:, at], out_ref.at[:, at], osem.at[j])

    kept = [None] * len(BLOCKS)
    gated_block(0)
    gated_block(1)
    late_block(3)
    product_block(0)
    gated_block(2)
    product_block(1)
    middle_y(0)
    gated_block(3)
    product_block(2)
    middle_y(1)
    middle_x(0)
    product_block(3)
    middle_y(2)
    product_block(4)
    middle_x(1)
    third_y(0)
    third_x(0)
    middle_y(3)
    middle_x(2)
    third_y(1)
    third_x(1)
    middle_y(4)
    last_block(0)
    middle_x(3)
    third_y(2)
    third_x(2)
    middle_x(4)
    third_y(3)
    third_x(3)
    last_block(1)
    third_y(4)
    third_x(4)
    last_block(2)
    last_block(3)
    last_block(4)
    for j in range(NR):
        leave(j).wait()


def per_device(
    hidden, ids, table, proj_weight, bc_weight, dt_weight, dt_bias, decay, conv_weight, conv_bias, skip,
    norm_gain, out_weight,
):
    T, D = hidden.shape
    EL = conv_bias.shape[0]
    H = EL // HEADDIM
    NB, NC = T // TB, T // L
    vm = pl.BlockSpec(memory_space=pltpu.VMEM)
    sm = pl.BlockSpec(memory_space=pltpu.SMEM)
    hbm = pl.BlockSpec(memory_space=pl.ANY)
    V = pltpu.VMEM
    dma = pltpu.SemaphoreType.DMA
    scratch = [
        V((T, D), BF16),
        V((D, 2, EL), BF16), V((2, D, EL), BF16), V((2, D, EL), BF16), V((2 * EL, D), BF16),
        V((17, 16, D), BF16), V((2 * (L + 16), D), BF16), V((D // 8, T), BF16), V((TB, TB), BF16),
        V((2, T + 16, EL), F32), V((2, T, EL), BF16), V((2, L, T), BF16), V((2, L, T), BF16), V((2, T, L), BF16),
        V((2, T, EL), F32), V((2, T, EL), F32),
        V((2, NC * H, L), F32), V((NC, L, L), F32), V((T, L), F32), V((2, NC, H, L), F32),
        V((2, NC, L, EL), F32), V((2, L, EL), F32),
        V((2, 16, EL), BF16), V((2, 16, EL), BF16),
        V((2, L + 16, EL), BF16), V((2, L + 16, EL), BF16),
        V((2, L + 16, EL // 2), BF16), V((8, L + 16, EL // 2), BF16),
        V((2, L, EL // 2), BF16), V((2, L, EL // 2), BF16),
        V((NB, 8, 8, TB), F32), V((T, 2 * EL), BF16), V((NR, 2, 4, TB, TB), BF16),
        V((NR, 4, XM, TB), BF16), V((NR, 4, XM, TB), BF16), V((NR, YM, TB), BF16), V((NR, YM, TB), BF16),
        V((NR, XH, TB), BF16), V((NR, XH, TB), BF16), V((NR, XH, TB), BF16), V((NR, XH, TB), BF16),
        V((NR, XM, TB), BF16), V((NR, XM, TB), BF16),
        V((NR, 2, YH, TB), BF16), V((NR, 2, YH, TB), BF16), V((NR, 2, YH, TB), BF16), V((NR, 2, YH, TB), BF16),
        V((NR, 2, YM, TB), BF16), V((NR, 2, YM, TB), BF16),
        dma((NB,)), dma((NB,)), dma, dma, dma((7,)), dma((8,)), dma((2,)), dma((2,)), dma((2,)), dma((2,)), dma((2,)), dma((2,)), dma((7,)), dma((7,)),
        dma, dma, dma((NB, 7)), dma((NB, 7)),
        dma((NR,)), dma((NR,)), dma((NR,)), dma((NR,)), dma((NR,)), dma((NR, 6)), dma((NR, 6)), dma((NR, 6)), dma((NR, 6)),
    ]
    return pl.pallas_call(
        kernel,
        out_shape=jax.ShapeDtypeStruct((D // 8, T), BF16),
        in_specs=[hbm, vm, vm, hbm, hbm, vm, vm, vm, vm, hbm, sm, sm, sm],
        out_specs=hbm,
        scratch_shapes=scratch,
        compiler_params=pltpu.CompilerParams(
            collective_id=0, has_side_effects=True, vmem_limit_bytes=60 * 1024 * 1024
        ),
        cost_estimate=pl.CostEstimate(flops=20_000_000_000, bytes_accessed=16_000_000, transcendentals=4_000_000),
    )(
        hidden, ids.reshape(1, T), table, proj_weight, bc_weight.T.reshape(2, 16, D), dt_weight.T,
        conv_weight, conv_bias.reshape(1, EL), norm_gain.reshape(1, EL), out_weight,
        dt_bias, decay, skip,
    )


def solution(mesh):
    in_specs = (
        P("ctx", None), P("ctx"), P(), P(None, None, "shard"), P(None, "shard"), P(None, "shard"), P("shard"),
        P("shard"), P(None, "shard"), P("shard"), P("shard"), P("shard"), P("shard", None),
    )
    return jax.shard_map(
        per_device, mesh=mesh, in_specs=in_specs, out_specs=P("shard", "ctx"), check_vma=False
    )
```
